32 devices in a mesh: dp: 8 (over z, y), cls: 4 (over x, core).
Axes of the slice: x: 2, y: 2, z: 4, core: 2. Of those that a mesh axis runs over, the one named last changes fastest.
Arguments:
- current_patches: bfloat16 [64, 196, 768], P('dp', 'cls'), may hold values from -6 to 6
- current_labels: int32 [64], P('dp'), may hold values from 0 to 999
- buffer_patches: bfloat16 [640, 196, 768], P('dp', 'cls'), may hold values from -6 to 6
- buffer_logits: bfloat16 [640, 1000], P('dp', 'cls'), may hold values from -8 to 8
- buffer_labels: int32 [640], P('dp'), may hold values from 0 to 999
- replay_owner: int32 [128, 1], replicated, may hold values from 0 to 7; in each aligned block of 16 rows (0 to 15, 16 to 31, ...) at most 2 rows name the same one
- replay_row: int32 [128], replicated, may hold values from 0 to 79
- seen_mask: int32 [192, 1000], P('dp', 'cls'), may hold values 0 or 1
- patch_weight: float32 [768, 384], P(('dp', 'cls')), may hold values from -0.21875 to 0.21875
- patch_moment: float32 [768, 384], P(('dp', 'cls')), may hold values from -1.9073486e-05 to 1.9073486e-05
- patch_average: float32 [768, 384], P(('dp', 'cls')), may hold values from -0.21875 to 0.21875
- attention_weight: float32 [1, 384, 1536], P(None, None, ('dp', 'cls')), may hold values from -0.3125 to 0.3125
- attention_moment: float32 [1, 384, 1536], P(None, None, ('dp', 'cls')), may hold values from -1.9073486e-05 to 1.9073486e-05
- attention_average: float32 [1, 384, 1536], P(None, None, ('dp', 'cls')), may hold values from -0.3125 to 0.3125
- up_weight: float32 [1, 384, 1536], P(None, 'dp', 'cls'), may hold values from -0.3125 to 0.3125
- up_moment: float32 [1, 384, 1536], P(None, 'dp', 'cls'), may hold values from -1.9073486e-05 to 1.9073486e-05
- up_average: float32 [1, 384, 1536], P(None, 'dp', 'cls'), may hold values from -0.3125 to 0.3125
- down_weight: float32 [1, 1536, 384], P(None, 'cls', 'dp'), may hold values from -0.15625 to 0.15625
- down_moment: float32 [1, 1536, 384], P(None, 'cls', 'dp'), may hold values from -1.9073486e-05 to 1.9073486e-05
- down_average: float32 [1, 1536, 384], P(None, 'cls', 'dp'), may hold values from -0.15625 to 0.15625
- head_weight: float32 [384, 1000], P('dp', 'cls'), may hold values from -2 to 2
- head_moment: float32 [384, 1000], P('dp', 'cls'), may hold values from -1.9073486e-05 to 1.9073486e-05
- head_average: float32 [384, 1000], P('dp', 'cls'), may hold values from -2 to 2
- vector_weight: float32 [82816], P(('dp', 'cls'))
- vector_moment: float32 [82816], P(('dp', 'cls')), may hold values from -1.9073486e-05 to 1.9073486e-05
- vector_average: float32 [82816], P(('dp', 'cls'))
Outputs:
- total_loss: float32 [], replicated
- grad_norm: float32 [], replicated
- new_patch: float32 [768, 384], P(('dp', 'cls'))
- new_patch_moment: float32 [768, 384], P(('dp', 'cls'))
- new_patch_average: float32 [768, 384], P(('dp', 'cls'))
- new_attention: float32 [1, 384, 1536], P(None, None, ('dp', 'cls'))
- new_attention_moment: float32 [1, 384, 1536], P(None, None, ('dp', 'cls'))
- new_attention_average: float32 [1, 384, 1536], P(None, None, ('dp', 'cls'))
- new_up: float32 [1, 384, 1536], P(None, 'dp', 'cls')
- new_up_moment: float32 [1, 384, 1536], P(None, 'dp', 'cls')
- new_up_average: float32 [1, 384, 1536], P(None, 'dp', 'cls')
- new_down: float32 [1, 1536, 384], P(None, 'cls', 'dp')
- new_down_moment: float32 [1, 1536, 384], P(None, 'cls', 'dp')
- new_down_average: float32 [1, 1536, 384], P(None, 'cls', 'dp')
- new_head: float32 [384, 1000], P('dp', 'cls')
- new_head_moment: float32 [384, 1000], P('dp', 'cls')
- new_head_average: float32 [384, 1000], P('dp', 'cls')
- new_vector: float32 [82816], P(('dp', 'cls'))
- new_vector_moment: float32 [82816], P(('dp', 'cls'))
- new_vector_average: float32 [82816], P(('dp', 'cls'))
The draws below stay inside these ranges and needn't reach their ends.
Inputs may be any that keep to these rules, and one draw needn't show every extreme that they name: `replay_owner`: aligned blocks of 16 rows belong to one index of dp each, in order; within a block no owner appears more than 2 times, and 2 is reached.
All inputs are finite; a program needn't handle non-finite values. No bound on the sum of `seen_mask` on one device may be relied on, other than what follows from the above.
Results may differ from the reference program's by a relative error of at most 0.00075.
The reference program's roundings to bfloat16 on the way count: a program that leaves them out, or rounds other values in their place, can miss the bound.
Values may be sent and summed in bfloat16 or wider, within the bound.
No kernel may reach another device: no remote copies, remote signals or barrier semaphores. Data moves between devices by JAX's collectives and lax.ppermute only.
A program may use at most 192 MiB of HBM per device.

```python
import math
import jax
import jax.numpy as jnp
import numpy as np
from jax import lax

D = 384
HEADS = 6
HD = 64
FF = 1536
C = 1000
PD = 768
NP = 196
TOK = 197
LAYERS = 1
BUF_DEV = 80
GROUP_KIND = 8
CURRENT = 64
REPLAY = 128
ROWS = 192
BUFFER = 640
CAP = 2
VLEN = 82816
PARAMS = 2531176
N_DP = 8


def vector_values(key):
    index = jnp.arange(VLEN)
    layer_at = TOK * D + 4 * D + C
    stride = 8 * D + FF
    within = (index - layer_at) % stride
    in_layers = (index >= layer_at) & (index < layer_at + LAYERS * stride)
    final_slot = (index >= TOK * D + D) & (index < TOK * D + 2 * D)
    layer_slot = in_layers & ((within < D) | (within >= 5 * D) & (within < 6 * D))
    gain_slot = final_slot | layer_slot
    noise = jax.random.normal(key, (VLEN,), jnp.float32)
    return jnp.where(gain_slot, 1.0 + 0.1 * noise, 0.5 * noise)


def draw_vector_weight(key, part):
    return vector_values(jax.random.fold_in(key, 101))


def draw_vector_average(key, part):
    return vector_values(jax.random.fold_in(key, 202))


def touch_ends(values, own_key, low, high):
    longest = values.shape.index(max(values.shape))
    spots = []
    for shift in (0, 1):
        where = [jax.random.randint(jax.random.fold_in(own_key, axis), (), 0, length) for axis, length in enumerate(values.shape)]
        where[longest] = (where[longest] + shift) % values.shape[longest]
        spots.append(tuple(where))
    return values.at[spots[0]].set(low).at[spots[1]].set(high)


def block_scale(key, extent, cuts, least, high):
    level = 1.0
    for dim, blocks in cuts:
        draws = jax.random.uniform(jax.random.fold_in(jax.random.fold_in(key, 6), dim), (blocks,), jnp.float32, least / len(cuts), high / len(cuts))
        level = level * jnp.repeat(jnp.exp(draws), extent[dim] // blocks).reshape((-1,) + (1,) * (len(extent) - 1 - dim))
    return level


def shared_out(stream_key, own, number, rows, number_of, top, bound, skew):
    ranking = jax.random.permutation(stream_key, number_of)
    packed, usual = portions_of(number_of, rows * top, bound, skew, True), portions_of(number_of, rows * top, bound, skew, False)
    places = jnp.arange(number_of)

    def named(tallies, turn):
        used = int((tallies > 0).sum())
        fixed = max(1, used // 4)
        shifted = fixed + (places - fixed + turn * (used - fixed)) % max(1, number_of - fixed)
        return jnp.zeros((number_of,), jnp.int32).at[ranking[jnp.where(places < fixed, places, shifted)]].set(jnp.asarray(tallies, jnp.int32))

    tallies = jnp.where(number % 4 == 0, named(packed, number // 4), named(usual, number - number // 4 - 1))
    mixed = jax.random.permutation(jax.random.fold_in(own, 3), number_of)
    giver, taker = mixed[0:number_of // 2 * 2:2], mixed[1:number_of // 2 * 2:2]
    margin = jnp.minimum(tallies[giver] - 1, bound - tallies[taker]) // 2
    margin = jnp.where((giver == ranking[0]) | (taker == ranking[0]) | (tallies[taker] == 0), 0, jnp.maximum(margin, 0))
    shifted = jax.random.randint(jax.random.fold_in(own, 4), (number_of // 2,), 0, 1 << 20) % (margin + 1)
    tallies = tallies.at[giver].add(-shifted).at[taker].add(shifted)
    items = jnp.searchsorted(jnp.cumsum(tallies), jnp.arange(rows * top), side="right").astype(jnp.int32)
    listing = items.reshape(top, rows).T
    listing = listing[jax.random.permutation(jax.random.fold_in(own, 1), rows)]
    turn = jax.random.randint(jax.random.fold_in(own, 2), (rows, 1), 0, top)
    return jnp.take_along_axis(listing, (jnp.arange(top)[None, :] + turn) % top, axis=1)


def portions_of(amount, total, limit, slope, full):
    portions = [(1 << 20) // math.isqrt(standing ** slope) + 1 for standing in range(1, amount + 1)]
    largest = limit if full else min(limit, max(-(-total // amount), total * portions[0] // sum(portions)))
    least = 1 if total - largest >= amount - 1 else 0
    counts, surplus = [largest] + [least] * (amount - 1), total - largest - least * (amount - 1)
    while surplus > 0:
        movable = [i for i in range(1, amount) if counts[i] < largest] or [i for i in range(1, amount) if counts[i] < limit]
        whole, budget = sum([portions[i] for i in movable]), surplus
        for i in movable:
            addition = min(limit - counts[i], max(1, budget * portions[i] // whole), surplus)
            counts[i] = counts[i] + addition
            surplus = surplus - addition
    return np.array(counts)


def bell_draw(own_key, dims, deviation, reach, pieces=(), held_as=jnp.bfloat16):
    values = jax.random.normal(own_key, dims, jnp.float32) * deviation
    if len(pieces) > 0:
        values = block_scale(own_key, dims, pieces, -0.22, 0.18) * values
    return jnp.clip(values, min=-reach, max=reach).astype(held_as)


def setup_inputs(seed: int = 0) -> dict:
    key_list = jax.random.split(jax.random.key(seed), 27)
    current_patches = bell_draw(key_list[0], (CURRENT, NP, PD), 1.0, 6.0, ((0, 8), (1, 4)))
    current_labels = touch_ends(jax.random.randint(key_list[1], (CURRENT,), 0, C), jax.random.fold_in(key_list[1], 1), 0, C - 1).astype(jnp.int32)
    buffer_patches = bell_draw(key_list[2], (BUFFER, NP, PD), 1.0, 6.0, ((0, 8), (1, 4)))
    buffer_logits = bell_draw(key_list[3], (BUFFER, C), 2.0, 8.0, ((0, 8), (1, 4)))
    buffer_labels = touch_ends(jax.random.randint(key_list[4], (BUFFER,), 0, C), jax.random.fold_in(key_list[4], 1), 0, C - 1).astype(jnp.int32)
    replay_owner_keys = jax.random.split(jax.random.fold_in(key_list[5], 1), REPLAY // (2 * GROUP_KIND))
    replay_owner_turns = jax.random.permutation(jax.random.fold_in(key_list[5], 3), REPLAY // (2 * GROUP_KIND))
    replay_owner = jax.vmap(lambda own, number: shared_out(jax.random.fold_in(key_list[5], 2), own, number, 2 * GROUP_KIND, N_DP, 1, CAP, 2))(replay_owner_keys, replay_owner_turns).reshape((REPLAY, 1))
    replay_row = touch_ends(jax.random.randint(key_list[6], (REPLAY,), 0, BUF_DEV), jax.random.fold_in(key_list[6], 1), 0, BUF_DEV - 1).astype(jnp.int32)
    seen_mask = touch_ends((jax.random.randint(key_list[7], (ROWS, C), 0, 4) < 3).astype(jnp.int32), jax.random.fold_in(key_list[7], 1), 0, 1)
    patch_weight = bell_draw(key_list[8], (PD, D), PD ** -0.5, 0.21875, ((0, 32),), jnp.float32)
    patch_moment = bell_draw(key_list[9], (PD, D), (0.005 / PARAMS ** 0.5), 1.9073486328125e-05, ((0, 32),), jnp.float32)
    patch_average = bell_draw(key_list[10], (PD, D), PD ** -0.5, 0.21875, ((0, 32),), jnp.float32)
    attention_weight = bell_draw(key_list[11], (LAYERS, D, 4 * D), D ** -0.5, 0.3125, ((2, 32),), jnp.float32)
    attention_moment = bell_draw(key_list[12], (LAYERS, D, 4 * D), (0.005 / PARAMS ** 0.5), 1.9073486328125e-05, ((2, 32),), jnp.float32)
    attention_average = bell_draw(key_list[13], (LAYERS, D, 4 * D), D ** -0.5, 0.3125, ((2, 32),), jnp.float32)
    up_weight = bell_draw(key_list[14], (LAYERS, D, FF), D ** -0.5, 0.3125, ((1, 8), (2, 4)), jnp.float32)
    up_moment = bell_draw(key_list[15], (LAYERS, D, FF), (0.005 / PARAMS ** 0.5), 1.9073486328125e-05, ((1, 8), (2, 4)), jnp.float32)
    up_average = bell_draw(key_list[16], (LAYERS, D, FF), D ** -0.5, 0.3125, ((1, 8), (2, 4)), jnp.float32)
    down_weight = bell_draw(key_list[17], (LAYERS, FF, D), FF ** -0.5, 0.15625, ((1, 4), (2, 8)), jnp.float32)
    down_moment = bell_draw(key_list[18], (LAYERS, FF, D), (0.005 / PARAMS ** 0.5), 1.9073486328125e-05, ((1, 4), (2, 8)), jnp.float32)
    down_average = bell_draw(key_list[19], (LAYERS, FF, D), FF ** -0.5, 0.15625, ((1, 4), (2, 8)), jnp.float32)
    head_weight = bell_draw(key_list[20], (D, C), (7.0 / D ** 0.5), 2.0, ((0, 8), (1, 4)), jnp.float32)
    head_moment = bell_draw(key_list[21], (D, C), (0.005 / PARAMS ** 0.5), 1.9073486328125e-05, ((0, 8), (1, 4)), jnp.float32)
    head_average = bell_draw(key_list[22], (D, C), (7.0 / D ** 0.5), 2.0, ((0, 8), (1, 4)), jnp.float32)
    vector_weight = draw_vector_weight(jax.random.fold_in(key_list[26], 71), 0)
    vector_moment = bell_draw(key_list[24], (VLEN,), (0.005 / PARAMS ** 0.5), 1.9073486328125e-05, ((0, 32),), jnp.float32)
    vector_average = draw_vector_average(jax.random.fold_in(key_list[26], 71), 0)
    return {"current_patches": current_patches, "current_labels": current_labels, "buffer_patches": buffer_patches, "buffer_logits": buffer_logits, "buffer_labels": buffer_labels, "replay_owner": replay_owner, "replay_row": replay_row, "seen_mask": seen_mask, "patch_weight": patch_weight, "patch_moment": patch_moment, "patch_average": patch_average, "attention_weight": attention_weight, "attention_moment": attention_moment, "attention_average": attention_average, "up_weight": up_weight, "up_moment": up_moment, "up_average": up_average, "down_weight": down_weight, "down_moment": down_moment, "down_average": down_average, "head_weight": head_weight, "head_moment": head_moment, "head_average": head_average, "vector_weight": vector_weight, "vector_moment": vector_moment, "vector_average": vector_average}


NORM_EPS = 1e-06
SCORE_SCALE = 0.125
LOGIT_WEIGHT = 0.3
LABEL_WEIGHT = 0.8
MOMENTUM_DECAY = 0.9
AVERAGE_KEEP = 0.75
CLIP_NORM = 0.005
HIGHEST = lax.Precision.HIGHEST

@jax.custom_vjp
def low(v):
    return lax.optimization_barrier(v.astype(jnp.bfloat16)).astype(jnp.float32)

@jax.custom_vjp
def low_back(v):
    return v

def low_keep(v):
    return (low(v), None)

def low_pass(kept, grad):
    return (grad,)

def back_keep(v):
    return (v, None)

def back_low(kept, grad):
    return (low(grad),)
low.defvjp(low_keep, low_pass)
low_back.defvjp(back_keep, back_low)

def vector_parts(vector):
    position_end = TOK * D
    position = vector[:position_end].reshape(TOK, D)
    singles = [vector[position_end + column * D:position_end + (column + 1) * D] for column in range(4)]
    heads_at = position_end + 4 * D
    layer_at = heads_at + C
    head_bias = vector[heads_at:layer_at]
    layered = [vector[layer_at + column * D:layer_at + (column + 1) * D] for column in range(8)]
    bias_up = vector[layer_at + 8 * D:layer_at + 8 * D + FF]
    return [position] + singles + [head_bias] + layered + [bias_up]

def normalize(values):
    centred = values - lax.optimization_barrier(jnp.mean(values, axis=-1, keepdims=True))
    inverse = lax.rsqrt(lax.optimization_barrier(jnp.mean(centred * centred, axis=-1, keepdims=True)) + NORM_EPS)
    return centred * inverse

def group_loss(weights, pixels, labels, soft_target, mask_rows, normal_count):
    patch, attention, upward, downward, head, vector = weights
    parts = vector_parts(vector)
    position, patch_bias, final_gain, final_shift, class_token, head_bias = parts[:6]
    gain_one, shift_one, bias_query, bias_value, bias_output, gain_two, shift_two, bias_down = parts[6:14]
    bias_up = parts[14]
    images = pixels.shape[0]
    embedded = low_back(jnp.einsum('inp,pd->ind', pixels, patch, precision=HIGHEST))
    leading = jnp.broadcast_to(class_token[None, None, :], (images, 1, D))
    tokens = jnp.concatenate([leading, embedded + patch_bias], axis=1) + position
    w_qkv = attention[0][:, :3 * D]
    w_out = attention[0][:, 3 * D:]
    normed_one = low(normalize(tokens) * gain_one + shift_one)
    qkv_bias = jnp.concatenate([bias_query, jnp.zeros((D,), jnp.float32), bias_value])
    projected = low_back(low(jnp.einsum('itd,de->ite', normed_one, w_qkv, precision=HIGHEST) + qkv_bias))
    projected = projected.reshape(images, TOK, 3, HEADS, HD)
    queries, keys_part, values_part = (projected[:, :, 0], projected[:, :, 1], projected[:, :, 2])
    scores = low_back(jnp.einsum('ithd,ishd->ihts', queries, keys_part, precision=HIGHEST) * SCORE_SCALE)
    probs = jax.nn.softmax(scores, axis=-1)
    attended = low_back(low(jnp.einsum('ihts,ishd->ithd', low(probs), values_part, precision=HIGHEST)))
    attended = attended.reshape(images, TOK, D)
    branch = low_back(jnp.einsum('itd,de->ite', attended, w_out, precision=HIGHEST) + bias_output)
    after_attention = tokens + branch
    normed_two = low(normalize(after_attention) * gain_two + shift_two)
    up_pre = low_back(jnp.einsum('itd,df->itf', normed_two, upward[0], precision=HIGHEST) + bias_up)
    activated = low(jax.nn.gelu(up_pre, approximate=False))
    mlp_branch = low_back(jnp.einsum('itf,fd->itd', activated, downward[0], precision=HIGHEST) + bias_down)
    final_rows = after_attention + mlp_branch
    pooled = low(lax.optimization_barrier(jnp.mean(normalize(final_rows) * final_gain + final_shift, axis=1)))
    logits = low_back(jnp.dot(pooled, head, precision=HIGHEST) + head_bias)
    kind_rows = images // 3
    target_hot = jnp.arange(C)[None, :] == labels[:, None]
    live = (mask_rows == 1) | target_hot
    row_top = lax.optimization_barrier(jnp.max(logits, axis=1, keepdims=True))
    log_norm = row_top[:, 0] + jnp.log(lax.optimization_barrier(jnp.sum(jnp.where(live, jnp.exp(logits - row_top), 0.0), axis=1)))
    cross = log_norm - lax.optimization_barrier(jnp.sum(jnp.where(target_hot, logits, 0.0), axis=1))
    replay_mask = mask_rows[kind_rows:2 * kind_rows] == 1
    error = jnp.sum(jnp.where(replay_mask, (logits[kind_rows:2 * kind_rows] - soft_target) ** 2, 0.0))
    first = jnp.sum(cross[:kind_rows]) + LABEL_WEIGHT * jnp.sum(cross[2 * kind_rows:])
    return first / normal_count + LOGIT_WEIGHT * error / (normal_count * C)

def reference(current_patches, current_labels, buffer_patches, buffer_logits, buffer_labels, replay_owner, replay_row, seen_mask, patch_weight, patch_moment, patch_average, attention_weight, attention_moment, attention_average, up_weight, up_moment, up_average, down_weight, down_moment, down_average, head_weight, head_moment, head_average, vector_weight, vector_moment, vector_average):
    kind_rows = current_patches.shape[0] // N_DP
    replay_count = 2 * kind_rows
    normal_count = kind_rows * N_DP
    source_index = (replay_owner[:, 0] * BUF_DEV + replay_row).astype(jnp.int32)
    masters = (patch_weight, attention_weight, up_weight, down_weight, head_weight, vector_weight)

    def loss_of(params):
        lowered = tuple((low(weight) for weight in params))

        def step_group(running, group):
            start = (group * kind_rows).astype(jnp.int32)
            current = lax.dynamic_slice_in_dim(current_patches, start, kind_rows, 0)
            current_lab = lax.dynamic_slice_in_dim(current_labels, start, kind_rows, 0)
            picked = lax.dynamic_slice_in_dim(source_index, (group * replay_count).astype(jnp.int32), replay_count, 0)
            replay_pixels = jnp.take(buffer_patches, picked, axis=0)
            replay_soft = jnp.take(buffer_logits, picked[:kind_rows], axis=0).astype(jnp.float32)
            replay_lab = jnp.take(buffer_labels, picked[kind_rows:], axis=0)
            pixels = jnp.concatenate([current, replay_pixels], axis=0).astype(jnp.float32)
            labels = jnp.concatenate([current_lab, jnp.zeros((kind_rows,), jnp.int32), replay_lab]).astype(jnp.int32)
            mask_rows = lax.dynamic_slice_in_dim(seen_mask, (group * 3 * kind_rows).astype(jnp.int32), 3 * kind_rows, 0)
            return (running + group_loss(lowered, pixels, labels, replay_soft, mask_rows, normal_count), None)
        total, _ = lax.scan(jax.checkpoint(step_group), jnp.float32(0.0), jnp.arange(N_DP, dtype=jnp.int32))
        return total
    loss_value, back_fn = jax.vjp(loss_of, masters)
    gradients = back_fn(jnp.float32(1.0))[0]
    squares = sum((jnp.sum(grad * grad) for grad in gradients))
    norm_value = jnp.sqrt(squares)
    clip_factor = jnp.minimum(1.0, CLIP_NORM / (norm_value + 1e-06))
    rate = 0.03 * math.sqrt(PARAMS) / CLIP_NORM
    moments = (patch_moment, attention_moment, up_moment, down_moment, head_moment, vector_moment)
    averages = (patch_average, attention_average, up_average, down_average, head_average, vector_average)
    results = [loss_value, norm_value]
    for weight, moment, average, grad in zip(masters, moments, averages, gradients):
        clipped = clip_factor * grad
        moment_new = MOMENTUM_DECAY * moment + clipped
        weight_new = weight - rate * (clipped + MOMENTUM_DECAY * moment_new)
        average_new = AVERAGE_KEEP * average + (1.0 - AVERAGE_KEEP) * weight_new
        results += [weight_new, moment_new, average_new]
    return tuple(results)
```

```python
import functools
import math

import jax
import jax.numpy as jnp
from jax import lax
from jax.experimental import pallas as pl
from jax.experimental.pallas import tpu as pltpu
from jax.sharding import PartitionSpec as P

D = 384
HEADS = 6
HD = 64
FF = 1536
C = 1000
PD = 768
TOK = 197
PATCHES = 196
PARAMS = 2531176

NORM_EPS = 1e-06
SCORE_SCALE = 0.125
LOGIT_WEIGHT = 0.3
LABEL_WEIGHT = 0.8
MOMENTUM_DECAY = 0.9
AVERAGE_KEEP = 0.75
CLIP_NORM = 0.005
RATE = 0.03 * math.sqrt(PARAMS) / CLIP_NORM

ROWS_T = 208
GRID_DP, GRID_CLS = 8, 4
BLOCKS = GRID_DP * GRID_CLS
CPART = C // GRID_CLS
CPAD = 256
R_ONE = 80
R_TWO = 128
R_MASK = 16
PIX_ROWS = 304
V_ROWS = 232
HEAD_AT = (TOK + 4) * D
LAYER_AT = HEAD_AT + C

bf16 = jnp.bfloat16
f32 = jnp.float32
i32 = jnp.int32

ANY = pl.BlockSpec(memory_space=pl.ANY)
VMEM = pl.BlockSpec(memory_space=pltpu.VMEM)
SMEM = pl.BlockSpec(memory_space=pltpu.SMEM)


def sds(shape, dtype):
    return jax.ShapeDtypeStruct(shape, dtype)


def cost(micros):
    return pl.CostEstimate(flops=int(micros * 1.15e9), bytes_accessed=1 << 20, transcendentals=0)


def params_of(limit_mib, **more):
    return pltpu.CompilerParams(vmem_limit_bytes=limit_mib << 20, **more)


def nn(a, b):
    return lax.dot_general(a, b, (((1,), (0,)), ((), ())), preferred_element_type=f32)


def nt(a, b):
    return lax.dot_general(a, b, (((1,), (1,)), ((), ())), preferred_element_type=f32)


def tn(a, b):
    return lax.dot_general(a, b, (((0,), (0,)), ((), ())), preferred_element_type=f32)


def gelu_parts(values):
    bell = jnp.exp(-0.5 * values * values)
    t = 1.0 / (1.0 + (0.3275911 * 0.5**0.5) * jnp.abs(values))
    tail = 0.5 * 1.061405429 * t - 0.5 * 1.453152027
    tail = tail * t + 0.5 * 1.421413741
    tail = tail * t - 0.5 * 0.284496736
    tail = (tail * t + 0.5 * 0.254829592) * t * bell
    return jnp.where(values < 0.0, tail, 1.0 - tail), bell * (1.0 / math.sqrt(2.0 * math.pi))


def normalize(values):
    centred = values - jnp.mean(values, axis=-1, keepdims=True)
    inverse = lax.rsqrt(jnp.mean(centred * centred, axis=-1, keepdims=True) + NORM_EPS)
    return (centred * inverse, inverse)


def normalize_back(unit, inverse, grad_unit):
    return inverse * (
        grad_unit
        - jnp.mean(grad_unit, axis=-1, keepdims=True)
        - unit * jnp.mean(grad_unit * unit, axis=-1, keepdims=True)
    )


def advance(weight, moment, average, grad, clip_factor):
    clipped = clip_factor * grad
    moment_new = MOMENTUM_DECAY * moment + clipped
    weight_new = weight - RATE * (clipped + MOMENTUM_DECAY * moment_new)
    average_new = AVERAGE_KEEP * average + (1.0 - AVERAGE_KEEP) * weight_new
    return (weight_new, moment_new, average_new)


def pack_head(block):
    a, b, c = block[..., :16, :], block[..., 16:32, :], block[..., 32:, :]
    top = jnp.concatenate([a, b[..., :128]], axis=-1)
    low = jnp.concatenate([b[..., 128:], c], axis=-1)
    return jnp.concatenate([top, low], axis=-2)


def unpack_head(block):
    top, low = block[..., :16, :], block[..., 16:, :]
    b = jnp.concatenate([top[..., 256:], low[..., :128]], axis=-1)
    return jnp.concatenate([top[..., :256], b, low[..., 128:]], axis=-2)


def me_of(tuned):
    if tuned:
        return lax.axis_index("dp") * GRID_CLS + lax.axis_index("cls")
    return 0


def grad_place(s):
    core, x, y, z = s & 1, (s >> 1) & 1, (s >> 2) & 1, s >> 3
    if z < 2:
        return core, (0 if x else 4) + 2 * y + z
    return core, (8 if y else 12) + 2 * x + (z - 2)


R_CODE = 16
SECTIONS_ONE = (0, 48, 72, 80)
SECTIONS_TWO = (0, 32, 80, 128)


def encode(block, sections, out):
    rows = sections[-1]
    powers = []
    for j, (a, b) in enumerate(zip(sections[:-1], sections[1:])):
        part = block[j] if isinstance(block, list) else block[a:b]
        most = jnp.max(jnp.abs(part), axis=0, keepdims=True)
        power = jnp.clip(jnp.ceil(jnp.log2(jnp.maximum(most, 1e-30))), -99.0, 126.0)
        code = jnp.round(part * jnp.exp2(15.0 - power))
        out[a:b, :] = jnp.clip(code, -32767.0, 32767.0).astype(i32).astype(jnp.int16)
        powers.append(power)
    powers.append(jnp.zeros((R_CODE - len(powers), D), f32))
    out[rows : rows + R_CODE, :] = jnp.concatenate(powers, axis=0).astype(i32).astype(jnp.int16)


def put_block(parts, sections, keep, send, core, place):
    if core:
        encode(parts, sections, send.at[place])
    else:
        for part, a, b in zip(parts, sections[:-1], sections[1:]):
            keep[place, a:b, :] = part


def decode(code, sections):
    rows = sections[-1]
    powers = code[rows : rows + R_CODE, :].astype(i32).astype(f32)
    return jnp.concatenate(
        [
            code[a:b, :].astype(i32).astype(f32) * jnp.exp2(powers[j : j + 1] - 15.0)
            for j, (a, b) in enumerate(zip(sections[:-1], sections[1:]))
        ],
        axis=0,
    )


def pack_mask(block):
    a, b, c = block[:8], block[8:16], block[16:]
    top = jnp.concatenate([a, b[:, :128]], axis=1)
    return jnp.concatenate([top, jnp.concatenate([b[:, 128:], c], axis=1)], axis=0)


def unpack_mask(block):
    top, low = block[:8], block[8:]
    b = jnp.concatenate([top[:, 256:], low[:, :128]], axis=1)
    return jnp.concatenate([top[:, :256], b, low[:, 128:]], axis=0)


def pack_weights_kernel(attn, patch, vec, up, down, head, seen, out):
    one, two = out.at[0:R_ONE], out.at[R_ONE:]
    one[0:48, :] = attn[...].astype(bf16)
    one[48:80, :] = jnp.concatenate([patch[...], vec[...]], axis=0).astype(bf16)
    block = jnp.concatenate([head[...], jnp.zeros((48, CPAD - CPART), f32)], axis=1)
    two[0:32, :] = pack_head(block).astype(bf16)
    two[32:80, :] = up[...].astype(bf16)
    two[80:128, :] = down[...].astype(bf16)
    mask = jnp.concatenate([seen[...].astype(f32), jnp.zeros((seen.shape[0], CPAD - CPART), f32)], axis=1)
    two[128:144, :] = pack_mask(mask).astype(bf16)


def pick_kernel(cur_own, rep_own, find, *refs):
    if find:
        owner, row, cur_labels, buf_labels, cur, buf, logits, o0, o1, far, meta, *scratch = refs
    else:
        row, cur, buf, logits, o0, o1, far, *scratch = refs
    stage, stage_cur, wide, wide_cur, soft, res, slots, sems = scratch
    parts, stored, _ = stage.shape
    kind = stage_cur.shape[1]
    chunk = 7
    copies = [pltpu.make_async_copy(cur, stage_cur, sems.at[parts // chunk])]
    for j in range(parts // chunk):
        part = pl.ds(j * chunk, chunk)
        copies.append(pltpu.make_async_copy(buf.at[part], stage.at[part], sems.at[j]))
    for copy in copies:
        copy.start()
    me = lax.axis_index("cls")
    if find:
        mine = lax.axis_index("dp")

        def look(i, count):
            hit = owner[i] == mine

            @pl.when(hit)
            def _():
                slots[count] = i

            return count + jnp.where(hit, 1, 0)

        lax.fori_loop(0, owner.shape[0], look, 0)
        for m in range(8):
            if m < cur_own:
                meta[0, m] = cur_labels[me * cur_own + m]
                meta[1, m] = 0
                meta[2, m] = mine * 3 * kind + me * cur_own + m
            elif m < cur_own + rep_own:
                i = slots[me * rep_own + m - cur_own]
                at = lax.rem(i, 2 * kind)
                meta[0, m] = jnp.where(at < kind, 0, buf_labels[row[i]])
                meta[1, m] = jnp.where(at < kind, 1, 2)
                meta[2, m] = lax.div(i, 2 * kind) * 3 * kind + kind + at
            else:
                meta[0, m] = 0
                meta[1, m] = 3
                meta[2, m] = 0
    else:
        for k in range(4 * rep_own):
            slots[k] = k
    soft[...] = jnp.zeros_like(soft)
    soft[:, :CPART] = logits[...].astype(f32)
    for j, copy in enumerate(copies):
        copy.wait()
        for lanes in range(PD // 128):
            at = slice(lanes * 128, (lanes + 1) * 128)
            if j == 0:
                wide_cur[lanes] = stage_cur[:, :, at].astype(f32).reshape(parts * kind, 128)
            else:
                one = stage[(j - 1) * chunk : j * chunk, :, at].astype(f32).reshape(chunk * stored, 128)
                wide[lanes, (j - 1) * chunk * stored : j * chunk * stored, :] = one
    images = cur_own + rep_own
    res[images * parts :, :] = jnp.zeros((PIX_ROWS - images * parts, PD), f32)
    for k, out in enumerate((o0, o1, far.at[0], far.at[1])):
        to = me ^ k
        for m in range(images):
            if m >= cur_own:
                r = row[slots[to * rep_own + m - cur_own]]
                at = (m % 3) * CPAD
                res[images * parts + m // 3 : images * parts + m // 3 + 1, at : at + CPAD] = soft[pl.ds(r, 1), :]
            for lanes in range(PD // 128):
                if m < cur_own:
                    one = wide_cur[lanes, pl.ds(to * cur_own + m, parts, stride=kind), :]
                else:
                    one = wide[lanes, pl.ds(r, parts, stride=stored), :]
                res[m * parts : (m + 1) * parts, lanes * 128 : (lanes + 1) * 128] = one
        out[...] = res[...].astype(bf16)


def spread_vector(vblock, blocks, flat):
    flat[...] = jnp.zeros_like(flat)
    lane = lax.broadcasted_iota(i32, (8, D), 1)
    for d in range(BLOCKS):
        q, s = divmod(vblock * d, D)
        b = blocks[d]
        if s:
            b = pltpu.roll(b, s, 1)
        flat[q : q + 8, :] = flat[q : q + 8, :] + jnp.where(lane >= s, b, 0.0)
        if s:
            flat[q + 1 : q + 9, :] = flat[q + 1 : q + 9, :] + jnp.where(lane < s, b, 0.0)


def cut_vector(vblock, flat, blocks):
    lane = lax.broadcasted_iota(i32, (8, D), 1)
    place = lax.broadcasted_iota(i32, (8, D), 0) * D + lane
    for d in range(BLOCKS):
        q, s = divmod(vblock * d, D)
        b = flat[q : q + 8, :]
        if s:
            a = pltpu.roll(b, D - s, 1)
            b = pltpu.roll(flat[q + 1 : q + 9, :], D - s, 1)
            b = jnp.where(lane < D - s, a, b)
        blocks[d] = jnp.where(place < vblock, b, 0.0)


def layer_vectors(flat):
    row, s = divmod(LAYER_AT, D)
    lane = lax.broadcasted_iota(i32, (12, D), 1)
    a = pltpu.roll(flat[row : row + 16, :], D - s, 1)
    return jnp.where(lane < D - s, a[0:12], a[1:13])


def head_vector(flat):
    rows = []
    wide = lax.broadcasted_iota(i32, (1, D), 1)
    for part in range(GRID_CLS):
        row, s = divmod(HEAD_AT + part * CPART, D)
        a = flat[row : row + 1, :]
        if s:
            a = pltpu.roll(jnp.broadcast_to(a, (8, D)), D - s, 1)[0:1]
            b = pltpu.roll(jnp.broadcast_to(flat[row + 1 : row + 2, :], (8, D)), D - s, 1)[0:1]
            a = jnp.where(wide < D - s, a, b)
        rows.append(jnp.where(wide < CPART, a, 0.0)[:, :CPAD])
    return jnp.concatenate(rows, axis=0)


def store_flat(flat, at, values, count):
    row, s = divmod(at, D)
    wide = lax.broadcasted_iota(i32, (1, D), 1)
    values = jnp.where(wide < count, values, 0.0)
    if s:
        values = pltpu.roll(jnp.broadcast_to(values, (8, D)), s, 1)[0:1]
        flat[row + 1 : row + 2, :] = flat[row + 1 : row + 2, :] + jnp.where(wide < s, values, 0.0)
    flat[row : row + 1, :] = flat[row : row + 1, :] + jnp.where(wide >= s, values, 0.0)


def pair_heads(low, first, second, axis):
    return jnp.where(low, first, second)


def embed_kernel(tuned, vblock, n, images, *refs):
    (w0, w1, w2, w3, w4, w5, w6, w7, p0, p1, p2, p3, x0_out, qkv_out, attn, prm, hb, soft,
     patch_wide, patch, blocks, flat, table, rows, x0_all) = refs
    weights = (w0, w1, w2, w3, w4, w5, w6, w7)
    p2 = p2.at[0]
    me = me_of(tuned)
    part = lax.axis_index("cls")
    per = PATCHES // 4

    @pl.when(pl.program_id(0) == 0)
    def _():
        for s in range(BLOCKS):
            d = s ^ me
            w = weights[s & 7]
            attn[pl.ds(pl.multiple_of(d * 48, 16), 48), :] = w[s >> 3, 0:48, :]
            rest = w[s >> 3, 48:80, :].astype(f32)
            patch_wide[pl.ds(pl.multiple_of(d * 24, 8), 24), :] = rest[0:24]
            blocks[d] = rest[24:32]
        patch[...] = patch_wide[...].astype(bf16)
        spread_vector(vblock, blocks, flat)
        prm[0:12, :] = layer_vectors(flat)
        prm[12:13, :] = flat[TOK + 1 : TOK + 2, :]
        prm[13:14, :] = flat[TOK + 2 : TOK + 3, :]
        prm[14:16, :] = jnp.zeros((2, D), f32)
        hb[0:4, :] = head_vector(flat)
        hb[4:8, :] = jnp.zeros((4, CPAD), f32)
        bias = flat[TOK : TOK + 1, :]
        table[...] = jnp.zeros_like(table)
        for k in range(4):
            for q in range(4):

                @pl.when((part ^ k) == q)
                def _(k=k, q=q):
                    table[k * per : k * per + per, :] = flat[1 + q * per : 1 + q * per + per, :] + bias

        table[PATCHES : PATCHES + 1, :] = flat[0:1, :] + flat[TOK + 3 : TOK + 4, :]
        soft[...] = jnp.zeros_like(soft)
        for k, piece in enumerate((p0, p1, p2, p3)):
            rows[k * PIX_ROWS : (k + 1) * PIX_ROWS, :] = nn(piece[...], patch[...])
            stored = piece[PIX_ROWS - 16 :, :].astype(f32)
            at = images * per - (PIX_ROWS - 16)
            for m in range(images):
                soft[part ^ k, m : m + 1, :] = stored[at + m // 3 : at + m // 3 + 1, (m % 3) * CPAD : (m % 3 + 1) * CPAD]
        for m in range(images):
            x0_all[m] = table[...]
            for k in range(4):
                at = slice(k * per, k * per + per)
                begin = k * PIX_ROWS + m * per
                x0_all[m, at, :] = x0_all[m, at, :] + rows[begin : begin + per, :]

    tokens = n * ROWS_T
    x0 = x0_all[pl.ds(pl.program_id(0) * n, n)]
    x0_out[...] = x0
    unit, _ = normalize(x0)
    normed = (unit * prm[0:1, :] + prm[1:2, :]).astype(bf16).reshape(tokens, D)
    for j, bias in ((0, prm[2:3, :]), (1, None), (2, prm[3:4, :])):
        one = nt(normed, attn[j * D : (j + 1) * D, :])
        if bias is not None:
            one = one + bias
        qkv_out[:, :, j * D : (j + 1) * D] = one.astype(bf16).reshape(n, ROWS_T, D)


def attend_kernel(n, w_out, prm, x0, qkv, att_out, x1_out):
    tokens = n * ROWS_T
    keys = lax.broadcasted_iota(i32, (ROWS_T, ROWS_T), 0) < TOK
    low = lax.broadcasted_iota(i32, (ROWS_T, 128), 1) < HD
    low_t = lax.broadcasted_iota(i32, (128, ROWS_T), 0) < HD
    for i in range(n):
        for p in range(HEADS // 2):
            at = p * 128
            q2 = qkv[i, :, at : at + 128]
            k2 = qkv[i, :, D + at : D + at + 128]
            v2 = qkv[i, :, 2 * D + at : 2 * D + at + 128]
            v2t = v2.T
            outs = []
            for head in range(2):
                ka = jnp.where(low if head == 0 else ~low, k2, jnp.zeros_like(k2))
                scores = jnp.where(keys, nt(ka, q2) * SCORE_SCALE, -1e30)
                top = jnp.max(scores, axis=0, keepdims=True)
                powers = jnp.exp(scores - top)
                probs = (powers * (1.0 / jnp.sum(powers, axis=0, keepdims=True))).astype(bf16)
                outs.append(nn(v2t, probs))
            both = jnp.where(low_t, outs[0], outs[1])
            att_out[i, :, at : at + 128] = both.T.astype(bf16)
    branch = nt(att_out[...].reshape(tokens, D), w_out[...]) + prm[4:5, :]
    x1_out[...] = x0[...] + branch.reshape(n, ROWS_T, D)


def middle_kernel(tuned, n, images, scales, *refs):
    if not tuned:
        given, *refs = refs
    (w0, w1, w2, w3, w4, w5, w6, w7, prm, hb, soft, meta, x1_in,
     dx1_out, keep, send, vgrad, hgrad, loss,
     w_up, w_down, w_head, act, slope, mask, masks_all, pooled, dpooled, glow, acc_up, acc_down) = refs
    weights = (w0, w1, w2, w3, w4, w5, w6, w7)
    me = me_of(tuned)
    step = pl.program_id(0)
    last = pl.num_programs(0) - 1

    @pl.when(step == 0)
    def _():
        for s in range(BLOCKS):
            d = s ^ me
            dp, cl = d >> 2, d & 3
            w = weights[s & 7]
            rows = pl.ds(pl.multiple_of(dp * 48, 16), 48)
            w_head[cl, rows, :] = unpack_head(w[s >> 3, 0:32, :])
            w_up[cl, rows, :] = w[s >> 3, 32:80, :]
            w_down[cl, rows, :] = w[s >> 3, 80:128, :]
            if tuned:
                seen = unpack_mask(w[s >> 3, 128:144, :].astype(f32))
                masks_all[cl, pl.ds(pl.multiple_of(dp * 24, 8), 24), :] = seen
        if tuned:
            mask[...] = jnp.zeros_like(mask)
            for m in range(images):
                for q in range(4):
                    mask[q, m : m + 1, :] = masks_all[q, pl.ds(meta[2, m], 1), :]
        else:
            mask[...] = given[...]
        acc_up[...] = jnp.zeros_like(acc_up)
        acc_down[...] = jnp.zeros_like(acc_down)
        vgrad[...] = jnp.zeros_like(vgrad)
        pooled[...] = jnp.zeros_like(pooled)

    tokens = n * ROWS_T
    x1 = x1_in[...].reshape(tokens, D)
    unit_two, inverse_two = normalize(x1)
    normed = (unit_two * prm[5:6, :] + prm[6:7, :]).astype(bf16)
    total = jnp.zeros((tokens, D), f32)
    for c in range(4):
        pre = nn(normed, w_up[c]) + prm[8 + c : 9 + c, :]
        half, bell = gelu_parts(pre)
        hot = (pre * half).astype(bf16)
        act[c] = hot
        slope[c] = half + pre * bell
        total = total + nt(hot, w_down[c])
    x2 = x1 + (total + prm[7:8, :])
    unit, inverse = normalize(x2)
    real = lax.broadcasted_iota(i32, (ROWS_T, D), 0) < TOK
    sums = []
    for i in range(n):
        u = unit[i * ROWS_T : (i + 1) * ROWS_T]
        sums.append(jnp.sum(jnp.where(real, u, 0.0), axis=0, keepdims=True))
        pooled[pl.ds(step * n + i, 1), :] = sums[i] * (1.0 / TOK) * prm[12:13, :] + prm[13:14, :]

    low = pooled[...].astype(bf16)
    rows8 = (16, CPAD)
    row_id = lax.broadcasted_iota(i32, rows8, 0)
    lane = lax.broadcasted_iota(i32, rows8, 1)
    label = jnp.full(rows8, -1, i32)
    weight = jnp.zeros(rows8, f32)
    squared = jnp.zeros(rows8, f32)
    for i in range(images):
        kind = meta[1, i]
        label = jnp.where(row_id == i, meta[0, i], label)
        weight = jnp.where(row_id == i, jnp.where(kind == 0, scales[0], jnp.where(kind == 2, scales[1], 0.0)), weight)
        squared = jnp.where(row_id == i, jnp.where(kind == 1, 1.0, 0.0), squared)
    inside = lane < CPART
    logits, hots, lives, masks, tops = [], [], [], [], []
    pad = jnp.zeros((8, CPAD), f32)
    for q in range(4):
        one = nn(low, w_head[q]) + hb[q : q + 1, :]
        hot = (lane + q * CPART == label) & inside
        seen = (jnp.concatenate([mask[q], pad], axis=0) > 0.5) & inside
        logits.append(one)
        hots.append(hot)
        masks.append(seen)
        lives.append(seen | hot)
        tops.append(jnp.max(jnp.where(inside, one, -3e38), axis=1, keepdims=True))
    top = jnp.maximum(jnp.maximum(tops[0], tops[1]), jnp.maximum(tops[2], tops[3]))
    alive = sum(
        jnp.sum(jnp.where(lives[q], jnp.exp(logits[q] - top), 0.0), axis=1, keepdims=True) for q in range(4)
    )
    norm = top + jnp.log(alive)
    target = sum(jnp.sum(jnp.where(hots[q], logits[q], 0.0), axis=1, keepdims=True) for q in range(4))
    cross = norm - target
    value = jnp.sum(jnp.where(weight[:, 0:1] > 0, weight[:, 0:1] * cross, 0.0))
    back = jnp.zeros((16, D), f32)
    for q in range(4):
        gap = jnp.where(masks[q], logits[q] - jnp.concatenate([soft[q], pad], axis=0), 0.0)
        value = value + scales[2] * jnp.sum(squared * gap * gap)
        share = jnp.where(lives[q], jnp.exp(logits[q] - norm), 0.0)
        grad = weight * (share - jnp.where(hots[q], 1.0, 0.0)) + squared * (2.0 * scales[2]) * gap
        g = grad.astype(bf16)
        glow[q] = g
        back = back + nt(g, w_head[q])
    dpooled[...] = back

    pieces = []
    for i in range(n):
        grad = dpooled[pl.ds(step * n + i, 1), :]
        vgrad[12:13, :] = vgrad[12:13, :] + grad * (1.0 / TOK) * sums[i]
        vgrad[13:14, :] = vgrad[13:14, :] + grad
        dz = grad * (1.0 / TOK) * prm[12:13, :]
        u = unit[i * ROWS_T : (i + 1) * ROWS_T]
        d = inverse[i * ROWS_T : (i + 1) * ROWS_T] * (
            dz - jnp.mean(dz, axis=-1, keepdims=True) - u * jnp.mean(dz * u, axis=-1, keepdims=True)
        )
        pieces.append(jnp.where(real, d, 0.0))
    dx2 = jnp.concatenate(pieces, axis=0)
    dy = dx2.astype(bf16)
    vgrad[7:8, :] = vgrad[7:8, :] + jnp.sum(dy.astype(f32), axis=0, keepdims=True)
    dyt = dy.T
    normed_t = normed.T
    dnormed = jnp.zeros((tokens, D), f32)
    for c in range(4):
        dact = nn(dy, w_down[c])
        dup = (dact * slope[c]).astype(bf16)
        vgrad[8 + c : 9 + c, :] = vgrad[8 + c : 9 + c, :] + jnp.sum(dup.astype(f32), axis=0, keepdims=True)
        acc_down[c] = acc_down[c] + nn(dyt, act[c])
        acc_up[c] = acc_up[c] + nn(normed_t, dup)
        dnormed = dnormed + nt(dup, w_up[c])
    vgrad[5:6, :] = vgrad[5:6, :] + jnp.sum(dnormed * unit_two, axis=0, keepdims=True)
    vgrad[6:7, :] = vgrad[6:7, :] + jnp.sum(dnormed, axis=0, keepdims=True)
    dx1 = dx2 + normalize_back(unit_two, inverse_two, dnormed * prm[5:6, :])
    dx1_out[...] = dx1.reshape(n, ROWS_T, D)

    @pl.when(step == last)
    def _():
        loss[...] = jnp.where(lax.broadcasted_iota(i32, loss.shape, 1) == 0, 0.0, value)
        hgrad[...] = jnp.zeros_like(hgrad)
        for q in range(4):
            hgrad[q : q + 1, :] = jnp.sum(glow[q].astype(f32), axis=0, keepdims=True)
        lowt = low.T
        for q in range(4):
            w_head_grad = nn(lowt, glow[q])
            slope[q, 0:D, 0:CPAD] = w_head_grad
        for s in range(BLOCKS):
            d = s ^ me
            dp, cl = d >> 2, d & 3
            core, place = grad_place(s)
            rows = pl.ds(pl.multiple_of(dp * 48, 8), 48)
            block = [pack_head(slope[cl, rows, 0:CPAD]), acc_up[cl, rows, :], acc_down[cl, rows, :]]
            put_block(block, SECTIONS_TWO, keep, send, core, place)


def attend_back_kernel(n, first, *refs):
    if first:
        (w_out, vgrad_in, qkv, att, dx1_in, dqkv, acc, vgrad) = refs
    else:
        (w_out, vgrad_in, qkv, att, dx1_in, acc_in, _, dqkv, acc, vgrad) = refs

    @pl.when(pl.program_id(0) == 0)
    def _():
        acc[...] = jnp.zeros_like(acc) if first else acc_in[...]
        vgrad[...] = vgrad_in[...]

    tokens = n * ROWS_T
    dout = dx1_in[...].reshape(tokens, D).astype(bf16)
    vgrad[4:5, :] = vgrad[4:5, :] + jnp.sum(dout.astype(f32), axis=0, keepdims=True)
    acc[...] = acc[...] + tn(dout, att[...].reshape(tokens, D))
    datt = nn(dout, w_out[...]).astype(bf16)
    keys = lax.broadcasted_iota(i32, (ROWS_T, ROWS_T), 0) < TOK
    low = lax.broadcasted_iota(i32, (ROWS_T, 128), 1) < HD
    low_t = lax.broadcasted_iota(i32, (128, ROWS_T), 0) < HD
    for i in range(n):
        rows = slice(i * ROWS_T, (i + 1) * ROWS_T)
        for p in range(HEADS // 2):
            at = p * 128
            q2 = qkv[i, :, at : at + 128]
            k2 = qkv[i, :, D + at : D + at + 128]
            v2 = qkv[i, :, 2 * D + at : 2 * D + at + 128]
            do = datt[rows, at : at + 128]
            k2t = k2.T
            dqs, dks, dvs = [], [], []
            for head in range(2):
                side = low if head == 0 else ~low
                ka = jnp.where(side, k2, jnp.zeros_like(k2))
                va = jnp.where(side, v2, jnp.zeros_like(v2))
                scores = jnp.where(keys, nt(ka, q2) * SCORE_SCALE, -1e30)
                top = jnp.max(scores, axis=0, keepdims=True)
                powers = jnp.exp(scores - top)
                probs = powers * (1.0 / jnp.sum(powers, axis=0, keepdims=True))
                dprobs = nt(va, do)
                mean = jnp.sum(probs * dprobs, axis=0, keepdims=True)
                dscores = (probs * (dprobs - mean)).astype(bf16)
                dks.append(nn(dscores, q2))
                dqs.append(nn(k2t, dscores))
                dvs.append(nn(probs.astype(bf16), do))
            dq = (jnp.where(low_t, dqs[0], dqs[1]) * SCORE_SCALE).T
            dqkv[i, :, at : at + 128] = dq.astype(bf16)
            dqkv[i, :, D + at : D + at + 128] = (jnp.where(low, dks[0], dks[1]) * SCORE_SCALE).astype(bf16)
            dqkv[i, :, 2 * D + at : 2 * D + at + 128] = jnp.where(low, dvs[0], dvs[1]).astype(bf16)


def unit_back_kernel(n, w_in, prm, vgrad_in, x0, dqkv_in, dx1_in, dx0_out, vgrad):
    @pl.when(pl.program_id(0) == 0)
    def _():
        vgrad[...] = vgrad_in[...]

    tokens = n * ROWS_T
    dx1 = dx1_in[...].reshape(tokens, D)
    dqkv = dqkv_in[...].reshape(tokens, 3 * D)
    vgrad[2:3, :] = vgrad[2:3, :] + jnp.sum(dqkv[:, 0:D].astype(f32), axis=0, keepdims=True)
    vgrad[3:4, :] = vgrad[3:4, :] + jnp.sum(dqkv[:, 2 * D : 3 * D].astype(f32), axis=0, keepdims=True)
    unit, inverse = normalize(x0[...].reshape(tokens, D))
    dnormed = nn(dqkv, w_in[...])
    vgrad[0:1, :] = vgrad[0:1, :] + jnp.sum(dnormed * unit, axis=0, keepdims=True)
    vgrad[1:2, :] = vgrad[1:2, :] + jnp.sum(dnormed, axis=0, keepdims=True)
    dx0 = dx1 + normalize_back(unit, inverse, dnormed * prm[0:1, :])
    dx0_out[...] = dx0.reshape(n, ROWS_T, D)


def qkv_back_kernel(n, prm, x0, dqkv_in, acc):
    @pl.when(pl.program_id(0) == 0)
    def _():
        acc[...] = jnp.zeros_like(acc)

    tokens = n * ROWS_T
    dqkv = dqkv_in[...].reshape(tokens, 3 * D)
    unit, _ = normalize(x0[...].reshape(tokens, D))
    normed = (unit * prm[0:1, :] + prm[1:2, :]).astype(bf16)
    for j in range(3):
        at = slice(j * D, (j + 1) * D)
        acc[at, :] = acc[at, :] + tn(dqkv[:, at], normed)


def embed_back_kernel(tuned, vblock, images, *refs):
    (vgrad, hgrad, acc_in, acc_out, p0, p1, p2, p3, dx0_all, keep, send, acc, acc_patch, rows, flat, blocks) = refs
    p2 = p2.at[0]
    me = me_of(tuned)
    part = lax.axis_index("cls")
    per = PATCHES // 4
    acc[0 : 3 * D, :] = acc_in[...]
    acc[3 * D : 4 * D, :] = acc_out[...]
    rows[...] = jnp.zeros_like(rows)
    for m in range(images):
        for k in range(4):
            begin = k * PIX_ROWS + m * per
            rows[begin : begin + per, :] = dx0_all[m, k * per : k * per + per, :]
    low = rows[...].astype(bf16)
    total = tn(p0[...], low[:PIX_ROWS])
    for k, piece in ((1, p1), (2, p2), (3, p3)):
        total = total + tn(piece[...], low[k * PIX_ROWS : (k + 1) * PIX_ROWS])
    acc_patch[...] = total
    position = dx0_all[0]
    for m in range(1, images):
        position = position + dx0_all[m]
    flat[...] = jnp.zeros_like(flat)
    for k in range(4):
        for q in range(4):

            @pl.when((part ^ k) == q)
            def _(k=k, q=q):
                flat[1 + q * per : 1 + q * per + per, :] = position[k * per : k * per + per, :]

    first = position[PATCHES : PATCHES + 1, :]
    flat[0:1, :] = first
    flat[TOK : TOK + 1, :] = jnp.sum(position[0:PATCHES, :], axis=0, keepdims=True)
    flat[TOK + 1 : TOK + 2, :] = vgrad[12:13, :]
    flat[TOK + 2 : TOK + 3, :] = vgrad[13:14, :]
    flat[TOK + 3 : TOK + 4, :] = first
    for q in range(GRID_CLS):
        wide = jnp.concatenate([hgrad[q : q + 1, :], jnp.zeros((1, D - CPAD), f32)], axis=1)
        store_flat(flat, HEAD_AT + q * CPART, wide, CPART)
    for j in range(12):
        store_flat(flat, LAYER_AT + j * D, vgrad[j : j + 1, :], D)
    cut_vector(vblock, flat, blocks)
    for s in range(BLOCKS):
        d = s ^ me
        core, place = grad_place(s)
        rows48, rows24 = pl.ds(pl.multiple_of(d * 48, 8), 48), pl.ds(pl.multiple_of(d * 24, 8), 24)
        put_block([acc[rows48, :], acc_patch[rows24, :], blocks[d]], SECTIONS_ONE, keep, send, core, place)


def update_kernel(clip_ref, one, two, *refs):
    ins, outs = refs[:15], refs[15:]
    clip = clip_ref[0, 0]
    grads = [
        one[48:72, :],
        one[0:48, :],
        two[32:80, :],
        two[80:128, :],
        unpack_head(two[0:32, :])[:, :CPART],
    ]
    for j, grad in enumerate(grads):
        news = advance(ins[3 * j][...], ins[3 * j + 1][...], ins[3 * j + 2][...], grad, clip)
        for k in range(3):
            outs[3 * j + k][...] = news[k]


def flip(n, k):
    return [(i, i ^ k) for i in range(n)]


def to_core(v):
    return lax.ppermute(v, "cls", flip(4, 1))


def to_x(v):
    return lax.ppermute(v, "cls", flip(4, 2))


def to_y(v):
    return lax.ppermute(v, "dp", flip(8, 1))


def to_z(v, k):
    return lax.ppermute(v, "dp", flip(8, 2 * k))


def gather_blocks(near, after=None):
    at_x = to_x(near)
    if after is not None:
        at_x, _ = lax.optimization_barrier((at_x, after))
    at_y, at_xy = to_y(near), to_y(at_x)
    return [near, to_core(near), at_x, to_core(at_x), at_y, to_core(at_y), at_xy]


def first_kernel(sections, keep, got, send_a, keep_a, send_b, keep_b):
    encode(keep[0, 0] + decode(got.at[0, 0], sections), sections, send_a.at[0])
    keep_a[0] = keep[1, 0] + decode(got.at[1, 0], sections)
    encode(keep[2, 0] + decode(got.at[2, 0], sections), sections, send_b.at[0])
    keep_b[0] = keep[3, 0] + decode(got.at[3, 0], sections)


def second_kernel(sections, keep_a, keep_b, got_a, got_b, send_a, rest_a, send_b, rest_b):
    for keep, got, send, rest in ((keep_a, got_a, send_a, rest_a), (keep_b, got_b, send_b, rest_b)):
        rest[0] = keep[0, 0] + decode(got.at[0, 0], sections)
        encode(keep[1, 0] + decode(got.at[1, 0], sections), sections, send.at[0])


def third_kernel(sections, keep_a, keep_b, got_a, got_b, own, send_1, send_2, send_3):
    own[...] = keep_a[0] + decode(got_a.at[0], sections)
    encode(keep_a[1] + decode(got_a.at[1], sections), sections, send_1)
    encode(keep_b[0] + decode(got_b.at[0], sections), sections, send_2)
    encode(keep_b[1] + decode(got_b.at[1], sections), sections, send_3)


def fourth_kernel(sections, own, got_1, got_2, got_3, before, share, sums):
    total = own[...] + decode(got_1, sections) + (decode(got_2, sections) + decode(got_3, sections))
    share[...] = total
    lane = lax.broadcasted_iota(i32, (8, 128), 1)
    sums[...] = before[...] + jnp.where(lane == 0, jnp.sum(total * total), 0.0)


def scatter_first(keep, got, sections):
    rows = sections[-1]
    quarters = [pl.BlockSpec((4, 1, r, D), lambda j: (0, j, 0, 0)) for r in (rows, rows + R_CODE)]
    wide, code = pl.BlockSpec((1, rows, D), lambda j: (j, 0, 0)), pl.BlockSpec((1, rows + R_CODE, D), lambda j: (j, 0, 0))
    return pl.pallas_call(
        functools.partial(first_kernel, sections),
        grid=(4,),
        in_specs=quarters,
        out_specs=[code, wide, code, wide],
        out_shape=[sds((4, rows + R_CODE, D), jnp.int16), sds((4, rows, D), f32)] * 2,
        cost_estimate=cost(4),
        compiler_params=params_of(16),
    )(*[v.reshape((4, 4) + v.shape[1:]) for v in (keep, got)])


def scatter_second(keep_a, keep_b, got_a, got_b, sections):
    rows = sections[-1]
    pairs, codes = [pl.BlockSpec((2, 1, r, D), lambda j: (0, j, 0, 0)) for r in (rows, rows + R_CODE)]
    wide, code = [pl.BlockSpec((1, r, D), lambda j: (j, 0, 0)) for r in (rows, rows + R_CODE)]
    return pl.pallas_call(
        functools.partial(second_kernel, sections),
        grid=(2,),
        in_specs=[pairs] * 2 + [codes] * 2,
        out_specs=[code, wide, code, wide],
        out_shape=[sds((2, rows + R_CODE, D), jnp.int16), sds((2, rows, D), f32)] * 2,
        cost_estimate=cost(2),
        compiler_params=params_of(16),
    )(*[v.reshape((2, 2) + v.shape[1:]) for v in (keep_a, keep_b, got_a, got_b)])


def scatter_third(keep_a, keep_b, got_a, got_b, sections):
    rows = sections[-1]
    return pl.pallas_call(
        functools.partial(third_kernel, sections),
        out_shape=[sds((rows, D), f32)] + [sds((rows + R_CODE, D), jnp.int16)] * 3,
        cost_estimate=cost(2),
        compiler_params=params_of(16),
    )(keep_a, keep_b, got_a, got_b)


def scatter_fourth(own, got, sections, before):
    return pl.pallas_call(
        functools.partial(fourth_kernel, sections),
        out_shape=[sds(own.shape, f32), sds((8, 128), f32)],
        cost_estimate=cost(2),
        compiler_params=params_of(16),
    )(own, *got, before)


def sum_all(v, tuned):
    if not tuned:
        return lax.psum(v, ("dp", "cls"))
    v = v + to_core(v)
    v = (v + to_x(v)) + (to_y(v) + lax.ppermute(v, ("dp", "cls"), flip(BLOCKS, GRID_CLS + 2)))
    return (v + to_z(v, 1)) + (to_z(v, 2) + to_z(v, 3))


def plain_gather(masters, vblock):
    patch, attention, up, down, head, vector = [w.astype(bf16) for w in masters]
    both = ("dp", "cls")
    patch = lax.all_gather(patch, both, axis=0, tiled=True).reshape(BLOCKS, 24, D)
    attention = lax.all_gather(attention, both, axis=2, tiled=True)[0].T.reshape(BLOCKS, 48, D)
    vector = lax.all_gather(vector, both, axis=0, tiled=True).reshape(BLOCKS, vblock)
    vector = jnp.pad(vector, ((0, 0), (0, 8 * D - vblock))).reshape(BLOCKS, 8, D)
    up = lax.all_gather(lax.all_gather(up, "dp", axis=1, tiled=True), "cls", axis=2, tiled=True)[0]
    down = lax.all_gather(lax.all_gather(down, "dp", axis=2, tiled=True), "cls", axis=1, tiled=True)[0].T
    head = lax.all_gather(lax.all_gather(head, "dp", axis=0, tiled=True), "cls", axis=1, tiled=True)
    up, down = [
        w.reshape(GRID_DP, 48, GRID_CLS, D).transpose(0, 2, 1, 3).reshape(BLOCKS, 48, D) for w in (up, down)
    ]
    head = head.reshape(GRID_DP, 48, GRID_CLS, CPART).transpose(0, 2, 1, 3).reshape(BLOCKS, 48, CPART)
    head = pack_head(jnp.pad(head, ((0, 0), (0, 0), (0, CPAD - CPART))))
    one = jnp.concatenate([attention, patch, vector], axis=1).reshape(4, 8, R_ONE, D)
    two = jnp.concatenate([head, up, down], axis=1).reshape(4, 8, R_TWO, D)
    return [one[:, a] for a in range(8)], [two[:, a] for a in range(8)]


def plain_scatter(one, two, vblock):
    def in_order(keep, send, sections):
        send = [decode(send[j], sections) for j in range(16)]
        return jnp.stack([(keep, send)[grad_place(s)[0]][grad_place(s)[1]] for s in range(BLOCKS)])

    one, two = in_order(*one, SECTIONS_ONE), in_order(*two, SECTIONS_TWO)
    both = ("dp", "cls")
    attention = one[:, 0:48].reshape(4 * D, D).T[None]
    patch = one[:, 48:72].reshape(PD, D)
    vector = one[:, 72:80].reshape(BLOCKS, 8 * D)[:, :vblock].reshape(-1)
    up, down = [
        w.reshape(GRID_DP, GRID_CLS, 48, D).transpose(0, 2, 1, 3).reshape(D, FF)
        for w in (two[:, 32:80], two[:, 80:128])
    ]
    head = unpack_head(two[:, 0:32])[:, :, :CPART]
    head = head.reshape(GRID_DP, GRID_CLS, 48, CPART).transpose(0, 2, 1, 3).reshape(D, C)

    def split(v, at_dp, at_cls):
        v = lax.psum_scatter(v, "dp", scatter_dimension=at_dp, tiled=True)
        return lax.psum_scatter(v, "cls", scatter_dimension=at_cls, tiled=True)

    return (
        lax.psum_scatter(patch, both, scatter_dimension=0, tiled=True),
        lax.psum_scatter(attention, both, scatter_dimension=2, tiled=True),
        split(up, 0, 1)[None],
        split(down.T, 1, 0)[None],
        split(head, 0, 1),
        lax.psum_scatter(vector, both, scatter_dimension=0, tiled=True),
    )


def take_rows_kernel(rows, source, out, sem):
    def one(i, carry):
        copy = pltpu.make_async_copy(source.at[rows[i]], out.at[i], sem)
        copy.start()
        copy.wait()
        return carry

    lax.fori_loop(0, out.shape[0], one, 0)


def take_rows(source, rows):
    return pl.pallas_call(
        take_rows_kernel,
        out_shape=sds((rows.shape[0],) + source.shape[1:], source.dtype),
        in_specs=[SMEM, ANY],
        out_specs=ANY,
        scratch_shapes=[pltpu.SemaphoreType.DMA(())],
    )(rows, source)


def pick_small(source, rows):
    hot = (rows[:, None] == jnp.arange(source.shape[0])[None, :]).astype(f32)
    return jnp.dot(hot, source.astype(f32), precision=lax.Precision.HIGHEST)


def plain_replay(buffer_patches, buffer_logits, buffer_labels, replay_owner, replay_row, kind_rows):
    dp_count, dp_index = lax.axis_size("dp"), lax.axis_index("dp")
    replay_count = 2 * kind_rows
    capacity = max(2, -(-replay_count // dp_count))
    table = lax.all_gather(buffer_labels, "dp", axis=0, tiled=True)
    owners = replay_owner[:, 0].reshape(dp_count, replay_count)
    local_rows = replay_row.reshape(dp_count, replay_count)
    earlier = jnp.arange(replay_count)[None, :] < jnp.arange(replay_count)[:, None]
    same_owner = owners[:, :, None] == owners[:, None, :]
    ranks = jnp.sum(jnp.where(same_owner & earlier[None], 1, 0), axis=2).astype(i32)
    slot_ids = jnp.arange(capacity, dtype=i32)
    wanted = (owners == dp_index)[:, :, None] & (ranks[:, :, None] == slot_ids[None, None, :])
    slot_rows = jnp.sum(jnp.where(wanted, local_rows[:, :, None], 0), axis=1).reshape(-1)
    pixels = take_rows(buffer_patches, slot_rows)
    logits = pick_small(buffer_logits, slot_rows).astype(bf16)
    pixels = lax.all_to_all(pixels, "dp", split_axis=0, concat_axis=0, tiled=True)
    logits = lax.all_to_all(logits, "dp", split_axis=0, concat_axis=0, tiled=True)
    my_owners, my_ranks, my_rows = [
        lax.dynamic_index_in_dim(v, dp_index, 0, keepdims=False) for v in (owners, ranks, local_rows)
    ]
    places = my_owners * buffer_labels.shape[0] + my_rows
    labels = jnp.sum(jnp.where(places[:, None] == jnp.arange(table.shape[0])[None, :], table[None, :], 0), axis=1)
    return pixels, logits, labels.astype(i32), (my_owners * capacity + my_ranks).astype(i32)


def on_device(
    current_patches,
    current_labels,
    buffer_patches,
    buffer_logits,
    buffer_labels,
    replay_owner,
    replay_row,
    seen_mask,
    patch_weight,
    patch_moment,
    patch_average,
    attention_weight,
    attention_moment,
    attention_average,
    up_weight,
    up_moment,
    up_average,
    down_weight,
    down_moment,
    down_average,
    head_weight,
    head_moment,
    head_average,
    vector_weight,
    vector_moment,
    vector_average,
):
    dp_count, cls_count = lax.axis_size("dp"), lax.axis_size("cls")
    dp_index, cls_index = lax.axis_index("dp"), lax.axis_index("cls")
    kind_rows = current_patches.shape[0]
    replay_count = 2 * kind_rows
    group_rows = 3 * kind_rows
    normal_count = kind_rows * dp_count
    patch_part = current_patches.shape[1]
    cur_own, rep_own = kind_rows // cls_count, replay_count // cls_count
    images = cur_own + rep_own
    class_part = head_weight.shape[1]
    vblock = vector_weight.shape[0] * dp_count * cls_count // BLOCKS
    tuned = dp_count == GRID_DP and cls_count == GRID_CLS and replay_count == 2 * dp_count
    masters = (patch_weight, attention_weight, up_weight, down_weight, head_weight, vector_weight)
    moments = (patch_moment, attention_moment, up_moment, down_moment, head_moment, vector_moment)
    averages = (patch_average, attention_average, up_average, down_average, head_average, vector_average)

    def views(v, j):
        return v[0].T if j in (1, 3) else v[0] if j == 2 else v

    current_view, buffer_view = current_patches.transpose(1, 0, 2), buffer_patches.transpose(1, 0, 2)
    if tuned:
        pack = pl.pallas_call(
            pack_weights_kernel,
            out_shape=sds((R_ONE + R_TWO + R_MASK, D), bf16),
            cost_estimate=cost(2),
        compiler_params=params_of(60),
        )

    def exchange(sent):
        own, near, far = sent
        far = lax.ppermute(far, "cls", flip(4, 2))
        return [own, lax.ppermute(near, "cls", flip(4, 1)), far, lax.ppermute(far[1], "cls", flip(4, 1))]

    def pick(find, stored, *operands):
        out_shape = [sds((PIX_ROWS, PD), bf16)] * 2 + [sds((2, PIX_ROWS, PD), bf16)]
        return pl.pallas_call(
            functools.partial(pick_kernel, cur_own, rep_own, find),
            out_shape=out_shape + ([sds((3, 8), i32)] if find else []),
            in_specs=[SMEM] * (4 if find else 1) + [ANY, ANY, VMEM],
            out_specs=[VMEM] * 3 + ([SMEM] if find else []),
            scratch_shapes=[
                pltpu.VMEM((patch_part, stored, PD), bf16),
                pltpu.VMEM((patch_part, kind_rows, PD), bf16),
                pltpu.VMEM((PD // 128, patch_part * stored, 128), f32),
                pltpu.VMEM((PD // 128, patch_part * kind_rows, 128), f32),
                pltpu.VMEM((stored, CPAD), f32),
                pltpu.VMEM((PIX_ROWS, PD), f32),
                pltpu.SMEM((replay_count,), i32),
                pltpu.SemaphoreType.DMA((patch_part // 7 + 1,)),
            ],
            cost_estimate=cost(7),
        compiler_params=params_of(60),
        )(*operands)

    if tuned:
        *sent, meta = pick(
            True,
            buffer_patches.shape[0],
            replay_owner.reshape(-1),
            replay_row,
            current_labels,
            buffer_labels,
            current_view,
            buffer_view,
            buffer_logits,
        )
        sent, vec = lax.optimization_barrier((sent, vector_weight))
        vec = jnp.pad(vec, (0, 8 * D - vblock)).reshape(8, D)
        got = exchange(sent)
        packed = pack(
            views(attention_weight, 1), patch_weight, vec, views(up_weight, 2), views(down_weight, 3), head_weight, seen_mask
        )
    else:
        moved, logits, labels, places = plain_replay(
            buffer_patches, buffer_logits, buffer_labels, replay_owner, replay_row, kind_rows
        )
        sent = pick(False, moved.shape[0], places, current_view, moved.transpose(1, 0, 2), logits)
        got = exchange(sent)
        row_mask = jnp.pad(seen_mask.astype(bf16), ((0, 0), (0, CPAD - class_part)))
        row_mask = lax.all_gather(row_mask, "cls").astype(f32)
        mask_rows = [
            lax.dynamic_slice_in_dim(row_mask, cls_index * cur_own, cur_own, 1),
            lax.dynamic_slice_in_dim(row_mask, kind_rows + cls_index * rep_own, rep_own, 1),
            jnp.zeros((cls_count, 8 - images, CPAD), f32),
        ]
        given = jnp.concatenate(mask_rows, axis=1)
        kinds = jnp.where(jnp.arange(replay_count) < kind_rows, 1, 2).astype(i32)
        labels = jnp.where(kinds == 1, 0, labels)

        def own(current, replayed, fill):
            return jnp.concatenate(
                [
                    lax.dynamic_slice_in_dim(current, cls_index * cur_own, cur_own, 0),
                    lax.dynamic_slice_in_dim(replayed, cls_index * rep_own, rep_own, 0),
                    jnp.full((8 - images,), fill, i32),
                ]
            )

        nothing = jnp.zeros_like(current_labels)
        meta = jnp.stack([own(current_labels, labels, 0), own(nothing, kinds, 3), jnp.zeros((8,), i32)])

    if tuned:
        column = [packed] + [to_z(packed, k) for k in (1, 2, 3)]
        near_one = jnp.stack([v[:R_ONE] for v in column])
        one = gather_blocks(near_one)
        one.append(to_core(one[6]))
        near_two = jnp.stack([v[R_ONE:] for v in column])
        near_two, got[2] = lax.optimization_barrier((near_two, got[2]))
    else:
        one, two = plain_gather(masters, vblock)
        two = [jnp.pad(v, ((0, 0), (0, R_MASK), (0, 0))) for v in two]

    n = 2
    steps = images // n
    whole = lambda shape: pl.BlockSpec(shape, lambda i: (0,) * len(shape))
    per = lambda width: pl.BlockSpec((n, ROWS_T, width), lambda i: (i, 0, 0))
    pieces = [whole((PIX_ROWS, PD))] * 2 + [pl.BlockSpec((1, PIX_ROWS, PD), lambda i: (0, 0, 0)), whole((PIX_ROWS, PD))]
    x0, qkv, attn, prm, hb, soft = pl.pallas_call(
        functools.partial(embed_kernel, tuned, vblock, n, images),
        grid=(steps,),
        in_specs=[whole((4, R_ONE, D))] * 8 + pieces,
        out_specs=[per(D), per(3 * D)] + [whole(shape) for shape in ((4 * D, D), (16, D), (8, CPAD), (4, 8, CPAD))],
        out_shape=[
            sds((images, ROWS_T, D), f32),
            sds((images, ROWS_T, 3 * D), bf16),
            sds((4 * D, D), bf16),
            sds((16, D), f32),
            sds((8, CPAD), f32),
            sds((4, 8, CPAD), f32),
        ],
        scratch_shapes=[
            pltpu.VMEM((PD, D), f32),
            pltpu.VMEM((PD, D), bf16),
            pltpu.VMEM((BLOCKS, 8, D), f32),
            pltpu.VMEM((V_ROWS, D), f32),
            pltpu.VMEM((ROWS_T, D), f32),
            pltpu.VMEM((4 * PIX_ROWS, D), f32),
            pltpu.VMEM((images, ROWS_T, D), f32),
        ],
        cost_estimate=cost(8),
        compiler_params=params_of(34),
    )(*one, *got)
    if tuned:
        two = gather_blocks(near_two, after=hb)
    out_part = pl.BlockSpec((D, D), lambda i: (3, 0))
    att, x1 = pl.pallas_call(
        functools.partial(attend_kernel, n),
        grid=(steps,),
        in_specs=[out_part, whole((16, D)), per(D), per(3 * D)],
        out_specs=[per(D), per(D)],
        out_shape=[sds((images, ROWS_T, D), bf16), sds((images, ROWS_T, D), f32)],
        cost_estimate=cost(10),
        compiler_params=params_of(20),
    )(attn, prm, x0, qkv)

    if tuned:
        two[6], x1 = lax.optimization_barrier((two[6], x1))
        two.append(to_core(two[6]))

    scales = (1.0 / normal_count, LABEL_WEIGHT / normal_count, LOGIT_WEIGHT / (normal_count * C))
    dx1, keep_two, send_two, vgrad, hgrad, loss = pl.pallas_call(
        functools.partial(middle_kernel, tuned, n, images, scales),
        grid=(steps,),
        in_specs=[whole((4, 8, CPAD))] * (0 if tuned else 1)
        + [whole((4, R_TWO + R_MASK, D))] * 8
        + [whole((16, D)), whole((8, CPAD)), whole((4, 8, CPAD))]
        + [SMEM, per(D)],
        out_specs=[
            per(D),
            whole((16, R_TWO, D)),
            whole((16, R_TWO + R_CODE, D)),
            whole((16, D)),
            whole((8, CPAD)),
            whole((8, 128)),
        ],
        out_shape=[
            sds((images, ROWS_T, D), f32),
            sds((16, R_TWO, D), f32),
            sds((16, R_TWO + R_CODE, D), jnp.int16),
            sds((16, D), f32),
            sds((8, CPAD), f32),
            sds((8, 128), f32),
        ],
        scratch_shapes=[
            pltpu.VMEM((4, D, D), bf16),
            pltpu.VMEM((4, D, D), bf16),
            pltpu.VMEM((4, D, CPAD), bf16),
            pltpu.VMEM((4, n * ROWS_T, D), bf16),
            pltpu.VMEM((4, n * ROWS_T, D), f32),
            pltpu.VMEM((4, 8, CPAD), f32),
            pltpu.VMEM((4, GRID_DP * 24, CPAD), f32),
            pltpu.VMEM((16, D), f32),
            pltpu.VMEM((16, D), f32),
            pltpu.VMEM((4, 16, CPAD), bf16),
            pltpu.VMEM((4, D, D), f32),
            pltpu.VMEM((4, D, D), f32),
        ],
        cost_estimate=cost(30),
        compiler_params=params_of(46),
    )(*([] if tuned else [given]), *two, prm, hb, soft, meta, x1)

    def attend_back(first, *operands):
        begin, count = (0, 1) if first else (1, steps - 1)
        some = lambda width: pl.BlockSpec((n, ROWS_T, width), lambda i: (i + begin, 0, 0))
        return pl.pallas_call(
            functools.partial(attend_back_kernel, n, first),
            grid=(count,),
            in_specs=[out_part, whole((16, D)), some(3 * D), some(D), some(D)] + ([] if first else [whole((D, D)), ANY]),
            out_specs=[some(3 * D), whole((D, D)), whole((16, D))],
            out_shape=[sds((images, ROWS_T, 3 * D), bf16), sds((D, D), f32), sds((16, D), f32)],
            input_output_aliases={} if first else {6: 0},
            cost_estimate=cost(6 * count),
            compiler_params=params_of(22),
        )(*operands)

    dqkv, acc_out, vgrad = attend_back(True, attn, vgrad, qkv, att, dx1)
    if tuned:
        a_code, a_keep, b_code, b_keep = scatter_first(keep_two, to_core(send_two), SECTIONS_TWO)
        a_code, b_code, vgrad = lax.optimization_barrier((a_code, b_code, vgrad))
        moving = (to_x(a_code), to_y(b_code))
    dqkv, acc_out, vgrad = attend_back(False, attn, vgrad, qkv, att, dx1, acc_out, dqkv)
    if tuned:
        a_code, a_rest, b_code, b_rest = scatter_second(a_keep, b_keep, *moving, SECTIONS_TWO)
        a_code, b_code, vgrad = lax.optimization_barrier((a_code, b_code, vgrad))
        moving = (to_y(a_code), to_x(b_code))
    dx0, vgrad = pl.pallas_call(
        functools.partial(unit_back_kernel, n),
        grid=(steps,),
        in_specs=[whole((3 * D, D)), whole((16, D)), whole((16, D)), per(D), per(3 * D), per(D)],
        out_specs=[per(D), whole((16, D))],
        out_shape=[sds((images, ROWS_T, D), f32), sds((16, D), f32)],
        cost_estimate=cost(6),
        compiler_params=params_of(22),
    )(attn, prm, vgrad, x0, dqkv, dx1)
    if tuned:
        own_two, *codes_two = scatter_third(a_rest, b_rest, *moving, SECTIONS_TWO)
        codes_two, dqkv = lax.optimization_barrier((codes_two, dqkv))
        last_two = [to_z(code, k + 1) for k, code in enumerate(codes_two)]
    acc_in = pl.pallas_call(
        functools.partial(qkv_back_kernel, n),
        grid=(steps,),
        in_specs=[whole((16, D)), per(D), per(3 * D)],
        out_specs=whole((3 * D, D)),
        out_shape=sds((3 * D, D), f32),
        cost_estimate=cost(6),
        compiler_params=params_of(22),
    )(prm, x0, dqkv)
    if tuned:
        share_two, sums = scatter_fourth(own_two, last_two, SECTIONS_TWO, loss)
        sums, dx0 = lax.optimization_barrier((sums, dx0))
    keep_one, send_one = pl.pallas_call(
        functools.partial(embed_back_kernel, tuned, vblock, images),
        in_specs=[VMEM] * 9,
        out_shape=[sds((16, R_ONE, D), f32), sds((16, R_ONE + R_CODE, D), jnp.int16)],
        scratch_shapes=[
            pltpu.VMEM((4 * D, D), f32),
            pltpu.VMEM((PD, D), f32),
            pltpu.VMEM((4 * PIX_ROWS, D), f32),
            pltpu.VMEM((V_ROWS, D), f32),
            pltpu.VMEM((BLOCKS, 8, D), f32),
        ],
        cost_estimate=cost(6),
        compiler_params=params_of(34),
    )(vgrad, hgrad, acc_in, acc_out, *got, dx0)

    if tuned:
        a_code, a_keep, b_code, b_keep = scatter_first(keep_one, to_core(send_one), SECTIONS_ONE)
        moving = (to_x(a_code), to_y(b_code))
        a_code, a_rest, b_code, b_rest = scatter_second(a_keep, b_keep, *moving, SECTIONS_ONE)
        moving = (to_y(a_code), to_x(b_code))
        own_one, *codes_one = scatter_third(a_rest, b_rest, *moving, SECTIONS_ONE)
        last_one = [to_z(code, k + 1) for k, code in enumerate(codes_one)]
        share_one, sums = scatter_fourth(own_one, last_one, SECTIONS_ONE, sums)
    else:
        shares = plain_scatter((keep_one, send_one), (keep_two, send_two), vblock)
        squares = sum(jnp.sum(share * share) for share in shares)
        sums = loss + jnp.where(lax.broadcasted_iota(i32, (8, 128), 1) == 0, squares, 0.0)
    sums = sum_all(sums, tuned)
    norm_value = jnp.sqrt(sums[0, 0])
    total_loss = sums[0, 1]
    clip_factor = jnp.minimum(1.0, CLIP_NORM / (norm_value + 1e-06))
    results = [total_loss, norm_value]
    if tuned:
        states = [views(v, j) for j in range(5) for v in (masters[j], moments[j], averages[j])]
        news = pl.pallas_call(
            update_kernel,
            out_shape=[sds(v.shape, f32) for v in states],
            in_specs=[SMEM] + [VMEM] * 17,
            compiler_params=params_of(24),
        )(clip_factor.reshape(1, 1), share_one, share_two, *states)
        for j in range(15):
            results.append(news[j].T[None] if j // 3 in (1, 3) else news[j][None] if j // 3 == 2 else news[j])
        vector_share = share_one[72:80].reshape(-1)[:vblock]
        results += list(advance(vector_weight, vector_moment, vector_average, vector_share, clip_factor))
    else:
        for weight, moment, average, share in zip(masters, moments, averages, shares):
            results += list(advance(weight, moment, average, share, clip_factor))
    return tuple(results)


def solution(mesh):
    split_rows, split_columns = P(("dp", "cls"), None), P(None, None, ("dp", "cls"))
    states = (
        [split_rows] * 3
        + [split_columns] * 3
        + [P(None, "dp", "cls")] * 3
        + [P(None, "cls", "dp")] * 3
        + [P("dp", "cls")] * 3
        + [P(("dp", "cls"))] * 3
    )
    in_specs = (
        P("dp", "cls", None),
        P("dp"),
        P("dp", "cls", None),
        P("dp", "cls"),
        P("dp"),
        P(),
        P(),
        P("dp", "cls"),
        *states,
    )
    out_specs = (P(), P(), *states)
    return jax.shard_map(on_device, mesh=mesh, in_specs=in_specs, out_specs=out_specs, check_vma=False)
```

```python
import functools
import math

import jax
import jax.numpy as jnp
from jax import lax
from jax.experimental import pallas as pl
from jax.experimental.pallas import tpu as pltpu
from jax.sharding import PartitionSpec as P

D = 384
HEADS = 6
HD = 64
FF = 1536
C = 1000
PD = 768
TOK = 197
PATCHES = 196
PARAMS = 2531176

NORM_EPS = 1e-06
SCORE_SCALE = 0.125
LOGIT_WEIGHT = 0.3
LABEL_WEIGHT = 0.8
MOMENTUM_DECAY = 0.9
AVERAGE_KEEP = 0.75
CLIP_NORM = 0.005
RATE = 0.03 * math.sqrt(PARAMS) / CLIP_NORM

ROWS_T = 208
GRID_DP, GRID_CLS = 8, 4
BLOCKS = GRID_DP * GRID_CLS
CPART = C // GRID_CLS
CPAD = 256
F_CHUNK = 512
R_ONE = 80
R_TWO = 128
R_MASK = 16
PIX_ROWS = 304
V_ROWS = 232
HEAD_AT = (TOK + 4) * D
LAYER_AT = HEAD_AT + C

bf16 = jnp.bfloat16
f32 = jnp.float32
i32 = jnp.int32

ANY = pl.BlockSpec(memory_space=pl.ANY)
VMEM = pl.BlockSpec(memory_space=pltpu.VMEM)
SMEM = pl.BlockSpec(memory_space=pltpu.SMEM)


def sds(shape, dtype):
    return jax.ShapeDtypeStruct(shape, dtype)


def cost(micros):
    return pl.CostEstimate(flops=int(micros * 1e8), bytes_accessed=1 << 20, transcendentals=0)


def params_of(limit_mib, **more):
    return pltpu.CompilerParams(vmem_limit_bytes=limit_mib << 20, **more)


def nn(a, b):
    return lax.dot_general(a, b, (((1,), (0,)), ((), ())), preferred_element_type=f32)


def nt(a, b):
    return lax.dot_general(a, b, (((1,), (1,)), ((), ())), preferred_element_type=f32)


def tn(a, b):
    return lax.dot_general(a, b, (((0,), (0,)), ((), ())), preferred_element_type=f32)


def gelu_parts(values):
    bell = jnp.exp(-0.5 * values * values)
    t = 1.0 / (1.0 + (0.3275911 * 0.5**0.5) * jnp.abs(values))
    tail = 0.5 * 1.061405429 * t - 0.5 * 1.453152027
    tail = tail * t + 0.5 * 1.421413741
    tail = tail * t - 0.5 * 0.284496736
    tail = (tail * t + 0.5 * 0.254829592) * t * bell
    return jnp.where(values < 0.0, tail, 1.0 - tail), bell * (1.0 / math.sqrt(2.0 * math.pi))


def normalize(values):
    centred = values - jnp.mean(values, axis=-1, keepdims=True)
    inverse = lax.rsqrt(jnp.mean(centred * centred, axis=-1, keepdims=True) + NORM_EPS)
    return (centred * inverse, inverse)


def normalize_back(unit, inverse, grad_unit):
    return inverse * (
        grad_unit
        - jnp.mean(grad_unit, axis=-1, keepdims=True)
        - unit * jnp.mean(grad_unit * unit, axis=-1, keepdims=True)
    )


def advance(weight, moment, average, grad, clip_factor):
    clipped = clip_factor * grad
    moment_new = MOMENTUM_DECAY * moment + clipped
    weight_new = weight - RATE * (clipped + MOMENTUM_DECAY * moment_new)
    average_new = AVERAGE_KEEP * average + (1.0 - AVERAGE_KEEP) * weight_new
    return (weight_new, moment_new, average_new)


def pack_head(block):
    a, b, c = block[..., :16, :], block[..., 16:32, :], block[..., 32:, :]
    top = jnp.concatenate([a, b[..., :128]], axis=-1)
    low = jnp.concatenate([b[..., 128:], c], axis=-1)
    return jnp.concatenate([top, low], axis=-2)


def unpack_head(block):
    top, low = block[..., :16, :], block[..., 16:, :]
    b = jnp.concatenate([top[..., 256:], low[..., :128]], axis=-1)
    return jnp.concatenate([top[..., :256], b, low[..., 128:]], axis=-2)


def me_of(tuned):
    if tuned:
        return lax.axis_index("dp") * GRID_CLS + lax.axis_index("cls")
    return 0


def grad_place(s):
    core, x, y, z = s & 1, (s >> 1) & 1, (s >> 2) & 1, s >> 3
    if z < 2:
        return core, (0 if x else 4) + 2 * y + z
    return core, (8 if y else 12) + 2 * x + (z - 2)


R_CODE = 16
SECTIONS_ONE = (0, 48, 72, 80)
SECTIONS_TWO = (0, 32, 80, 128)


def encode(block, sections, out):
    rows = sections[-1]
    powers = []
    for j, (a, b) in enumerate(zip(sections[:-1], sections[1:])):
        part = block[j] if isinstance(block, list) else block[a:b]
        most = jnp.max(jnp.abs(part), axis=0, keepdims=True)
        power = jnp.clip(jnp.ceil(jnp.log2(jnp.maximum(most, 1e-30))), -99.0, 126.0)
        code = jnp.round(part * jnp.exp2(15.0 - power))
        out[a:b, :] = jnp.clip(code, -32767.0, 32767.0).astype(i32).astype(jnp.int16)
        powers.append(power)
    powers.append(jnp.zeros((R_CODE - len(powers), D), f32))
    out[rows : rows + R_CODE, :] = jnp.concatenate(powers, axis=0).astype(i32).astype(jnp.int16)


def put_block(parts, sections, keep, send, core, place):
    if core:
        encode(parts, sections, send.at[place])
    else:
        for part, a, b in zip(parts, sections[:-1], sections[1:]):
            keep[place, a:b, :] = part


def decode(code, sections):
    rows = sections[-1]
    powers = code[rows : rows + R_CODE, :].astype(i32).astype(f32)
    return jnp.concatenate(
        [
            code[a:b, :].astype(i32).astype(f32) * jnp.exp2(powers[j : j + 1] - 15.0)
            for j, (a, b) in enumerate(zip(sections[:-1], sections[1:]))
        ],
        axis=0,
    )


def pack_mask(block):
    a, b, c = block[:8], block[8:16], block[16:]
    top = jnp.concatenate([a, b[:, :128]], axis=1)
    return jnp.concatenate([top, jnp.concatenate([b[:, 128:], c], axis=1)], axis=0)


def unpack_mask(block):
    top, low = block[:8], block[8:]
    b = jnp.concatenate([top[:, 256:], low[:, :128]], axis=1)
    return jnp.concatenate([top[:, :256], b, low[:, 128:]], axis=0)


def pack_weights_kernel(attn, patch, vec, up, down, head, seen, out):
    one, two = out.at[0:R_ONE], out.at[R_ONE:]
    one[0:48, :] = attn[...].astype(bf16)
    one[48:80, :] = jnp.concatenate([patch[...], vec[...]], axis=0).astype(bf16)
    block = jnp.concatenate([head[...], jnp.zeros((48, CPAD - CPART), f32)], axis=1)
    two[0:32, :] = pack_head(block).astype(bf16)
    two[32:80, :] = up[...].astype(bf16)
    two[80:128, :] = down[...].astype(bf16)
    mask = jnp.concatenate([seen[...].astype(f32), jnp.zeros((seen.shape[0], CPAD - CPART), f32)], axis=1)
    two[128:144, :] = pack_mask(mask).astype(bf16)


def pick_kernel(cur_own, rep_own, find, *refs):
    if find:
        owner, row, cur_labels, buf_labels, cur, buf, logits, o0, o1, far, meta, *scratch = refs
    else:
        row, cur, buf, logits, o0, o1, far, *scratch = refs
    stage, stage_cur, wide, wide_cur, soft, res, slots, sems = scratch
    parts, stored, _ = stage.shape
    kind = stage_cur.shape[1]
    chunk = 7
    copies = [pltpu.make_async_copy(cur, stage_cur, sems.at[parts // chunk])]
    for j in range(parts // chunk):
        part = pl.ds(j * chunk, chunk)
        copies.append(pltpu.make_async_copy(buf.at[part], stage.at[part], sems.at[j]))
    for copy in copies:
        copy.start()
    me = lax.axis_index("cls")
    if find:
        mine = lax.axis_index("dp")

        def look(i, count):
            hit = owner[i] == mine

            @pl.when(hit)
            def _():
                slots[count] = i

            return count + jnp.where(hit, 1, 0)

        lax.fori_loop(0, owner.shape[0], look, 0)
        for m in range(8):
            if m < cur_own:
                meta[0, m] = cur_labels[me * cur_own + m]
                meta[1, m] = 0
                meta[2, m] = mine * 3 * kind + me * cur_own + m
            elif m < cur_own + rep_own:
                i = slots[me * rep_own + m - cur_own]
                at = lax.rem(i, 2 * kind)
                meta[0, m] = jnp.where(at < kind, 0, buf_labels[row[i]])
                meta[1, m] = jnp.where(at < kind, 1, 2)
                meta[2, m] = lax.div(i, 2 * kind) * 3 * kind + kind + at
            else:
                meta[0, m] = 0
                meta[1, m] = 3
                meta[2, m] = 0
    else:
        for k in range(4 * rep_own):
            slots[k] = k
    soft[...] = jnp.zeros_like(soft)
    soft[:, :CPART] = logits[...].astype(f32)
    for j, copy in enumerate(copies):
        copy.wait()
        for lanes in range(PD // 128):
            at = slice(lanes * 128, (lanes + 1) * 128)
            if j == 0:
                wide_cur[lanes] = stage_cur[:, :, at].astype(f32).reshape(parts * kind, 128)
            else:
                one = stage[(j - 1) * chunk : j * chunk, :, at].astype(f32).reshape(chunk * stored, 128)
                wide[lanes, (j - 1) * chunk * stored : j * chunk * stored, :] = one
    images = cur_own + rep_own
    res[images * parts :, :] = jnp.zeros((PIX_ROWS - images * parts, PD), f32)
    for k, out in enumerate((o0, o1, far.at[0], far.at[1])):
        to = me ^ k
        for m in range(images):
            if m >= cur_own:
                r = row[slots[to * rep_own + m - cur_own]]
                at = (m % 3) * CPAD
                res[images * parts + m // 3 : images * parts + m // 3 + 1, at : at + CPAD] = soft[pl.ds(r, 1), :]
            for lanes in range(PD // 128):
                if m < cur_own:
                    one = wide_cur[lanes, pl.ds(to * cur_own + m, parts, stride=kind), :]
                else:
                    one = wide[lanes, pl.ds(r, parts, stride=stored), :]
                res[m * parts : (m + 1) * parts, lanes * 128 : (lanes + 1) * 128] = one
        out[...] = res[...].astype(bf16)


def spread_vector(vblock, blocks, flat):
    flat[...] = jnp.zeros_like(flat)
    lane = lax.broadcasted_iota(i32, (8, D), 1)
    for d in range(BLOCKS):
        q, s = divmod(vblock * d, D)
        b = blocks[d]
        if s:
            b = pltpu.roll(b, s, 1)
        flat[q : q + 8, :] = flat[q : q + 8, :] + jnp.where(lane >= s, b, 0.0)
        if s:
            flat[q + 1 : q + 9, :] = flat[q + 1 : q + 9, :] + jnp.where(lane < s, b, 0.0)


def cut_vector(vblock, flat, blocks):
    lane = lax.broadcasted_iota(i32, (8, D), 1)
    place = lax.broadcasted_iota(i32, (8, D), 0) * D + lane
    for d in range(BLOCKS):
        q, s = divmod(vblock * d, D)
        b = flat[q : q + 8, :]
        if s:
            a = pltpu.roll(b, D - s, 1)
            b = pltpu.roll(flat[q + 1 : q + 9, :], D - s, 1)
            b = jnp.where(lane < D - s, a, b)
        blocks[d] = jnp.where(place < vblock, b, 0.0)


def layer_vectors(flat):
    row, s = divmod(LAYER_AT, D)
    lane = lax.broadcasted_iota(i32, (12, D), 1)
    a = pltpu.roll(flat[row : row + 16, :], D - s, 1)
    return jnp.where(lane < D - s, a[0:12], a[1:13])


def head_vector(flat):
    rows = []
    wide = lax.broadcasted_iota(i32, (1, D), 1)
    for part in range(GRID_CLS):
        row, s = divmod(HEAD_AT + part * CPART, D)
        a = flat[row : row + 1, :]
        if s:
            a = pltpu.roll(jnp.broadcast_to(a, (8, D)), D - s, 1)[0:1]
            b = pltpu.roll(jnp.broadcast_to(flat[row + 1 : row + 2, :], (8, D)), D - s, 1)[0:1]
            a = jnp.where(wide < D - s, a, b)
        rows.append(jnp.where(wide < CPART, a, 0.0)[:, :CPAD])
    return jnp.concatenate(rows, axis=0)


def store_flat(flat, at, values, count):
    row, s = divmod(at, D)
    wide = lax.broadcasted_iota(i32, (1, D), 1)
    values = jnp.where(wide < count, values, 0.0)
    if s:
        values = pltpu.roll(jnp.broadcast_to(values, (8, D)), s, 1)[0:1]
        flat[row + 1 : row + 2, :] = flat[row + 1 : row + 2, :] + jnp.where(wide < s, values, 0.0)
    flat[row : row + 1, :] = flat[row : row + 1, :] + jnp.where(wide >= s, values, 0.0)


def pair_heads(low, first, second, axis):
    return jnp.where(low, first, second)


def embed_kernel(tuned, vblock, n, images, *refs):
    (w0, w1, w2, w3, w4, w5, w6, w7, p0, p1, p2, p3, x0_out, qkv_out, attn, prm, hb, soft,
     patch_wide, patch, blocks, flat, table, rows, x0_all) = refs
    weights = (w0, w1, w2, w3, w4, w5, w6, w7)
    p2 = p2.at[0]
    me = me_of(tuned)
    part = lax.axis_index("cls")
    per = PATCHES // 4

    @pl.when(pl.program_id(0) == 0)
    def _():
        for s in range(BLOCKS):
            d = s ^ me
            w = weights[s & 7]
            attn[pl.ds(pl.multiple_of(d * 48, 16), 48), :] = w[s >> 3, 0:48, :]
            rest = w[s >> 3, 48:80, :].astype(f32)
            patch_wide[pl.ds(pl.multiple_of(d * 24, 8), 24), :] = rest[0:24]
            blocks[d] = rest[24:32]
        patch[...] = patch_wide[...].astype(bf16)
        spread_vector(vblock, blocks, flat)
        prm[0:12, :] = layer_vectors(flat)
        prm[12:13, :] = flat[TOK + 1 : TOK + 2, :]
        prm[13:14, :] = flat[TOK + 2 : TOK + 3, :]
        prm[14:16, :] = jnp.zeros((2, D), f32)
        hb[0:4, :] = head_vector(flat)
        hb[4:8, :] = jnp.zeros((4, CPAD), f32)
        bias = flat[TOK : TOK + 1, :]
        table[...] = jnp.zeros_like(table)
        for k in range(4):
            for q in range(4):

                @pl.when((part ^ k) == q)
                def _(k=k, q=q):
                    table[k * per : k * per + per, :] = flat[1 + q * per : 1 + q * per + per, :] + bias

        table[PATCHES : PATCHES + 1, :] = flat[0:1, :] + flat[TOK + 3 : TOK + 4, :]
        soft[...] = jnp.zeros_like(soft)
        for k, piece in enumerate((p0, p1, p2, p3)):
            rows[k * PIX_ROWS : (k + 1) * PIX_ROWS, :] = nn(piece[...], patch[...])
            stored = piece[PIX_ROWS - 16 :, :].astype(f32)
            at = images * per - (PIX_ROWS - 16)
            for m in range(images):
                soft[part ^ k, m : m + 1, :] = stored[at + m // 3 : at + m // 3 + 1, (m % 3) * CPAD : (m % 3 + 1) * CPAD]
        for m in range(images):
            x0_all[m] = table[...]
            for k in range(4):
                at = slice(k * per, k * per + per)
                begin = k * PIX_ROWS + m * per
                x0_all[m, at, :] = x0_all[m, at, :] + rows[begin : begin + per, :]

    tokens = n * ROWS_T
    x0 = x0_all[pl.ds(pl.program_id(0) * n, n)]
    x0_out[...] = x0
    unit, _ = normalize(x0)
    normed = (unit * prm[0:1, :] + prm[1:2, :]).astype(bf16).reshape(tokens, D)
    for j, bias in ((0, prm[2:3, :]), (1, None), (2, prm[3:4, :])):
        one = nt(normed, attn[j * D : (j + 1) * D, :])
        if bias is not None:
            one = one + bias
        qkv_out[:, :, j * D : (j + 1) * D] = one.astype(bf16).reshape(n, ROWS_T, D)


def attend_kernel(n, w_out, prm, x0, qkv, att_out, x1_out):
    tokens = n * ROWS_T
    keys = lax.broadcasted_iota(i32, (ROWS_T, ROWS_T), 0) < TOK
    low = lax.broadcasted_iota(i32, (ROWS_T, 128), 1) < HD
    low_t = lax.broadcasted_iota(i32, (128, ROWS_T), 0) < HD
    for i in range(n):
        for p in range(HEADS // 2):
            at = p * 128
            q2 = qkv[i, :, at : at + 128]
            k2 = qkv[i, :, D + at : D + at + 128]
            v2 = qkv[i, :, 2 * D + at : 2 * D + at + 128]
            v2t = v2.T
            outs = []
            for head in range(2):
                ka = jnp.where(low if head == 0 else ~low, k2, jnp.zeros_like(k2))
                scores = jnp.where(keys, nt(ka, q2) * SCORE_SCALE, -1e30)
                top = jnp.max(scores, axis=0, keepdims=True)
                powers = jnp.exp(scores - top)
                probs = (powers * (1.0 / jnp.sum(powers, axis=0, keepdims=True))).astype(bf16)
                outs.append(nn(v2t, probs))
            both = jnp.where(low_t, outs[0], outs[1])
            att_out[i, :, at : at + 128] = both.T.astype(bf16)
    branch = nt(att_out[...].reshape(tokens, D), w_out[...]) + prm[4:5, :]
    x1_out[...] = x0[...] + branch.reshape(n, ROWS_T, D)


def middle_kernel(tuned, n, images, scales, *refs):
    if not tuned:
        given, *refs = refs
    (w0, w1, w2, w3, w4, w5, w6, w7, prm, hb, soft, meta, x1_in,
     dx1_out, keep, send, vgrad, hgrad, loss,
     w_up, w_down, w_head, act, slope, mask, masks_all, pooled, dpooled, glow, acc_up, acc_down,
     normed_all, dy_all, dup_all, up_bias, up_sum) = refs
    weights = (w0, w1, w2, w3, w4, w5, w6, w7)
    me = me_of(tuned)
    step = pl.program_id(0)
    last = pl.num_programs(0) - 1

    @pl.when(step == 0)
    def _():
        for s in range(BLOCKS):
            d = s ^ me
            dp, cl = d >> 2, d & 3
            w = weights[s & 7]
            rows = pl.ds(pl.multiple_of(dp * 48, 16), 48)
            w_head[cl, rows, :] = unpack_head(w[s >> 3, 0:32, :])
            columns = pl.ds(pl.multiple_of(cl * D, 128), D)
            w_up[rows, columns] = w[s >> 3, 32:80, :]
            w_down[rows, columns] = w[s >> 3, 80:128, :]
            if tuned:
                seen = unpack_mask(w[s >> 3, 128:144, :].astype(f32))
                masks_all[cl, pl.ds(pl.multiple_of(dp * 24, 8), 24), :] = seen
        if tuned:
            mask[...] = jnp.zeros_like(mask)
            for m in range(images):
                for q in range(4):
                    mask[q, m : m + 1, :] = masks_all[q, pl.ds(meta[2, m], 1), :]
        else:
            mask[...] = given[...]
        for c in range(4):
            up_bias[:, c * D : (c + 1) * D] = prm[8 + c : 9 + c, :]
        up_sum[...] = jnp.zeros_like(up_sum)
        vgrad[...] = jnp.zeros_like(vgrad)
        pooled[...] = jnp.zeros_like(pooled)

    tokens = n * ROWS_T
    x1 = x1_in[...].reshape(tokens, D)
    unit_two, inverse_two = normalize(x1)
    normed = (unit_two * prm[5:6, :] + prm[6:7, :]).astype(bf16)
    total = jnp.zeros((tokens, D), f32)
    mine = pl.ds(pl.multiple_of(step * tokens, 16), tokens)
    normed_all[mine, :] = normed
    chunks = [slice(c, c + F_CHUNK) for c in range(0, FF, F_CHUNK)]
    for c in chunks:
        pre = nn(normed, w_up[:, c]) + up_bias[:, c]
        half, bell = gelu_parts(pre)
        hot = (pre * half).astype(bf16)
        act[mine, c] = hot
        slope[:, c] = half + pre * bell
        total = total + nt(hot, w_down[:, c])
    x2 = x1 + (total + prm[7:8, :])
    unit, inverse = normalize(x2)
    real = lax.broadcasted_iota(i32, (ROWS_T, D), 0) < TOK
    sums = []
    for i in range(n):
        u = unit[i * ROWS_T : (i + 1) * ROWS_T]
        sums.append(jnp.sum(jnp.where(real, u, 0.0), axis=0, keepdims=True))
        pooled[pl.ds(step * n + i, 1), :] = sums[i] * (1.0 / TOK) * prm[12:13, :] + prm[13:14, :]

    low = pooled[...].astype(bf16)
    rows8 = (16, CPAD)
    row_id = lax.broadcasted_iota(i32, rows8, 0)
    lane = lax.broadcasted_iota(i32, rows8, 1)
    label = jnp.full(rows8, -1, i32)
    weight = jnp.zeros(rows8, f32)
    squared = jnp.zeros(rows8, f32)
    for i in range(images):
        kind = meta[1, i]
        label = jnp.where(row_id == i, meta[0, i], label)
        weight = jnp.where(row_id == i, jnp.where(kind == 0, scales[0], jnp.where(kind == 2, scales[1], 0.0)), weight)
        squared = jnp.where(row_id == i, jnp.where(kind == 1, 1.0, 0.0), squared)
    inside = lane < CPART
    logits, hots, lives, masks, tops = [], [], [], [], []
    pad = jnp.zeros((8, CPAD), f32)
    for q in range(4):
        one = nn(low, w_head[q]) + hb[q : q + 1, :]
        hot = (lane + q * CPART == label) & inside
        seen = (jnp.concatenate([mask[q], pad], axis=0) > 0.5) & inside
        logits.append(one)
        hots.append(hot)
        masks.append(seen)
        lives.append(seen | hot)
        tops.append(jnp.max(jnp.where(inside, one, -3e38), axis=1, keepdims=True))
    top = jnp.maximum(jnp.maximum(tops[0], tops[1]), jnp.maximum(tops[2], tops[3]))
    alive = sum(
        jnp.sum(jnp.where(lives[q], jnp.exp(logits[q] - top), 0.0), axis=1, keepdims=True) for q in range(4)
    )
    norm = top + jnp.log(alive)
    target = sum(jnp.sum(jnp.where(hots[q], logits[q], 0.0), axis=1, keepdims=True) for q in range(4))
    cross = norm - target
    value = jnp.sum(jnp.where(weight[:, 0:1] > 0, weight[:, 0:1] * cross, 0.0))
    back = jnp.zeros((16, D), f32)
    for q in range(4):
        gap = jnp.where(masks[q], logits[q] - jnp.concatenate([soft[q], pad], axis=0), 0.0)
        value = value + scales[2] * jnp.sum(squared * gap * gap)
        share = jnp.where(lives[q], jnp.exp(logits[q] - norm), 0.0)
        grad = weight * (share - jnp.where(hots[q], 1.0, 0.0)) + squared * (2.0 * scales[2]) * gap
        g = grad.astype(bf16)
        glow[q] = g
        back = back + nt(g, w_head[q])
    dpooled[...] = back

    pieces = []
    for i in range(n):
        grad = dpooled[pl.ds(step * n + i, 1), :]
        vgrad[12:13, :] = vgrad[12:13, :] + grad * (1.0 / TOK) * sums[i]
        vgrad[13:14, :] = vgrad[13:14, :] + grad
        dz = grad * (1.0 / TOK) * prm[12:13, :]
        u = unit[i * ROWS_T : (i + 1) * ROWS_T]
        d = inverse[i * ROWS_T : (i + 1) * ROWS_T] * (
            dz - jnp.mean(dz, axis=-1, keepdims=True) - u * jnp.mean(dz * u, axis=-1, keepdims=True)
        )
        pieces.append(jnp.where(real, d, 0.0))
    dx2 = jnp.concatenate(pieces, axis=0)
    dy = dx2.astype(bf16)
    vgrad[7:8, :] = vgrad[7:8, :] + jnp.sum(dy.astype(f32), axis=0, keepdims=True)
    dy_all[mine, :] = dy
    dnormed = jnp.zeros((tokens, D), f32)
    for c in chunks:
        dup = (nn(dy, w_down[:, c]) * slope[:, c]).astype(bf16)
        up_sum[:, c] = up_sum[:, c] + jnp.sum(dup.astype(f32), axis=0, keepdims=True)
        dup_all[mine, c] = dup
        dnormed = dnormed + nt(dup, w_up[:, c])
    vgrad[5:6, :] = vgrad[5:6, :] + jnp.sum(dnormed * unit_two, axis=0, keepdims=True)
    vgrad[6:7, :] = vgrad[6:7, :] + jnp.sum(dnormed, axis=0, keepdims=True)
    dx1 = dx2 + normalize_back(unit_two, inverse_two, dnormed * prm[5:6, :])
    dx1_out[...] = dx1.reshape(n, ROWS_T, D)

    @pl.when(step == last)
    def _():
        loss[...] = jnp.where(lax.broadcasted_iota(i32, loss.shape, 1) == 0, 0.0, value)
        hgrad[...] = jnp.zeros_like(hgrad)
        for q in range(4):
            hgrad[q : q + 1, :] = jnp.sum(glow[q].astype(f32), axis=0, keepdims=True)
        for c in range(4):
            vgrad[8 + c : 9 + c, :] = up_sum[:, c * D : (c + 1) * D]
        for q in range(4):
            slope[0:D, q * CPAD : (q + 1) * CPAD] = tn(low, glow[q])
        for c in chunks:
            acc_down[:, c] = tn(dy_all[...], act[:, c])
            acc_up[:, c] = tn(normed_all[...], dup_all[:, c])
        for s in range(BLOCKS):
            d = s ^ me
            dp, cl = d >> 2, d & 3
            core, place = grad_place(s)
            rows = pl.ds(pl.multiple_of(dp * 48, 8), 48)
            columns = pl.ds(pl.multiple_of(cl * D, 128), D)
            head = slope[rows, pl.ds(pl.multiple_of(cl * CPAD, 128), CPAD)]
            block = [pack_head(head), acc_up[rows, columns], acc_down[rows, columns]]
            put_block(block, SECTIONS_TWO, keep, send, core, place)


def run_middle(tuned, n, images, scales, *operands):
    steps = images // n
    whole = lambda shape: pl.BlockSpec(shape, lambda i: (0,) * len(shape))
    per = lambda width: pl.BlockSpec((n, ROWS_T, width), lambda i: (i, 0, 0))
    return pl.pallas_call(
        functools.partial(middle_kernel, tuned, n, images, scales),
        grid=(steps,),
        in_specs=[whole((4, 8, CPAD))] * (0 if tuned else 1)
        + [whole((4, R_TWO + R_MASK, D))] * 8
        + [whole((16, D)), whole((8, CPAD)), whole((4, 8, CPAD))]
        + [SMEM, per(D)],
        out_specs=[
            per(D),
            whole((16, R_TWO, D)),
            whole((16, R_TWO + R_CODE, D)),
            whole((16, D)),
            whole((8, CPAD)),
            whole((8, 128)),
        ],
        out_shape=[
            sds((images, ROWS_T, D), f32),
            sds((16, R_TWO, D), f32),
            sds((16, R_TWO + R_CODE, D), jnp.int16),
            sds((16, D), f32),
            sds((8, CPAD), f32),
            sds((8, 128), f32),
        ],
        scratch_shapes=[
            pltpu.VMEM((D, FF), bf16),
            pltpu.VMEM((D, FF), bf16),
            pltpu.VMEM((4, D, CPAD), bf16),
            pltpu.VMEM((images * ROWS_T, FF), bf16),
            pltpu.VMEM((n * ROWS_T, FF), f32),
            pltpu.VMEM((4, 8, CPAD), f32),
            pltpu.VMEM((4, GRID_DP * 24, CPAD), f32),
            pltpu.VMEM((16, D), f32),
            pltpu.VMEM((16, D), f32),
            pltpu.VMEM((4, 16, CPAD), bf16),
            pltpu.VMEM((D, FF), f32),
            pltpu.VMEM((D, FF), f32),
            pltpu.VMEM((images * ROWS_T, D), bf16),
            pltpu.VMEM((images * ROWS_T, D), bf16),
            pltpu.VMEM((images * ROWS_T, FF), bf16),
            pltpu.VMEM((1, FF), f32),
            pltpu.VMEM((1, FF), f32),
        ],
        cost_estimate=cost(30),
        compiler_params=params_of(36),
    )(*operands)


def attend_back_kernel(n, first, *refs):
    if first:
        (w_out, vgrad_in, qkv, att, dx1_in, dqkv, acc, vgrad) = refs
    else:
        (w_out, vgrad_in, qkv, att, dx1_in, acc_in, _, dqkv, acc, vgrad) = refs

    @pl.when(pl.program_id(0) == 0)
    def _():
        acc[...] = jnp.zeros_like(acc) if first else acc_in[...]
        vgrad[...] = vgrad_in[...]

    tokens = n * ROWS_T
    dout = dx1_in[...].reshape(tokens, D).astype(bf16)
    vgrad[4:5, :] = vgrad[4:5, :] + jnp.sum(dout.astype(f32), axis=0, keepdims=True)
    acc[...] = acc[...] + tn(dout, att[...].reshape(tokens, D))
    datt = nn(dout, w_out[...]).astype(bf16)
    keys = lax.broadcasted_iota(i32, (ROWS_T, ROWS_T), 0) < TOK
    low = lax.broadcasted_iota(i32, (ROWS_T, 128), 1) < HD
    low_t = lax.broadcasted_iota(i32, (128, ROWS_T), 0) < HD
    for i in range(n):
        rows = slice(i * ROWS_T, (i + 1) * ROWS_T)
        for p in range(HEADS // 2):
            at = p * 128
            q2 = qkv[i, :, at : at + 128]
            k2 = qkv[i, :, D + at : D + at + 128]
            v2 = qkv[i, :, 2 * D + at : 2 * D + at + 128]
            do = datt[rows, at : at + 128]
            k2t = k2.T
            dqs, dks, dvs = [], [], []
            for head in range(2):
                side = low if head == 0 else ~low
                ka = jnp.where(side, k2, jnp.zeros_like(k2))
                va = jnp.where(side, v2, jnp.zeros_like(v2))
                scores = jnp.where(keys, nt(ka, q2) * SCORE_SCALE, -1e30)
                top = jnp.max(scores, axis=0, keepdims=True)
                powers = jnp.exp(scores - top)
                probs = powers * (1.0 / jnp.sum(powers, axis=0, keepdims=True))
                dprobs = nt(va, do)
                mean = jnp.sum(probs * dprobs, axis=0, keepdims=True)
                dscores = (probs * (dprobs - mean)).astype(bf16)
                dks.append(nn(dscores, q2))
                dqs.append(nn(k2t, dscores))
                dvs.append(nn(probs.astype(bf16), do))
            dq = (jnp.where(low_t, dqs[0], dqs[1]) * SCORE_SCALE).T
            dqkv[i, :, at : at + 128] = dq.astype(bf16)
            dqkv[i, :, D + at : D + at + 128] = (jnp.where(low, dks[0], dks[1]) * SCORE_SCALE).astype(bf16)
            dqkv[i, :, 2 * D + at : 2 * D + at + 128] = jnp.where(low, dvs[0], dvs[1]).astype(bf16)


def unit_back_kernel(n, w_in, prm, vgrad_in, x0, dqkv_in, dx1_in, dx0_out, vgrad):
    @pl.when(pl.program_id(0) == 0)
    def _():
        vgrad[...] = vgrad_in[...]

    tokens = n * ROWS_T
    dx1 = dx1_in[...].reshape(tokens, D)
    dqkv = dqkv_in[...].reshape(tokens, 3 * D)
    vgrad[2:3, :] = vgrad[2:3, :] + jnp.sum(dqkv[:, 0:D].astype(f32), axis=0, keepdims=True)
    vgrad[3:4, :] = vgrad[3:4, :] + jnp.sum(dqkv[:, 2 * D : 3 * D].astype(f32), axis=0, keepdims=True)
    unit, inverse = normalize(x0[...].reshape(tokens, D))
    dnormed = nn(dqkv, w_in[...])
    vgrad[0:1, :] = vgrad[0:1, :] + jnp.sum(dnormed * unit, axis=0, keepdims=True)
    vgrad[1:2, :] = vgrad[1:2, :] + jnp.sum(dnormed, axis=0, keepdims=True)
    dx0 = dx1 + normalize_back(unit, inverse, dnormed * prm[0:1, :])
    dx0_out[...] = dx0.reshape(n, ROWS_T, D)


def qkv_back_kernel(n, prm, x0, dqkv_in, acc):
    @pl.when(pl.program_id(0) == 0)
    def _():
        acc[...] = jnp.zeros_like(acc)

    tokens = n * ROWS_T
    dqkv = dqkv_in[...].reshape(tokens, 3 * D)
    unit, _ = normalize(x0[...].reshape(tokens, D))
    normed = (unit * prm[0:1, :] + prm[1:2, :]).astype(bf16)
    for j in range(3):
        at = slice(j * D, (j + 1) * D)
        acc[at, :] = acc[at, :] + tn(dqkv[:, at], normed)


def embed_back_kernel(tuned, vblock, images, *refs):
    (vgrad, hgrad, acc_in, acc_out, p0, p1, p2, p3, dx0_all, keep, send, acc, acc_patch, rows, flat, blocks) = refs
    p2 = p2.at[0]
    me = me_of(tuned)
    part = lax.axis_index("cls")
    per = PATCHES // 4
    acc[0 : 3 * D, :] = acc_in[...]
    acc[3 * D : 4 * D, :] = acc_out[...]
    rows[...] = jnp.zeros_like(rows)
    for m in range(images):
        for k in range(4):
            begin = k * PIX_ROWS + m * per
            rows[begin : begin + per, :] = dx0_all[m, k * per : k * per + per, :]
    low = rows[...].astype(bf16)
    total = tn(p0[...], low[:PIX_ROWS])
    for k, piece in ((1, p1), (2, p2), (3, p3)):
        total = total + tn(piece[...], low[k * PIX_ROWS : (k + 1) * PIX_ROWS])
    acc_patch[...] = total
    position = dx0_all[0]
    for m in range(1, images):
        position = position + dx0_all[m]
    flat[...] = jnp.zeros_like(flat)
    for k in range(4):
        for q in range(4):

            @pl.when((part ^ k) == q)
            def _(k=k, q=q):
                flat[1 + q * per : 1 + q * per + per, :] = position[k * per : k * per + per, :]

    first = position[PATCHES : PATCHES + 1, :]
    flat[0:1, :] = first
    flat[TOK : TOK + 1, :] = jnp.sum(position[0:PATCHES, :], axis=0, keepdims=True)
    flat[TOK + 1 : TOK + 2, :] = vgrad[12:13, :]
    flat[TOK + 2 : TOK + 3, :] = vgrad[13:14, :]
    flat[TOK + 3 : TOK + 4, :] = first
    for q in range(GRID_CLS):
        wide = jnp.concatenate([hgrad[q : q + 1, :], jnp.zeros((1, D - CPAD), f32)], axis=1)
        store_flat(flat, HEAD_AT + q * CPART, wide, CPART)
    for j in range(12):
        store_flat(flat, LAYER_AT + j * D, vgrad[j : j + 1, :], D)
    cut_vector(vblock, flat, blocks)
    for s in range(BLOCKS):
        d = s ^ me
        core, place = grad_place(s)
        rows48, rows24 = pl.ds(pl.multiple_of(d * 48, 8), 48), pl.ds(pl.multiple_of(d * 24, 8), 24)
        put_block([acc[rows48, :], acc_patch[rows24, :], blocks[d]], SECTIONS_ONE, keep, send, core, place)


def update_kernel(clip_ref, one, two, *refs):
    ins, outs = refs[:15], refs[15:]
    clip = clip_ref[0, 0]
    grads = [
        one[48:72, :],
        one[0:48, :],
        two[32:80, :],
        two[80:128, :],
        unpack_head(two[0:32, :])[:, :CPART],
    ]
    for j, grad in enumerate(grads):
        news = advance(ins[3 * j][...], ins[3 * j + 1][...], ins[3 * j + 2][...], grad, clip)
        for k in range(3):
            outs[3 * j + k][...] = news[k]


def flip(n, k):
    return [(i, i ^ k) for i in range(n)]


def to_core(v):
    return lax.ppermute(v, "cls", flip(4, 1))


def to_x(v):
    return lax.ppermute(v, "cls", flip(4, 2))


def to_y(v):
    return lax.ppermute(v, "dp", flip(8, 1))


def to_z(v, k):
    return lax.ppermute(v, "dp", flip(8, 2 * k))


def gather_blocks(near, at_x, at_y, at_xy):
    return [near, to_core(near), at_x, to_core(at_x), at_y, to_core(at_y), at_xy, to_core(at_xy)]


def first_kernel(sections, keep, got, send_a, keep_a, send_b, keep_b):
    encode(keep[0, 0] + decode(got.at[0, 0], sections), sections, send_a.at[0])
    keep_a[0] = keep[1, 0] + decode(got.at[1, 0], sections)
    encode(keep[2, 0] + decode(got.at[2, 0], sections), sections, send_b.at[0])
    keep_b[0] = keep[3, 0] + decode(got.at[3, 0], sections)


def second_kernel(sections, keep_a, keep_b, got_a, got_b, send_a, rest_a, send_b, rest_b):
    for keep, got, send, rest in ((keep_a, got_a, send_a, rest_a), (keep_b, got_b, send_b, rest_b)):
        rest[0] = keep[0, 0] + decode(got.at[0, 0], sections)
        encode(keep[1, 0] + decode(got.at[1, 0], sections), sections, send.at[0])


def third_kernel(sections, keep_a, keep_b, got_a, got_b, own, send_1, send_2, send_3):
    own[...] = keep_a[0] + decode(got_a.at[0], sections)
    encode(keep_a[1] + decode(got_a.at[1], sections), sections, send_1)
    encode(keep_b[0] + decode(got_b.at[0], sections), sections, send_2)
    encode(keep_b[1] + decode(got_b.at[1], sections), sections, send_3)


def third_pair_kernel(sections, keep_a, keep_b, got_a, got_b, rest, send):
    for j, (keep, got) in enumerate(((keep_a, got_a), (keep_b, got_b))):
        rest[j] = keep[0] + decode(got.at[0], sections)
        encode(keep[1] + decode(got.at[1], sections), sections, send.at[j])


def near_kernel(sections, rest, got, own, send):
    own[...] = rest[0] + decode(got.at[0], sections)
    encode(rest[1] + decode(got.at[1], sections), sections, send)


def fourth_kernel(sections, own, *refs):
    *got, before, share, sums = refs
    total = own[...]
    for code in got:
        total = total + decode(code, sections)
    share[...] = total
    lane = lax.broadcasted_iota(i32, (8, 128), 1)
    sums[...] = before[...] + jnp.where(lane == 0, jnp.sum(total * total), 0.0)


def scatter_first(keep, got, sections):
    rows = sections[-1]
    quarters = [pl.BlockSpec((4, 1, r, D), lambda j: (0, j, 0, 0)) for r in (rows, rows + R_CODE)]
    wide, code = pl.BlockSpec((1, rows, D), lambda j: (j, 0, 0)), pl.BlockSpec((1, rows + R_CODE, D), lambda j: (j, 0, 0))
    return pl.pallas_call(
        functools.partial(first_kernel, sections),
        grid=(4,),
        in_specs=quarters,
        out_specs=[code, wide, code, wide],
        out_shape=[sds((4, rows + R_CODE, D), jnp.int16), sds((4, rows, D), f32)] * 2,
        cost_estimate=cost(4),
        compiler_params=params_of(16),
    )(*[v.reshape((4, 4) + v.shape[1:]) for v in (keep, got)])


def scatter_second(keep_a, keep_b, got_a, got_b, sections):
    rows = sections[-1]
    pairs, codes = [pl.BlockSpec((2, 1, r, D), lambda j: (0, j, 0, 0)) for r in (rows, rows + R_CODE)]
    wide, code = [pl.BlockSpec((1, r, D), lambda j: (j, 0, 0)) for r in (rows, rows + R_CODE)]
    return pl.pallas_call(
        functools.partial(second_kernel, sections),
        grid=(2,),
        in_specs=[pairs] * 2 + [codes] * 2,
        out_specs=[code, wide, code, wide],
        out_shape=[sds((2, rows + R_CODE, D), jnp.int16), sds((2, rows, D), f32)] * 2,
        cost_estimate=cost(2),
        compiler_params=params_of(16),
    )(*[v.reshape((2, 2) + v.shape[1:]) for v in (keep_a, keep_b, got_a, got_b)])


def scatter_third(keep_a, keep_b, got_a, got_b, sections):
    rows = sections[-1]
    return pl.pallas_call(
        functools.partial(third_kernel, sections),
        out_shape=[sds((rows, D), f32)] + [sds((rows + R_CODE, D), jnp.int16)] * 3,
        cost_estimate=cost(2),
        compiler_params=params_of(16),
    )(keep_a, keep_b, got_a, got_b)


def scatter_third_pair(keep_a, keep_b, got_a, got_b, sections):
    rows = sections[-1]
    return pl.pallas_call(
        functools.partial(third_pair_kernel, sections),
        out_shape=[sds((2, rows, D), f32), sds((2, rows + R_CODE, D), jnp.int16)],
        compiler_params=params_of(16),
    )(keep_a, keep_b, got_a, got_b)


def scatter_near(rest, got, sections):
    rows = sections[-1]
    return pl.pallas_call(
        functools.partial(near_kernel, sections),
        out_shape=[sds((rows, D), f32), sds((rows + R_CODE, D), jnp.int16)],
        compiler_params=params_of(16),
    )(rest, got)


def scatter_fourth(own, got, sections, before):
    return pl.pallas_call(
        functools.partial(fourth_kernel, sections),
        out_shape=[sds(own.shape, f32), sds((8, 128), f32)],
        cost_estimate=cost(2),
        compiler_params=params_of(16),
    )(own, *got, before)


def sum_all(v, tuned):
    if not tuned:
        return lax.psum(v, ("dp", "cls"))
    v = v + to_core(v)
    v = (v + to_x(v)) + (to_y(v) + lax.ppermute(v, ("dp", "cls"), flip(BLOCKS, GRID_CLS + 2)))
    return (v + to_z(v, 1)) + (to_z(v, 2) + to_z(v, 3))


def plain_gather(masters, vblock):
    patch, attention, up, down, head, vector = [w.astype(bf16) for w in masters]
    both = ("dp", "cls")
    patch = lax.all_gather(patch, both, axis=0, tiled=True).reshape(BLOCKS, 24, D)
    attention = lax.all_gather(attention, both, axis=2, tiled=True)[0].T.reshape(BLOCKS, 48, D)
    vector = lax.all_gather(vector, both, axis=0, tiled=True).reshape(BLOCKS, vblock)
    vector = jnp.pad(vector, ((0, 0), (0, 8 * D - vblock))).reshape(BLOCKS, 8, D)
    up = lax.all_gather(lax.all_gather(up, "dp", axis=1, tiled=True), "cls", axis=2, tiled=True)[0]
    down = lax.all_gather(lax.all_gather(down, "dp", axis=2, tiled=True), "cls", axis=1, tiled=True)[0].T
    head = lax.all_gather(lax.all_gather(head, "dp", axis=0, tiled=True), "cls", axis=1, tiled=True)
    up, down = [
        w.reshape(GRID_DP, 48, GRID_CLS, D).transpose(0, 2, 1, 3).reshape(BLOCKS, 48, D) for w in (up, down)
    ]
    head = head.reshape(GRID_DP, 48, GRID_CLS, CPART).transpose(0, 2, 1, 3).reshape(BLOCKS, 48, CPART)
    head = pack_head(jnp.pad(head, ((0, 0), (0, 0), (0, CPAD - CPART))))
    one = jnp.concatenate([attention, patch, vector], axis=1).reshape(4, 8, R_ONE, D)
    two = jnp.concatenate([head, up, down], axis=1).reshape(4, 8, R_TWO, D)
    return [one[:, a] for a in range(8)], [two[:, a] for a in range(8)]


def plain_scatter(one, two, vblock):
    def in_order(keep, send, sections):
        send = [decode(send[j], sections) for j in range(16)]
        return jnp.stack([(keep, send)[grad_place(s)[0]][grad_place(s)[1]] for s in range(BLOCKS)])

    one, two = in_order(*one, SECTIONS_ONE), in_order(*two, SECTIONS_TWO)
    both = ("dp", "cls")
    attention = one[:, 0:48].reshape(4 * D, D).T[None]
    patch = one[:, 48:72].reshape(PD, D)
    vector = one[:, 72:80].reshape(BLOCKS, 8 * D)[:, :vblock].reshape(-1)
    up, down = [
        w.reshape(GRID_DP, GRID_CLS, 48, D).transpose(0, 2, 1, 3).reshape(D, FF)
        for w in (two[:, 32:80], two[:, 80:128])
    ]
    head = unpack_head(two[:, 0:32])[:, :, :CPART]
    head = head.reshape(GRID_DP, GRID_CLS, 48, CPART).transpose(0, 2, 1, 3).reshape(D, C)

    def split(v, at_dp, at_cls):
        v = lax.psum_scatter(v, "dp", scatter_dimension=at_dp, tiled=True)
        return lax.psum_scatter(v, "cls", scatter_dimension=at_cls, tiled=True)

    return (
        lax.psum_scatter(patch, both, scatter_dimension=0, tiled=True),
        lax.psum_scatter(attention, both, scatter_dimension=2, tiled=True),
        split(up, 0, 1)[None],
        split(down.T, 1, 0)[None],
        split(head, 0, 1),
        lax.psum_scatter(vector, both, scatter_dimension=0, tiled=True),
    )


def take_rows_kernel(rows, source, out, sem):
    def one(i, carry):
        copy = pltpu.make_async_copy(source.at[rows[i]], out.at[i], sem)
        copy.start()
        copy.wait()
        return carry

    lax.fori_loop(0, out.shape[0], one, 0)


def take_rows(source, rows):
    return pl.pallas_call(
        take_rows_kernel,
        out_shape=sds((rows.shape[0],) + source.shape[1:], source.dtype),
        in_specs=[SMEM, ANY],
        out_specs=ANY,
        scratch_shapes=[pltpu.SemaphoreType.DMA(())],
    )(rows, source)


def pick_small(source, rows):
    hot = (rows[:, None] == jnp.arange(source.shape[0])[None, :]).astype(f32)
    return jnp.dot(hot, source.astype(f32), precision=lax.Precision.HIGHEST)


def plain_replay(buffer_patches, buffer_logits, buffer_labels, replay_owner, replay_row, kind_rows):
    dp_count, dp_index = lax.axis_size("dp"), lax.axis_index("dp")
    replay_count = 2 * kind_rows
    capacity = max(2, -(-replay_count // dp_count))
    table = lax.all_gather(buffer_labels, "dp", axis=0, tiled=True)
    owners = replay_owner[:, 0].reshape(dp_count, replay_count)
    local_rows = replay_row.reshape(dp_count, replay_count)
    earlier = jnp.arange(replay_count)[None, :] < jnp.arange(replay_count)[:, None]
    same_owner = owners[:, :, None] == owners[:, None, :]
    ranks = jnp.sum(jnp.where(same_owner & earlier[None], 1, 0), axis=2).astype(i32)
    slot_ids = jnp.arange(capacity, dtype=i32)
    wanted = (owners == dp_index)[:, :, None] & (ranks[:, :, None] == slot_ids[None, None, :])
    slot_rows = jnp.sum(jnp.where(wanted, local_rows[:, :, None], 0), axis=1).reshape(-1)
    pixels = take_rows(buffer_patches, slot_rows)
    logits = pick_small(buffer_logits, slot_rows).astype(bf16)
    pixels = lax.all_to_all(pixels, "dp", split_axis=0, concat_axis=0, tiled=True)
    logits = lax.all_to_all(logits, "dp", split_axis=0, concat_axis=0, tiled=True)
    my_owners, my_ranks, my_rows = [
        lax.dynamic_index_in_dim(v, dp_index, 0, keepdims=False) for v in (owners, ranks, local_rows)
    ]
    places = my_owners * buffer_labels.shape[0] + my_rows
    labels = jnp.sum(jnp.where(places[:, None] == jnp.arange(table.shape[0])[None, :], table[None, :], 0), axis=1)
    return pixels, logits, labels.astype(i32), (my_owners * capacity + my_ranks).astype(i32)


def on_device(
    current_patches,
    current_labels,
    buffer_patches,
    buffer_logits,
    buffer_labels,
    replay_owner,
    replay_row,
    seen_mask,
    patch_weight,
    patch_moment,
    patch_average,
    attention_weight,
    attention_moment,
    attention_average,
    up_weight,
    up_moment,
    up_average,
    down_weight,
    down_moment,
    down_average,
    head_weight,
    head_moment,
    head_average,
    vector_weight,
    vector_moment,
    vector_average,
):
    dp_count, cls_count = lax.axis_size("dp"), lax.axis_size("cls")
    dp_index, cls_index = lax.axis_index("dp"), lax.axis_index("cls")
    kind_rows = current_patches.shape[0]
    replay_count = 2 * kind_rows
    group_rows = 3 * kind_rows
    normal_count = kind_rows * dp_count
    patch_part = current_patches.shape[1]
    cur_own, rep_own = kind_rows // cls_count, replay_count // cls_count
    images = cur_own + rep_own
    class_part = head_weight.shape[1]
    vblock = vector_weight.shape[0] * dp_count * cls_count // BLOCKS
    tuned = dp_count == GRID_DP and cls_count == GRID_CLS and replay_count == 2 * dp_count
    masters = (patch_weight, attention_weight, up_weight, down_weight, head_weight, vector_weight)
    moments = (patch_moment, attention_moment, up_moment, down_moment, head_moment, vector_moment)
    averages = (patch_average, attention_average, up_average, down_average, head_average, vector_average)

    def views(v, j):
        return v[0].T if j in (1, 3) else v[0] if j == 2 else v

    current_view, buffer_view = current_patches.transpose(1, 0, 2), buffer_patches.transpose(1, 0, 2)
    if tuned:
        pack = pl.pallas_call(
            pack_weights_kernel,
            out_shape=sds((R_ONE + R_TWO + R_MASK, D), bf16),
            cost_estimate=cost(2),
            compiler_params=params_of(60),
        )

    def exchange(sent):
        own, near, far = sent
        far = lax.ppermute(far, "cls", flip(4, 2))
        return [own, lax.ppermute(near, "cls", flip(4, 1)), far, lax.ppermute(far[1], "cls", flip(4, 1))]

    def pick(find, stored, *operands):
        out_shape = [sds((PIX_ROWS, PD), bf16)] * 2 + [sds((2, PIX_ROWS, PD), bf16)]
        return pl.pallas_call(
            functools.partial(pick_kernel, cur_own, rep_own, find),
            out_shape=out_shape + ([sds((3, 8), i32)] if find else []),
            in_specs=[SMEM] * (4 if find else 1) + [ANY, ANY, VMEM],
            out_specs=[VMEM] * 3 + ([SMEM] if find else []),
            scratch_shapes=[
                pltpu.VMEM((patch_part, stored, PD), bf16),
                pltpu.VMEM((patch_part, kind_rows, PD), bf16),
                pltpu.VMEM((PD // 128, patch_part * stored, 128), f32),
                pltpu.VMEM((PD // 128, patch_part * kind_rows, 128), f32),
                pltpu.VMEM((stored, CPAD), f32),
                pltpu.VMEM((PIX_ROWS, PD), f32),
                pltpu.SMEM((replay_count,), i32),
                pltpu.SemaphoreType.DMA((patch_part // 7 + 1,)),
            ],
            cost_estimate=cost(7),
            compiler_params=params_of(60),
        )(*operands)

    if tuned:
        *sent, meta = pick(
            True,
            buffer_patches.shape[0],
            replay_owner.reshape(-1),
            replay_row,
            current_labels,
            buffer_labels,
            current_view,
            buffer_view,
            buffer_logits,
        )
        got = exchange(sent)
        got[1], vec = lax.optimization_barrier((got[1], vector_weight))
        vec = jnp.pad(vec, (0, 8 * D - vblock)).reshape(8, D)
        packed = pack(
            views(attention_weight, 1), patch_weight, vec, views(up_weight, 2), views(down_weight, 3), head_weight, seen_mask
        )
    else:
        moved, logits, labels, places = plain_replay(
            buffer_patches, buffer_logits, buffer_labels, replay_owner, replay_row, kind_rows
        )
        sent = pick(False, moved.shape[0], places, current_view, moved.transpose(1, 0, 2), logits)
        got = exchange(sent)
        row_mask = jnp.pad(seen_mask.astype(bf16), ((0, 0), (0, CPAD - class_part)))
        row_mask = lax.all_gather(row_mask, "cls").astype(f32)
        mask_rows = [
            lax.dynamic_slice_in_dim(row_mask, cls_index * cur_own, cur_own, 1),
            lax.dynamic_slice_in_dim(row_mask, kind_rows + cls_index * rep_own, rep_own, 1),
            jnp.zeros((cls_count, 8 - images, CPAD), f32),
        ]
        given = jnp.concatenate(mask_rows, axis=1)
        kinds = jnp.where(jnp.arange(replay_count) < kind_rows, 1, 2).astype(i32)
        labels = jnp.where(kinds == 1, 0, labels)

        def own(current, replayed, fill):
            return jnp.concatenate(
                [
                    lax.dynamic_slice_in_dim(current, cls_index * cur_own, cur_own, 0),
                    lax.dynamic_slice_in_dim(replayed, cls_index * rep_own, rep_own, 0),
                    jnp.full((8 - images,), fill, i32),
                ]
            )

        nothing = jnp.zeros_like(current_labels)
        meta = jnp.stack([own(current_labels, labels, 0), own(nothing, kinds, 3), jnp.zeros((8,), i32)])

    if tuned:
        column = [packed] + [to_z(packed, k) for k in (1, 2, 3)]
        near_one = jnp.stack([v[:R_ONE] for v in column])
        near_two = jnp.stack([v[R_ONE:] for v in column])
        near_one, got[2] = lax.optimization_barrier((near_one, got[2]))
        at_x, at_y = to_x(near_one), to_y(near_one)
        at_x, near_two = lax.optimization_barrier((at_x, near_two))
        at_x, at_y, at_xy = lax.optimization_barrier((at_x, at_y, to_y(at_x)))
        one = gather_blocks(near_one, at_x, at_y, at_xy)
        two_x, two_y = to_x(near_two), to_y(near_two)
    else:
        one, two = plain_gather(masters, vblock)
        two = [jnp.pad(v, ((0, 0), (0, R_MASK), (0, 0))) for v in two]

    n = 2
    steps = images // n
    whole = lambda shape: pl.BlockSpec(shape, lambda i: (0,) * len(shape))
    per = lambda width: pl.BlockSpec((n, ROWS_T, width), lambda i: (i, 0, 0))
    pieces = [whole((PIX_ROWS, PD))] * 2 + [pl.BlockSpec((1, PIX_ROWS, PD), lambda i: (0, 0, 0)), whole((PIX_ROWS, PD))]
    x0, qkv, attn, prm, hb, soft = pl.pallas_call(
        functools.partial(embed_kernel, tuned, vblock, n, images),
        grid=(steps,),
        in_specs=[whole((4, R_ONE, D))] * 8 + pieces,
        out_specs=[per(D), per(3 * D)] + [whole(shape) for shape in ((4 * D, D), (16, D), (8, CPAD), (4, 8, CPAD))],
        out_shape=[
            sds((images, ROWS_T, D), f32),
            sds((images, ROWS_T, 3 * D), bf16),
            sds((4 * D, D), bf16),
            sds((16, D), f32),
            sds((8, CPAD), f32),
            sds((4, 8, CPAD), f32),
        ],
        scratch_shapes=[
            pltpu.VMEM((PD, D), f32),
            pltpu.VMEM((PD, D), bf16),
            pltpu.VMEM((BLOCKS, 8, D), f32),
            pltpu.VMEM((V_ROWS, D), f32),
            pltpu.VMEM((ROWS_T, D), f32),
            pltpu.VMEM((4 * PIX_ROWS, D), f32),
            pltpu.VMEM((images, ROWS_T, D), f32),
        ],
        cost_estimate=cost(8),
        compiler_params=params_of(34),
    )(*one, *got)
    if tuned:
        two_x, two_y, hb = lax.optimization_barrier((two_x, two_y, hb))
        two_xy = to_y(two_x)
    out_part = pl.BlockSpec((D, D), lambda i: (3, 0))
    att, x1 = pl.pallas_call(
        functools.partial(attend_kernel, n),
        grid=(steps,),
        in_specs=[out_part, whole((16, D)), per(D), per(3 * D)],
        out_specs=[per(D), per(D)],
        out_shape=[sds((images, ROWS_T, D), bf16), sds((images, ROWS_T, D), f32)],
        cost_estimate=cost(10),
        compiler_params=params_of(20),
    )(attn, prm, x0, qkv)

    if tuned:
        two_xy, x1 = lax.optimization_barrier((two_xy, x1))
        two = gather_blocks(near_two, two_x, two_y, two_xy)

    scales = (1.0 / normal_count, LABEL_WEIGHT / normal_count, LOGIT_WEIGHT / (normal_count * C))
    dx1, keep_two, send_two, vgrad, hgrad, loss = run_middle(
        tuned, images // 2, images, scales, *([] if tuned else [given]), *two, prm, hb, soft, meta, x1
    )

    def attend_back(first, *operands):
        begin, count = (0, 1) if first else (1, steps - 1)
        some = lambda width: pl.BlockSpec((n, ROWS_T, width), lambda i: (i + begin, 0, 0))
        return pl.pallas_call(
            functools.partial(attend_back_kernel, n, first),
            grid=(count,),
            in_specs=[out_part, whole((16, D)), some(3 * D), some(D), some(D)] + ([] if first else [whole((D, D)), ANY]),
            out_specs=[some(3 * D), whole((D, D)), whole((16, D))],
            out_shape=[sds((images, ROWS_T, 3 * D), bf16), sds((D, D), f32), sds((16, D), f32)],
            input_output_aliases={} if first else {6: 0},
            cost_estimate=cost(6 * count),
            compiler_params=params_of(22),
        )(*operands)

    dqkv, acc_out, vgrad = attend_back(True, attn, vgrad, qkv, att, dx1)
    if tuned:
        a_code, a_keep, b_code, b_keep = scatter_first(keep_two, to_core(send_two), SECTIONS_TWO)
        a_code, b_code, vgrad = lax.optimization_barrier((a_code, b_code, vgrad))
        moving = (to_x(a_code), to_y(b_code))
    dqkv, acc_out, vgrad = attend_back(False, attn, vgrad, qkv, att, dx1, acc_out, dqkv)
    if tuned:
        a_code, a_rest, b_code, b_rest = scatter_second(a_keep, b_keep, *moving, SECTIONS_TWO)
        a_code, b_code, vgrad, dqkv = lax.optimization_barrier((a_code, b_code, vgrad, dqkv))
        moving = (to_y(a_code), to_x(b_code))
    dx0, vgrad = pl.pallas_call(
        functools.partial(unit_back_kernel, n),
        grid=(steps,),
        in_specs=[whole((3 * D, D)), whole((16, D)), whole((16, D)), per(D), per(3 * D), per(D)],
        out_specs=[per(D), whole((16, D))],
        out_shape=[sds((images, ROWS_T, D), f32), sds((16, D), f32)],
        cost_estimate=cost(6),
        compiler_params=params_of(22),
    )(attn, prm, vgrad, x0, dqkv, dx1)
    if tuned:
        rest_two, code_two = scatter_third_pair(a_rest, b_rest, *moving, SECTIONS_TWO)
        code_two, dx0 = lax.optimization_barrier((code_two, dx0))
    acc_in = pl.pallas_call(
        functools.partial(qkv_back_kernel, n),
        grid=(steps,),
        in_specs=[whole((16, D)), per(D), per(3 * D)],
        out_specs=whole((3 * D, D)),
        out_shape=sds((3 * D, D), f32),
        cost_estimate=cost(6),
        compiler_params=params_of(22),
    )(prm, x0, dqkv)
    keep_one, send_one = pl.pallas_call(
        functools.partial(embed_back_kernel, tuned, vblock, images),
        in_specs=[VMEM] * 9,
        out_shape=[sds((16, R_ONE, D), f32), sds((16, R_ONE + R_CODE, D), jnp.int16)],
        scratch_shapes=[
            pltpu.VMEM((4 * D, D), f32),
            pltpu.VMEM((PD, D), f32),
            pltpu.VMEM((4 * PIX_ROWS, D), f32),
            pltpu.VMEM((V_ROWS, D), f32),
            pltpu.VMEM((BLOCKS, 8, D), f32),
        ],
        cost_estimate=cost(6),
        compiler_params=params_of(34),
    )(vgrad, hgrad, acc_in, acc_out, *got, dx0)

    if tuned:
        a_code, a_keep, b_code, b_keep = scatter_first(keep_one, to_core(send_one), SECTIONS_ONE)
        code_two, a_code, b_code = lax.optimization_barrier((code_two, a_code, b_code))
        moving = (to_x(a_code), to_y(b_code))
        own_two, code_two = scatter_near(rest_two, to_z(code_two, 1), SECTIONS_TWO)
        code_two, a_keep = lax.optimization_barrier((code_two, a_keep))
        a_code, a_rest, b_code, b_rest = scatter_second(a_keep, b_keep, *moving, SECTIONS_ONE)
        code_two, a_code, b_code = lax.optimization_barrier((code_two, a_code, b_code))
        moving = (to_y(a_code), to_x(b_code))
        share_two, sums = scatter_fourth(own_two, [to_z(code_two, 2)], SECTIONS_TWO, loss)
        own_one, *codes_one = scatter_third(a_rest, b_rest, *moving, SECTIONS_ONE)
        last_one = [to_z(code, k + 1) for k, code in enumerate(codes_one)]
        share_one, sums = scatter_fourth(own_one, last_one, SECTIONS_ONE, sums)
    else:
        shares = plain_scatter((keep_one, send_one), (keep_two, send_two), vblock)
        squares = sum(jnp.sum(share * share) for share in shares)
        sums = loss + jnp.where(lax.broadcasted_iota(i32, (8, 128), 1) == 0, squares, 0.0)
    sums = sum_all(sums, tuned)
    norm_value = jnp.sqrt(sums[0, 0])
    total_loss = sums[0, 1]
    clip_factor = jnp.minimum(1.0, CLIP_NORM / (norm_value + 1e-06))
    results = [total_loss, norm_value]
    if tuned:
        states = [views(v, j) for j in range(5) for v in (masters[j], moments[j], averages[j])]
        news = pl.pallas_call(
            update_kernel,
            out_shape=[sds(v.shape, f32) for v in states],
            in_specs=[SMEM] + [VMEM] * 17,
            compiler_params=params_of(24),
        )(clip_factor.reshape(1, 1), share_one, share_two, *states)
        for j in range(15):
            results.append(news[j].T[None] if j // 3 in (1, 3) else news[j][None] if j // 3 == 2 else news[j])
        vector_share = share_one[72:80].reshape(-1)[:vblock]
        results += list(advance(vector_weight, vector_moment, vector_average, vector_share, clip_factor))
    else:
        for weight, moment, average, share in zip(masters, moments, averages, shares):
            results += list(advance(weight, moment, average, share, clip_factor))
    return tuple(results)


def solution(mesh):
    split_rows, split_columns = P(("dp", "cls"), None), P(None, None, ("dp", "cls"))
    states = (
        [split_rows] * 3
        + [split_columns] * 3
        + [P(None, "dp", "cls")] * 3
        + [P(None, "cls", "dp")] * 3
        + [P("dp", "cls")] * 3
        + [P(("dp", "cls"))] * 3
    )
    in_specs = (
        P("dp", "cls", None),
        P("dp"),
        P("dp", "cls", None),
        P("dp", "cls"),
        P("dp"),
        P(),
        P(),
        P("dp", "cls"),
        *states,
    )
    out_specs = (P(), P(), *states)
    return jax.shard_map(on_device, mesh=mesh, in_specs=in_specs, out_specs=out_specs, check_vma=False)
```

```python
import functools
import math

import jax
import jax.numpy as jnp
from jax import lax
from jax.experimental import pallas as pl
from jax.experimental.pallas import tpu as pltpu
from jax.sharding import PartitionSpec as P

D = 384
HEADS = 6
HD = 64
FF = 1536
C = 1000
PD = 768
TOK = 197
PATCHES = 196
PARAMS = 2531176

NORM_EPS = 1e-06
SCORE_SCALE = 0.125
LOGIT_WEIGHT = 0.3
LABEL_WEIGHT = 0.8
MOMENTUM_DECAY = 0.9
AVERAGE_KEEP = 0.75
CLIP_NORM = 0.005
RATE = 0.03 * math.sqrt(PARAMS) / CLIP_NORM

ROWS_T = 208
GRID_DP, GRID_CLS = 8, 4
BLOCKS = GRID_DP * GRID_CLS
CPART = C // GRID_CLS
CPAD = 256
F_CHUNK = 512
R_ONE = 80
R_TWO = 128
R_MASK = 16
PIX_ROWS = 304
V_ROWS = 232
HEAD_AT = (TOK + 4) * D
LAYER_AT = HEAD_AT + C

bf16 = jnp.bfloat16
f32 = jnp.float32
i32 = jnp.int32

ANY = pl.BlockSpec(memory_space=pl.ANY)
VMEM = pl.BlockSpec(memory_space=pltpu.VMEM)
SMEM = pl.BlockSpec(memory_space=pltpu.SMEM)


def sds(shape, dtype):
    return jax.ShapeDtypeStruct(shape, dtype)


def cost(micros):
    return pl.CostEstimate(flops=int(micros * 1e8), bytes_accessed=1 << 20, transcendentals=0)


def params_of(limit_mib, **more):
    return pltpu.CompilerParams(vmem_limit_bytes=limit_mib << 20, **more)


def nn(a, b):
    return lax.dot_general(a, b, (((1,), (0,)), ((), ())), preferred_element_type=f32)


def nt(a, b):
    return lax.dot_general(a, b, (((1,), (1,)), ((), ())), preferred_element_type=f32)


def tn(a, b):
    return lax.dot_general(a, b, (((0,), (0,)), ((), ())), preferred_element_type=f32)


def gelu_parts(values):
    bell = jnp.exp(-0.5 * values * values)
    t = 1.0 / (1.0 + (0.3275911 * 0.5**0.5) * jnp.abs(values))
    tail = 0.5 * 1.061405429 * t - 0.5 * 1.453152027
    tail = tail * t + 0.5 * 1.421413741
    tail = tail * t - 0.5 * 0.284496736
    tail = (tail * t + 0.5 * 0.254829592) * t * bell
    return jnp.where(values < 0.0, tail, 1.0 - tail), bell * (1.0 / math.sqrt(2.0 * math.pi))


def normalize(values):
    centred = values - jnp.mean(values, axis=-1, keepdims=True)
    inverse = lax.rsqrt(jnp.mean(centred * centred, axis=-1, keepdims=True) + NORM_EPS)
    return (centred * inverse, inverse)


def normalize_back(unit, inverse, grad_unit):
    return inverse * (
        grad_unit
        - jnp.mean(grad_unit, axis=-1, keepdims=True)
        - unit * jnp.mean(grad_unit * unit, axis=-1, keepdims=True)
    )


def advance(weight, moment, average, grad, clip_factor):
    clipped = clip_factor * grad
    moment_new = MOMENTUM_DECAY * moment + clipped
    weight_new = weight - RATE * (clipped + MOMENTUM_DECAY * moment_new)
    average_new = AVERAGE_KEEP * average + (1.0 - AVERAGE_KEEP) * weight_new
    return (weight_new, moment_new, average_new)


def pack_head(block):
    a, b, c = block[..., :16, :], block[..., 16:32, :], block[..., 32:, :]
    top = jnp.concatenate([a, b[..., :128]], axis=-1)
    low = jnp.concatenate([b[..., 128:], c], axis=-1)
    return jnp.concatenate([top, low], axis=-2)


def unpack_head(block):
    top, low = block[..., :16, :], block[..., 16:, :]
    b = jnp.concatenate([top[..., 256:], low[..., :128]], axis=-1)
    return jnp.concatenate([top[..., :256], b, low[..., 128:]], axis=-2)


def me_of(tuned):
    if tuned:
        return lax.axis_index("dp") * GRID_CLS + lax.axis_index("cls")
    return 0


def grad_place(s):
    core, x, y, z = s & 1, (s >> 1) & 1, (s >> 2) & 1, s >> 3
    if z < 2:
        return core, (0 if x else 4) + 2 * y + z
    return core, (8 if y else 12) + 2 * x + (z - 2)


R_CODE = 16
SECTIONS_ONE = (0, 48, 72, 80)
SECTIONS_TWO = (0, 32, 80, 128)


def encode(block, sections, out):
    rows = sections[-1]
    powers = []
    for j, (a, b) in enumerate(zip(sections[:-1], sections[1:])):
        part = block[j] if isinstance(block, list) else block[a:b]
        most = jnp.max(jnp.abs(part), axis=0, keepdims=True)
        power = jnp.clip(jnp.ceil(jnp.log2(jnp.maximum(most, 1e-30))), -99.0, 126.0)
        code = jnp.round(part * jnp.exp2(15.0 - power))
        out[a:b, :] = jnp.clip(code, -32767.0, 32767.0).astype(i32).astype(jnp.int16)
        powers.append(power)
    powers.append(jnp.zeros((R_CODE - len(powers), D), f32))
    out[rows : rows + R_CODE, :] = jnp.concatenate(powers, axis=0).astype(i32).astype(jnp.int16)


def put_block(parts, sections, keep, send, core, place):
    if core:
        encode(parts, sections, send.at[place])
    else:
        for part, a, b in zip(parts, sections[:-1], sections[1:]):
            keep[place, a:b, :] = part


def decode(code, sections):
    rows = sections[-1]
    powers = code[rows : rows + R_CODE, :].astype(i32).astype(f32)
    return jnp.concatenate(
        [
            code[a:b, :].astype(i32).astype(f32) * jnp.exp2(powers[j : j + 1] - 15.0)
            for j, (a, b) in enumerate(zip(sections[:-1], sections[1:]))
        ],
        axis=0,
    )


def pack_mask(block):
    a, b, c = block[:8], block[8:16], block[16:]
    top = jnp.concatenate([a, b[:, :128]], axis=1)
    return jnp.concatenate([top, jnp.concatenate([b[:, 128:], c], axis=1)], axis=0)


def unpack_mask(block):
    top, low = block[:8], block[8:]
    b = jnp.concatenate([top[:, 256:], low[:, :128]], axis=1)
    return jnp.concatenate([top[:, :256], b, low[:, 128:]], axis=0)


def pack_weights_kernel(attn, patch, vec, up, down, head, seen, out):
    one, two = out.at[0:R_ONE], out.at[R_ONE:]
    one[0:48, :] = attn[...].astype(bf16)
    one[48:80, :] = jnp.concatenate([patch[...], vec[...]], axis=0).astype(bf16)
    block = jnp.concatenate([head[...], jnp.zeros((48, CPAD - CPART), f32)], axis=1)
    two[0:32, :] = pack_head(block).astype(bf16)
    two[32:80, :] = up[...].astype(bf16)
    two[80:128, :] = down[...].astype(bf16)
    mask = jnp.concatenate([seen[...].astype(f32), jnp.zeros((seen.shape[0], CPAD - CPART), f32)], axis=1)
    two[128:144, :] = pack_mask(mask).astype(bf16)


def pick_kernel(cur_own, rep_own, find, *refs):
    if find:
        owner, row, cur_labels, buf_labels, cur, buf, logits, o0, o1, far, meta, *scratch = refs
    else:
        row, cur, buf, logits, o0, o1, far, *scratch = refs
    stage, stage_cur, wide, wide_cur, soft, res, slots, sems = scratch
    parts, stored, _ = stage.shape
    kind = stage_cur.shape[1]
    chunk = 7
    copies = [pltpu.make_async_copy(cur, stage_cur, sems.at[parts // chunk])]
    for j in range(parts // chunk):
        part = pl.ds(j * chunk, chunk)
        copies.append(pltpu.make_async_copy(buf.at[part], stage.at[part], sems.at[j]))
    for copy in copies:
        copy.start()
    me = lax.axis_index("cls")
    if find:
        mine = lax.axis_index("dp")

        def look(i, count):
            hit = owner[i] == mine

            @pl.when(hit)
            def _():
                slots[count] = i

            return count + jnp.where(hit, 1, 0)

        lax.fori_loop(0, owner.shape[0], look, 0)
        for m in range(8):
            if m < cur_own:
                meta[0, m] = cur_labels[me * cur_own + m]
                meta[1, m] = 0
                meta[2, m] = mine * 3 * kind + me * cur_own + m
            elif m < cur_own + rep_own:
                i = slots[me * rep_own + m - cur_own]
                at = lax.rem(i, 2 * kind)
                meta[0, m] = jnp.where(at < kind, 0, buf_labels[row[i]])
                meta[1, m] = jnp.where(at < kind, 1, 2)
                meta[2, m] = lax.div(i, 2 * kind) * 3 * kind + kind + at
            else:
                meta[0, m] = 0
                meta[1, m] = 3
                meta[2, m] = 0
    else:
        for k in range(4 * rep_own):
            slots[k] = k
    soft[...] = jnp.zeros_like(soft)
    soft[:, :CPART] = logits[...].astype(f32)
    for j, copy in enumerate(copies):
        copy.wait()
        for lanes in range(PD // 128):
            at = slice(lanes * 128, (lanes + 1) * 128)
            if j == 0:
                wide_cur[lanes] = stage_cur[:, :, at].astype(f32).reshape(parts * kind, 128)
            else:
                one = stage[(j - 1) * chunk : j * chunk, :, at].astype(f32).reshape(chunk * stored, 128)
                wide[lanes, (j - 1) * chunk * stored : j * chunk * stored, :] = one
    images = cur_own + rep_own
    res[images * parts :, :] = jnp.zeros((PIX_ROWS - images * parts, PD), f32)
    for k, out in enumerate((o0, o1, far.at[0], far.at[1])):
        to = me ^ k
        for m in range(images):
            if m >= cur_own:
                r = row[slots[to * rep_own + m - cur_own]]
                at = (m % 3) * CPAD
                res[images * parts + m // 3 : images * parts + m // 3 + 1, at : at + CPAD] = soft[pl.ds(r, 1), :]
            for lanes in range(PD // 128):
                if m < cur_own:
                    one = wide_cur[lanes, pl.ds(to * cur_own + m, parts, stride=kind), :]
                else:
                    one = wide[lanes, pl.ds(r, parts, stride=stored), :]
                res[m * parts : (m + 1) * parts, lanes * 128 : (lanes + 1) * 128] = one
        out[...] = res[...].astype(bf16)


def spread_vector(vblock, blocks, flat):
    flat[...] = jnp.zeros_like(flat)
    lane = lax.broadcasted_iota(i32, (8, D), 1)
    for d in range(BLOCKS):
        q, s = divmod(vblock * d, D)
        b = blocks[d]
        if s:
            b = pltpu.roll(b, s, 1)
        flat[q : q + 8, :] = flat[q : q + 8, :] + jnp.where(lane >= s, b, 0.0)
        if s:
            flat[q + 1 : q + 9, :] = flat[q + 1 : q + 9, :] + jnp.where(lane < s, b, 0.0)


def cut_vector(vblock, flat, blocks):
    lane = lax.broadcasted_iota(i32, (8, D), 1)
    place = lax.broadcasted_iota(i32, (8, D), 0) * D + lane
    for d in range(BLOCKS):
        q, s = divmod(vblock * d, D)
        b = flat[q : q + 8, :]
        if s:
            a = pltpu.roll(b, D - s, 1)
            b = pltpu.roll(flat[q + 1 : q + 9, :], D - s, 1)
            b = jnp.where(lane < D - s, a, b)
        blocks[d] = jnp.where(place < vblock, b, 0.0)


def layer_vectors(flat):
    row, s = divmod(LAYER_AT, D)
    lane = lax.broadcasted_iota(i32, (12, D), 1)
    a = pltpu.roll(flat[row : row + 16, :], D - s, 1)
    return jnp.where(lane < D - s, a[0:12], a[1:13])


def head_vector(flat):
    rows = []
    wide = lax.broadcasted_iota(i32, (1, D), 1)
    for part in range(GRID_CLS):
        row, s = divmod(HEAD_AT + part * CPART, D)
        a = flat[row : row + 1, :]
        if s:
            a = pltpu.roll(jnp.broadcast_to(a, (8, D)), D - s, 1)[0:1]
            b = pltpu.roll(jnp.broadcast_to(flat[row + 1 : row + 2, :], (8, D)), D - s, 1)[0:1]
            a = jnp.where(wide < D - s, a, b)
        rows.append(jnp.where(wide < CPART, a, 0.0)[:, :CPAD])
    return jnp.concatenate(rows, axis=0)


def store_flat(flat, at, values, count):
    row, s = divmod(at, D)
    wide = lax.broadcasted_iota(i32, (1, D), 1)
    values = jnp.where(wide < count, values, 0.0)
    if s:
        values = pltpu.roll(jnp.broadcast_to(values, (8, D)), s, 1)[0:1]
        flat[row + 1 : row + 2, :] = flat[row + 1 : row + 2, :] + jnp.where(wide < s, values, 0.0)
    flat[row : row + 1, :] = flat[row : row + 1, :] + jnp.where(wide >= s, values, 0.0)


def head_masks():
    keys = lax.broadcasted_iota(i32, (1, ROWS_T, ROWS_T), 1) < TOK
    low = lax.broadcasted_iota(i32, (ROWS_T, 128), 1) < HD
    low_t = lax.broadcasted_iota(i32, (128, ROWS_T), 0) < HD
    return keys, low, low_t


def apart(two, low, axis):
    none = jnp.zeros_like(two)
    return jnp.concatenate([jnp.where(low, two, none), jnp.where(low, none, two)], axis=axis)


def pair_probs(q2, k2, keys, low):
    scores = nt(apart(k2, low, 0), q2).reshape(2, ROWS_T, ROWS_T) * SCORE_SCALE
    scores = jnp.where(keys, scores, -1e30)
    powers = jnp.exp(scores - jnp.max(scores, axis=1, keepdims=True))
    return powers * (1.0 / jnp.sum(powers, axis=1, keepdims=True))


def embed_kernel(tuned, vblock, n, images, *refs):
    (w0, w1, w2, w3, w4, w5, w6, w7, p0, p1, p2, p3, x0_out, qkv_out, attn, prm, hb, soft,
     patch_wide, patch, blocks, flat, table, rows, x0_all) = refs
    weights = (w0, w1, w2, w3, w4, w5, w6, w7)
    p2 = p2.at[0]
    me = me_of(tuned)
    part = lax.axis_index("cls")
    per = PATCHES // 4

    @pl.when(pl.program_id(0) == 0)
    def _():
        for s in range(BLOCKS):
            d = s ^ me
            w = weights[s & 7]
            attn[pl.ds(pl.multiple_of(d * 48, 16), 48), :] = w[s >> 3, 0:48, :]
            rest = w[s >> 3, 48:80, :].astype(f32)
            patch_wide[pl.ds(pl.multiple_of(d * 24, 8), 24), :] = rest[0:24]
            blocks[d] = rest[24:32]
        patch[...] = patch_wide[...].astype(bf16)
        spread_vector(vblock, blocks, flat)
        prm[0:12, :] = layer_vectors(flat)
        prm[12:13, :] = flat[TOK + 1 : TOK + 2, :]
        prm[13:14, :] = flat[TOK + 2 : TOK + 3, :]
        prm[14:16, :] = jnp.zeros((2, D), f32)
        hb[0:4, :] = head_vector(flat)
        hb[4:8, :] = jnp.zeros((4, CPAD), f32)
        bias = flat[TOK : TOK + 1, :]
        table[...] = jnp.zeros_like(table)
        for k in range(4):
            for q in range(4):

                @pl.when((part ^ k) == q)
                def _(k=k, q=q):
                    table[k * per : k * per + per, :] = flat[1 + q * per : 1 + q * per + per, :] + bias

        table[PATCHES : PATCHES + 1, :] = flat[0:1, :] + flat[TOK + 3 : TOK + 4, :]
        soft[...] = jnp.zeros_like(soft)
        for k, piece in enumerate((p0, p1, p2, p3)):
            rows[k * PIX_ROWS : (k + 1) * PIX_ROWS, :] = nn(piece[...], patch[...])
            stored = piece[PIX_ROWS - 16 :, :].astype(f32)
            at = images * per - (PIX_ROWS - 16)
            for m in range(images):
                soft[part ^ k, m : m + 1, :] = stored[at + m // 3 : at + m // 3 + 1, (m % 3) * CPAD : (m % 3 + 1) * CPAD]
        for m in range(images):
            x0_all[m] = table[...]
            for k in range(4):
                at = slice(k * per, k * per + per)
                begin = k * PIX_ROWS + m * per
                x0_all[m, at, :] = x0_all[m, at, :] + rows[begin : begin + per, :]

    tokens = n * ROWS_T
    x0 = x0_all[pl.ds(pl.program_id(0) * n, n)]
    x0_out[...] = x0
    unit, _ = normalize(x0)
    normed = (unit * prm[0:1, :] + prm[1:2, :]).astype(bf16).reshape(tokens, D)
    for j, bias in ((0, prm[2:3, :]), (1, None), (2, prm[3:4, :])):
        one = nt(normed, attn[j * D : (j + 1) * D, :])
        if bias is not None:
            one = one + bias
        qkv_out[:, :, j * D : (j + 1) * D] = one.astype(bf16).reshape(n, ROWS_T, D)


def attend_kernel(n, w_out, prm, x0, qkv, att_out, x1_out):
    tokens = n * ROWS_T
    keys, low, low_t = head_masks()
    for i in range(n):
        for p in range(HEADS // 2):
            at = p * 128
            q2 = qkv[i, :, at : at + 128]
            v2t = qkv[i, :, 2 * D + at : 2 * D + at + 128].T
            probs = pair_probs(q2, qkv[i, :, D + at : D + at + 128], keys, low).astype(bf16)
            both = nn(apart(v2t, low_t, 1), probs.reshape(2 * ROWS_T, ROWS_T))
            att_out[i, :, at : at + 128] = both.T.astype(bf16)
    branch = nt(att_out[...].reshape(tokens, D), w_out[...]) + prm[4:5, :]
    x1_out[...] = x0[...] + branch.reshape(n, ROWS_T, D)


def middle_kernel(tuned, n, images, scales, *refs):
    if not tuned:
        given, *refs = refs
    (w0, w1, w2, w3, w4, w5, w6, w7, prm, hb, soft, meta, x1_in,
     dx1_out, keep, send, vgrad, hgrad, loss,
     w_up, w_down, w_head, act, slope, mask, masks_all, pooled, dpooled, glow, acc_up, acc_down,
     normed_all, dy_all, dup_all, up_bias, up_sum) = refs
    weights = (w0, w1, w2, w3, w4, w5, w6, w7)
    me = me_of(tuned)
    step = pl.program_id(0)
    last = pl.num_programs(0) - 1

    @pl.when(step == 0)
    def _():
        for s in range(BLOCKS):
            d = s ^ me
            dp, cl = d >> 2, d & 3
            w = weights[s & 7]
            rows = pl.ds(pl.multiple_of(dp * 48, 16), 48)
            w_head[cl, rows, :] = unpack_head(w[s >> 3, 0:32, :])
            columns = pl.ds(pl.multiple_of(cl * D, 128), D)
            w_up[rows, columns] = w[s >> 3, 32:80, :]
            w_down[rows, columns] = w[s >> 3, 80:128, :]
            if tuned:
                seen = unpack_mask(w[s >> 3, 128:144, :].astype(f32))
                masks_all[cl, pl.ds(pl.multiple_of(dp * 24, 8), 24), :] = seen
        if tuned:
            mask[...] = jnp.zeros_like(mask)
            for m in range(images):
                for q in range(4):
                    mask[q, m : m + 1, :] = masks_all[q, pl.ds(meta[2, m], 1), :]
        else:
            mask[...] = given[...]
        for c in range(4):
            up_bias[:, c * D : (c + 1) * D] = prm[8 + c : 9 + c, :]
        up_sum[...] = jnp.zeros_like(up_sum)
        vgrad[...] = jnp.zeros_like(vgrad)
        pooled[...] = jnp.zeros_like(pooled)

    tokens = n * ROWS_T
    x1 = x1_in[...].reshape(tokens, D)
    unit_two, inverse_two = normalize(x1)
    normed = (unit_two * prm[5:6, :] + prm[6:7, :]).astype(bf16)
    total = jnp.zeros((tokens, D), f32)
    mine = pl.ds(pl.multiple_of(step * tokens, 16), tokens)
    normed_all[mine, :] = normed
    chunks = [slice(c, c + F_CHUNK) for c in range(0, FF, F_CHUNK)]
    for c in chunks:
        pre = nn(normed, w_up[:, c]) + up_bias[:, c]
        half, bell = gelu_parts(pre)
        hot = (pre * half).astype(bf16)
        act[mine, c] = hot
        slope[:, c] = half + pre * bell
        total = total + nt(hot, w_down[:, c])
    x2 = x1 + (total + prm[7:8, :])
    unit, inverse = normalize(x2)
    real = lax.broadcasted_iota(i32, (ROWS_T, D), 0) < TOK
    sums = []
    for i in range(n):
        u = unit[i * ROWS_T : (i + 1) * ROWS_T]
        sums.append(jnp.sum(jnp.where(real, u, 0.0), axis=0, keepdims=True))
        pooled[pl.ds(step * n + i, 1), :] = sums[i] * (1.0 / TOK) * prm[12:13, :] + prm[13:14, :]

    low = pooled[...].astype(bf16)
    rows8 = (16, CPAD)
    row_id = lax.broadcasted_iota(i32, rows8, 0)
    lane = lax.broadcasted_iota(i32, rows8, 1)
    label = jnp.full(rows8, -1, i32)
    weight = jnp.zeros(rows8, f32)
    squared = jnp.zeros(rows8, f32)
    for i in range(images):
        kind = meta[1, i]
        label = jnp.where(row_id == i, meta[0, i], label)
        weight = jnp.where(row_id == i, jnp.where(kind == 0, scales[0], jnp.where(kind == 2, scales[1], 0.0)), weight)
        squared = jnp.where(row_id == i, jnp.where(kind == 1, 1.0, 0.0), squared)
    inside = lane < CPART
    logits, hots, lives, masks, tops = [], [], [], [], []
    pad = jnp.zeros((8, CPAD), f32)
    for q in range(4):
        one = nn(low, w_head[q]) + hb[q : q + 1, :]
        hot = (lane + q * CPART == label) & inside
        seen = (jnp.concatenate([mask[q], pad], axis=0) > 0.5) & inside
        logits.append(one)
        hots.append(hot)
        masks.append(seen)
        lives.append(seen | hot)
        tops.append(jnp.max(jnp.where(inside, one, -3e38), axis=1, keepdims=True))
    top = jnp.maximum(jnp.maximum(tops[0], tops[1]), jnp.maximum(tops[2], tops[3]))
    alive = sum(
        jnp.sum(jnp.where(lives[q], jnp.exp(logits[q] - top), 0.0), axis=1, keepdims=True) for q in range(4)
    )
    norm = top + jnp.log(alive)
    target = sum(jnp.sum(jnp.where(hots[q], logits[q], 0.0), axis=1, keepdims=True) for q in range(4))
    cross = norm - target
    value = jnp.sum(jnp.where(weight[:, 0:1] > 0, weight[:, 0:1] * cross, 0.0))
    back = jnp.zeros((16, D), f32)
    for q in range(4):
        gap = jnp.where(masks[q], logits[q] - jnp.concatenate([soft[q], pad], axis=0), 0.0)
        value = value + scales[2] * jnp.sum(squared * gap * gap)
        share = jnp.where(lives[q], jnp.exp(logits[q] - norm), 0.0)
        grad = weight * (share - jnp.where(hots[q], 1.0, 0.0)) + squared * (2.0 * scales[2]) * gap
        g = grad.astype(bf16)
        glow[q] = g
        back = back + nt(g, w_head[q])
    dpooled[...] = back

    pieces = []
    for i in range(n):
        grad = dpooled[pl.ds(step * n + i, 1), :]
        vgrad[12:13, :] = vgrad[12:13, :] + grad * (1.0 / TOK) * sums[i]
        vgrad[13:14, :] = vgrad[13:14, :] + grad
        dz = grad * (1.0 / TOK) * prm[12:13, :]
        u = unit[i * ROWS_T : (i + 1) * ROWS_T]
        d = inverse[i * ROWS_T : (i + 1) * ROWS_T] * (
            dz - jnp.mean(dz, axis=-1, keepdims=True) - u * jnp.mean(dz * u, axis=-1, keepdims=True)
        )
        pieces.append(jnp.where(real, d, 0.0))
    dx2 = jnp.concatenate(pieces, axis=0)
    dy = dx2.astype(bf16)
    vgrad[7:8, :] = vgrad[7:8, :] + jnp.sum(dy.astype(f32), axis=0, keepdims=True)
    dy_all[mine, :] = dy
    dnormed = jnp.zeros((tokens, D), f32)
    for c in chunks:
        dup = (nn(dy, w_down[:, c]) * slope[:, c]).astype(bf16)
        up_sum[:, c] = up_sum[:, c] + jnp.sum(dup.astype(f32), axis=0, keepdims=True)
        dup_all[mine, c] = dup
        dnormed = dnormed + nt(dup, w_up[:, c])
    vgrad[5:6, :] = vgrad[5:6, :] + jnp.sum(dnormed * unit_two, axis=0, keepdims=True)
    vgrad[6:7, :] = vgrad[6:7, :] + jnp.sum(dnormed, axis=0, keepdims=True)
    dx1 = dx2 + normalize_back(unit_two, inverse_two, dnormed * prm[5:6, :])
    dx1_out[...] = dx1.reshape(n, ROWS_T, D)

    @pl.when(step == last)
    def _():
        loss[...] = jnp.where(lax.broadcasted_iota(i32, loss.shape, 1) == 0, 0.0, value)
        hgrad[...] = jnp.zeros_like(hgrad)
        for q in range(4):
            hgrad[q : q + 1, :] = jnp.sum(glow[q].astype(f32), axis=0, keepdims=True)
        for c in range(4):
            vgrad[8 + c : 9 + c, :] = up_sum[:, c * D : (c + 1) * D]
        for q in range(4):
            slope[0:D, q * CPAD : (q + 1) * CPAD] = tn(low, glow[q])
        for c in chunks:
            acc_down[:, c] = tn(dy_all[...], act[:, c])
            acc_up[:, c] = tn(normed_all[...], dup_all[:, c])
        for s in range(BLOCKS):
            d = s ^ me
            dp, cl = d >> 2, d & 3
            core, place = grad_place(s)
            rows = pl.ds(pl.multiple_of(dp * 48, 8), 48)
            columns = pl.ds(pl.multiple_of(cl * D, 128), D)
            head = slope[rows, pl.ds(pl.multiple_of(cl * CPAD, 128), CPAD)]
            block = [pack_head(head), acc_up[rows, columns], acc_down[rows, columns]]
            put_block(block, SECTIONS_TWO, keep, send, core, place)


def run_middle(tuned, n, images, scales, *operands):
    steps = images // n
    whole = lambda shape: pl.BlockSpec(shape, lambda i: (0,) * len(shape))
    per = lambda width: pl.BlockSpec((n, ROWS_T, width), lambda i: (i, 0, 0))
    return pl.pallas_call(
        functools.partial(middle_kernel, tuned, n, images, scales),
        grid=(steps,),
        in_specs=[whole((4, 8, CPAD))] * (0 if tuned else 1)
        + [whole((4, R_TWO + R_MASK, D))] * 8
        + [whole((16, D)), whole((8, CPAD)), whole((4, 8, CPAD))]
        + [SMEM, per(D)],
        out_specs=[
            per(D),
            whole((16, R_TWO, D)),
            whole((16, R_TWO + R_CODE, D)),
            whole((16, D)),
            whole((8, CPAD)),
            whole((8, 128)),
        ],
        out_shape=[
            sds((images, ROWS_T, D), f32),
            sds((16, R_TWO, D), f32),
            sds((16, R_TWO + R_CODE, D), jnp.int16),
            sds((16, D), f32),
            sds((8, CPAD), f32),
            sds((8, 128), f32),
        ],
        scratch_shapes=[
            pltpu.VMEM((D, FF), bf16),
            pltpu.VMEM((D, FF), bf16),
            pltpu.VMEM((4, D, CPAD), bf16),
            pltpu.VMEM((images * ROWS_T, FF), bf16),
            pltpu.VMEM((n * ROWS_T, FF), f32),
            pltpu.VMEM((4, 8, CPAD), f32),
            pltpu.VMEM((4, GRID_DP * 24, CPAD), f32),
            pltpu.VMEM((16, D), f32),
            pltpu.VMEM((16, D), f32),
            pltpu.VMEM((4, 16, CPAD), bf16),
            pltpu.VMEM((D, FF), f32),
            pltpu.VMEM((D, FF), f32),
            pltpu.VMEM((images * ROWS_T, D), bf16),
            pltpu.VMEM((images * ROWS_T, D), bf16),
            pltpu.VMEM((images * ROWS_T, FF), bf16),
            pltpu.VMEM((1, FF), f32),
            pltpu.VMEM((1, FF), f32),
        ],
        cost_estimate=cost(30),
        compiler_params=params_of(36),
    )(*operands)


def attend_back_kernel(n, first, *refs):
    if first:
        (w_out, vgrad_in, qkv, att, dx1_in, dqkv, acc, vgrad) = refs
    else:
        (w_out, vgrad_in, qkv, att, dx1_in, acc_in, _, dqkv, acc, vgrad) = refs

    @pl.when(pl.program_id(0) == 0)
    def _():
        acc[...] = jnp.zeros_like(acc) if first else acc_in[...]
        vgrad[...] = vgrad_in[...]

    tokens = n * ROWS_T
    dout = dx1_in[...].reshape(tokens, D).astype(bf16)
    vgrad[4:5, :] = vgrad[4:5, :] + jnp.sum(dout.astype(f32), axis=0, keepdims=True)
    acc[...] = acc[...] + tn(dout, att[...].reshape(tokens, D))
    datt = nn(dout, w_out[...]).astype(bf16)
    keys, low, low_t = head_masks()
    both = (2 * ROWS_T, ROWS_T)
    for i in range(n):
        rows = slice(i * ROWS_T, (i + 1) * ROWS_T)
        for p in range(HEADS // 2):
            at = p * 128
            q2 = qkv[i, :, at : at + 128]
            k2 = qkv[i, :, D + at : D + at + 128]
            v2 = qkv[i, :, 2 * D + at : 2 * D + at + 128]
            do = datt[rows, at : at + 128]
            probs = pair_probs(q2, k2, keys, low)
            dprobs = nt(apart(v2, low, 0), do).reshape(probs.shape)
            mean = jnp.sum(probs * dprobs, axis=1, keepdims=True)
            dscores = (probs * (dprobs - mean)).astype(bf16).reshape(both)
            dq = nn(apart(k2.T, low_t, 1), dscores)
            dk = nn(dscores, q2)
            dv = nn(probs.astype(bf16).reshape(both), do)
            dqkv[i, :, at : at + 128] = (dq * SCORE_SCALE).T.astype(bf16)
            dk = jnp.where(low, dk[:ROWS_T], dk[ROWS_T:]) * SCORE_SCALE
            dqkv[i, :, D + at : D + at + 128] = dk.astype(bf16)
            dv = jnp.where(low, dv[:ROWS_T], dv[ROWS_T:])
            dqkv[i, :, 2 * D + at : 2 * D + at + 128] = dv.astype(bf16)


def unit_back_kernel(n, vblock, images, *refs):
    (w_in, prm, vgrad_in, hgrad, p0, p1, p2, p3, x0, dqkv_in, dx1_in,
     acc_patch, blocks, vgrad, dx0_all, rows, flat) = refs
    p2 = p2.at[0]
    part = lax.axis_index("cls")
    per = PATCHES // 4

    @pl.when(pl.program_id(0) == 0)
    def _():
        vgrad[...] = vgrad_in[...]

    tokens = n * ROWS_T
    dx1 = dx1_in[...].reshape(tokens, D)
    dqkv = dqkv_in[...].reshape(tokens, 3 * D)
    vgrad[2:3, :] = vgrad[2:3, :] + jnp.sum(dqkv[:, 0:D].astype(f32), axis=0, keepdims=True)
    vgrad[3:4, :] = vgrad[3:4, :] + jnp.sum(dqkv[:, 2 * D : 3 * D].astype(f32), axis=0, keepdims=True)
    unit, inverse = normalize(x0[...].reshape(tokens, D))
    dnormed = nn(dqkv, w_in[...])
    vgrad[0:1, :] = vgrad[0:1, :] + jnp.sum(dnormed * unit, axis=0, keepdims=True)
    vgrad[1:2, :] = vgrad[1:2, :] + jnp.sum(dnormed, axis=0, keepdims=True)
    dx0 = dx1 + normalize_back(unit, inverse, dnormed * prm[0:1, :])
    dx0_all[pl.ds(pl.program_id(0) * n, n)] = dx0.reshape(n, ROWS_T, D)

    @pl.when(pl.program_id(0) == pl.num_programs(0) - 1)
    def _():
        rows[...] = jnp.zeros_like(rows)
        for m in range(images):
            for k in range(4):
                begin = k * PIX_ROWS + m * per
                rows[begin : begin + per, :] = dx0_all[m, k * per : k * per + per, :]
        low = rows[...].astype(bf16)
        total = tn(p0[...], low[:PIX_ROWS])
        for k, piece in ((1, p1), (2, p2), (3, p3)):
            total = total + tn(piece[...], low[k * PIX_ROWS : (k + 1) * PIX_ROWS])
        acc_patch[...] = total
        position = dx0_all[0]
        for m in range(1, images):
            position = position + dx0_all[m]
        flat[...] = jnp.zeros_like(flat)
        for k in range(4):
            for q in range(4):

                @pl.when((part ^ k) == q)
                def _(k=k, q=q):
                    flat[1 + q * per : 1 + q * per + per, :] = position[k * per : k * per + per, :]

        first = position[PATCHES : PATCHES + 1, :]
        flat[0:1, :] = first
        flat[TOK : TOK + 1, :] = jnp.sum(position[0:PATCHES, :], axis=0, keepdims=True)
        flat[TOK + 1 : TOK + 2, :] = vgrad[12:13, :]
        flat[TOK + 2 : TOK + 3, :] = vgrad[13:14, :]
        flat[TOK + 3 : TOK + 4, :] = first
        for q in range(GRID_CLS):
            wide = jnp.concatenate([hgrad[q : q + 1, :], jnp.zeros((1, D - CPAD), f32)], axis=1)
            store_flat(flat, HEAD_AT + q * CPART, wide, CPART)
        for j in range(12):
            store_flat(flat, LAYER_AT + j * D, vgrad[j : j + 1, :], D)
        cut_vector(vblock, flat, blocks)


def qkv_back_kernel(n, prm, x0, dqkv_in, acc_out, acc):
    @pl.when(pl.program_id(0) == 0)
    def _():
        acc[0 : 3 * D, :] = jnp.zeros((3 * D, D), f32)
        acc[3 * D : 4 * D, :] = acc_out[...]

    tokens = n * ROWS_T
    dqkv = dqkv_in[...].reshape(tokens, 3 * D)
    unit, _ = normalize(x0[...].reshape(tokens, D))
    normed = (unit * prm[0:1, :] + prm[1:2, :]).astype(bf16)
    for j in range(3):
        at = slice(j * D, (j + 1) * D)
        acc[at, :] = acc[at, :] + tn(dqkv[:, at], normed)


def block_back_kernel(tuned, acc, acc_patch, blocks, keep, send):
    me = me_of(tuned)
    for s in range(BLOCKS):
        d = s ^ me
        core, place = grad_place(s)
        rows48, rows24 = pl.ds(pl.multiple_of(d * 48, 8), 48), pl.ds(pl.multiple_of(d * 24, 8), 24)
        put_block([acc[rows48, :], acc_patch[rows24, :], blocks[d]], SECTIONS_ONE, keep, send, core, place)


def update_kernel(v0, v1, v2, v3, one, two, vec, *refs):
    ins, (sums_out, *outs) = refs[:18], refs[18:]
    sums = (v0[...] + v1[...]) + (v2[...] + v3[...])
    norm = jnp.sqrt(sums[0, 0])
    sums_out[0] = sums[0, 1]
    sums_out[1] = norm
    clip = jnp.minimum(1.0, CLIP_NORM / (norm + 1e-06))
    grads = [
        one[48:72, :],
        one[0:48, :],
        two[32:80, :],
        two[80:128, :],
        unpack_head(two[0:32, :])[:, :CPART],
        vec[...],
    ]
    for j, grad in enumerate(grads):
        news = advance(ins[3 * j][...], ins[3 * j + 1][...], ins[3 * j + 2][...], grad, clip)
        for k in range(3):
            outs[3 * j + k][...] = news[k]


def flip(n, k):
    return [(i, i ^ k) for i in range(n)]


def to_core(v):
    return lax.ppermute(v, "cls", flip(4, 1))


def to_x(v):
    return lax.ppermute(v, "cls", flip(4, 2))


def to_y(v):
    return lax.ppermute(v, "dp", flip(8, 1))


def to_z(v, k):
    return lax.ppermute(v, "dp", flip(8, 2 * k))


def gather_blocks(near, at_x, at_y, at_xy):
    return [near, to_core(near), at_x, to_core(at_x), at_y, to_core(at_y), at_xy, to_core(at_xy)]


def first_kernel(sections, keep, got, send_a, keep_a, send_b, keep_b):
    encode(keep[0, 0] + decode(got.at[0, 0], sections), sections, send_a.at[0])
    keep_a[0] = keep[1, 0] + decode(got.at[1, 0], sections)
    encode(keep[2, 0] + decode(got.at[2, 0], sections), sections, send_b.at[0])
    keep_b[0] = keep[3, 0] + decode(got.at[3, 0], sections)


def second_kernel(sections, keep_a, keep_b, got_a, got_b, send_a, rest_a, send_b, rest_b):
    for keep, got, send, rest in ((keep_a, got_a, send_a, rest_a), (keep_b, got_b, send_b, rest_b)):
        rest[0] = keep[0, 0] + decode(got.at[0, 0], sections)
        encode(keep[1, 0] + decode(got.at[1, 0], sections), sections, send.at[0])


def third_kernel(sections, keep_a, keep_b, got_a, got_b, own, send_1, send_2, send_3):
    own[...] = keep_a[0] + decode(got_a.at[0], sections)
    encode(keep_a[1] + decode(got_a.at[1], sections), sections, send_1)
    encode(keep_b[0] + decode(got_b.at[0], sections), sections, send_2)
    encode(keep_b[1] + decode(got_b.at[1], sections), sections, send_3)


def third_pair_kernel(sections, keep_a, keep_b, got_a, got_b, rest, send):
    for j, (keep, got) in enumerate(((keep_a, got_a), (keep_b, got_b))):
        rest[j] = keep[0] + decode(got.at[0], sections)
        encode(keep[1] + decode(got.at[1], sections), sections, send.at[j])


def near_kernel(sections, rest, got, own, send):
    own[...] = rest[0] + decode(got.at[0], sections)
    encode(rest[1] + decode(got.at[1], sections), sections, send)


def fourth_kernel(sections, own, *refs):
    *got, before, share, sums = refs
    total = own[...]
    for code in got:
        total = total + decode(code, sections)
    share[...] = total
    lane = lax.broadcasted_iota(i32, (8, 128), 1)
    sums[...] = before[...] + jnp.where(lane == 0, jnp.sum(total * total), 0.0)


def scatter_first(keep, got, sections):
    rows = sections[-1]
    quarters = [pl.BlockSpec((4, 1, r, D), lambda j: (0, j, 0, 0)) for r in (rows, rows + R_CODE)]
    wide, code = pl.BlockSpec((1, rows, D), lambda j: (j, 0, 0)), pl.BlockSpec((1, rows + R_CODE, D), lambda j: (j, 0, 0))
    return pl.pallas_call(
        functools.partial(first_kernel, sections),
        grid=(4,),
        in_specs=quarters,
        out_specs=[code, wide, code, wide],
        out_shape=[sds((4, rows + R_CODE, D), jnp.int16), sds((4, rows, D), f32)] * 2,
        cost_estimate=cost(4),
        compiler_params=params_of(16),
    )(*[v.reshape((4, 4) + v.shape[1:]) for v in (keep, got)])


def scatter_second(keep_a, keep_b, got_a, got_b, sections):
    rows = sections[-1]
    pairs, codes = [pl.BlockSpec((2, 1, r, D), lambda j: (0, j, 0, 0)) for r in (rows, rows + R_CODE)]
    wide, code = [pl.BlockSpec((1, r, D), lambda j: (j, 0, 0)) for r in (rows, rows + R_CODE)]
    return pl.pallas_call(
        functools.partial(second_kernel, sections),
        grid=(2,),
        in_specs=[pairs] * 2 + [codes] * 2,
        out_specs=[code, wide, code, wide],
        out_shape=[sds((2, rows + R_CODE, D), jnp.int16), sds((2, rows, D), f32)] * 2,
        cost_estimate=cost(2),
        compiler_params=params_of(16),
    )(*[v.reshape((2, 2) + v.shape[1:]) for v in (keep_a, keep_b, got_a, got_b)])


def scatter_third(keep_a, keep_b, got_a, got_b, sections):
    rows = sections[-1]
    return pl.pallas_call(
        functools.partial(third_kernel, sections),
        out_shape=[sds((rows, D), f32)] + [sds((rows + R_CODE, D), jnp.int16)] * 3,
        cost_estimate=cost(2),
        compiler_params=params_of(16),
    )(keep_a, keep_b, got_a, got_b)


def scatter_third_pair(keep_a, keep_b, got_a, got_b, sections):
    rows = sections[-1]
    return pl.pallas_call(
        functools.partial(third_pair_kernel, sections),
        out_shape=[sds((2, rows, D), f32), sds((2, rows + R_CODE, D), jnp.int16)],
        compiler_params=params_of(16),
    )(keep_a, keep_b, got_a, got_b)


def scatter_near(rest, got, sections):
    rows = sections[-1]
    return pl.pallas_call(
        functools.partial(near_kernel, sections),
        out_shape=[sds((rows, D), f32), sds((rows + R_CODE, D), jnp.int16)],
        compiler_params=params_of(16),
    )(rest, got)


def scatter_fourth(own, got, sections, before):
    return pl.pallas_call(
        functools.partial(fourth_kernel, sections),
        out_shape=[sds(own.shape, f32), sds((8, 128), f32)],
        cost_estimate=cost(2),
        compiler_params=params_of(16),
    )(own, *got, before)


def sums_along_z(v):
    v = v + to_core(v)
    v = (v + to_x(v)) + (to_y(v) + lax.ppermute(v, ("dp", "cls"), flip(BLOCKS, GRID_CLS + 2)))
    return [v] + [to_z(v, k) for k in (1, 2, 3)]


def plain_gather(masters, vblock):
    patch, attention, up, down, head, vector = [w.astype(bf16) for w in masters]
    both = ("dp", "cls")
    patch = lax.all_gather(patch, both, axis=0, tiled=True).reshape(BLOCKS, 24, D)
    attention = lax.all_gather(attention, both, axis=2, tiled=True)[0].T.reshape(BLOCKS, 48, D)
    vector = lax.all_gather(vector, both, axis=0, tiled=True).reshape(BLOCKS, vblock)
    vector = jnp.pad(vector, ((0, 0), (0, 8 * D - vblock))).reshape(BLOCKS, 8, D)
    up = lax.all_gather(lax.all_gather(up, "dp", axis=1, tiled=True), "cls", axis=2, tiled=True)[0]
    down = lax.all_gather(lax.all_gather(down, "dp", axis=2, tiled=True), "cls", axis=1, tiled=True)[0].T
    head = lax.all_gather(lax.all_gather(head, "dp", axis=0, tiled=True), "cls", axis=1, tiled=True)
    up, down = [
        w.reshape(GRID_DP, 48, GRID_CLS, D).transpose(0, 2, 1, 3).reshape(BLOCKS, 48, D) for w in (up, down)
    ]
    head = head.reshape(GRID_DP, 48, GRID_CLS, CPART).transpose(0, 2, 1, 3).reshape(BLOCKS, 48, CPART)
    head = pack_head(jnp.pad(head, ((0, 0), (0, 0), (0, CPAD - CPART))))
    one = jnp.concatenate([attention, patch, vector], axis=1).reshape(4, 8, R_ONE, D)
    two = jnp.concatenate([head, up, down], axis=1).reshape(4, 8, R_TWO, D)
    return [one[:, a] for a in range(8)], [two[:, a] for a in range(8)]


def plain_scatter(one, two, vblock):
    def in_order(keep, send, sections):
        send = [decode(send[j], sections) for j in range(16)]
        return jnp.stack([(keep, send)[grad_place(s)[0]][grad_place(s)[1]] for s in range(BLOCKS)])

    one, two = in_order(*one, SECTIONS_ONE), in_order(*two, SECTIONS_TWO)
    both = ("dp", "cls")
    attention = one[:, 0:48].reshape(4 * D, D).T[None]
    patch = one[:, 48:72].reshape(PD, D)
    vector = one[:, 72:80].reshape(BLOCKS, 8 * D)[:, :vblock].reshape(-1)
    up, down = [
        w.reshape(GRID_DP, GRID_CLS, 48, D).transpose(0, 2, 1, 3).reshape(D, FF)
        for w in (two[:, 32:80], two[:, 80:128])
    ]
    head = unpack_head(two[:, 0:32])[:, :, :CPART]
    head = head.reshape(GRID_DP, GRID_CLS, 48, CPART).transpose(0, 2, 1, 3).reshape(D, C)

    def split(v, at_dp, at_cls):
        v = lax.psum_scatter(v, "dp", scatter_dimension=at_dp, tiled=True)
        return lax.psum_scatter(v, "cls", scatter_dimension=at_cls, tiled=True)

    return (
        lax.psum_scatter(patch, both, scatter_dimension=0, tiled=True),
        lax.psum_scatter(attention, both, scatter_dimension=2, tiled=True),
        split(up, 0, 1)[None],
        split(down.T, 1, 0)[None],
        split(head, 0, 1),
        lax.psum_scatter(vector, both, scatter_dimension=0, tiled=True),
    )


def take_rows_kernel(rows, source, out, sem):
    def one(i, carry):
        copy = pltpu.make_async_copy(source.at[rows[i]], out.at[i], sem)
        copy.start()
        copy.wait()
        return carry

    lax.fori_loop(0, out.shape[0], one, 0)


def take_rows(source, rows):
    return pl.pallas_call(
        take_rows_kernel,
        out_shape=sds((rows.shape[0],) + source.shape[1:], source.dtype),
        in_specs=[SMEM, ANY],
        out_specs=ANY,
        scratch_shapes=[pltpu.SemaphoreType.DMA(())],
    )(rows, source)


def pick_small(source, rows):
    hot = (rows[:, None] == jnp.arange(source.shape[0])[None, :]).astype(f32)
    return jnp.dot(hot, source.astype(f32), precision=lax.Precision.HIGHEST)


def plain_replay(buffer_patches, buffer_logits, buffer_labels, replay_owner, replay_row, kind_rows):
    dp_count, dp_index = lax.axis_size("dp"), lax.axis_index("dp")
    replay_count = 2 * kind_rows
    capacity = max(2, -(-replay_count // dp_count))
    table = lax.all_gather(buffer_labels, "dp", axis=0, tiled=True)
    owners = replay_owner[:, 0].reshape(dp_count, replay_count)
    local_rows = replay_row.reshape(dp_count, replay_count)
    earlier = jnp.arange(replay_count)[None, :] < jnp.arange(replay_count)[:, None]
    same_owner = owners[:, :, None] == owners[:, None, :]
    ranks = jnp.sum(jnp.where(same_owner & earlier[None], 1, 0), axis=2).astype(i32)
    slot_ids = jnp.arange(capacity, dtype=i32)
    wanted = (owners == dp_index)[:, :, None] & (ranks[:, :, None] == slot_ids[None, None, :])
    slot_rows = jnp.sum(jnp.where(wanted, local_rows[:, :, None], 0), axis=1).reshape(-1)
    pixels = take_rows(buffer_patches, slot_rows)
    logits = pick_small(buffer_logits, slot_rows).astype(bf16)
    pixels = lax.all_to_all(pixels, "dp", split_axis=0, concat_axis=0, tiled=True)
    logits = lax.all_to_all(logits, "dp", split_axis=0, concat_axis=0, tiled=True)
    my_owners, my_ranks, my_rows = [
        lax.dynamic_index_in_dim(v, dp_index, 0, keepdims=False) for v in (owners, ranks, local_rows)
    ]
    places = my_owners * buffer_labels.shape[0] + my_rows
    labels = jnp.sum(jnp.where(places[:, None] == jnp.arange(table.shape[0])[None, :], table[None, :], 0), axis=1)
    return pixels, logits, labels.astype(i32), (my_owners * capacity + my_ranks).astype(i32)


def on_device(
    current_patches,
    current_labels,
    buffer_patches,
    buffer_logits,
    buffer_labels,
    replay_owner,
    replay_row,
    seen_mask,
    patch_weight,
    patch_moment,
    patch_average,
    attention_weight,
    attention_moment,
    attention_average,
    up_weight,
    up_moment,
    up_average,
    down_weight,
    down_moment,
    down_average,
    head_weight,
    head_moment,
    head_average,
    vector_weight,
    vector_moment,
    vector_average,
):
    dp_count, cls_count = lax.axis_size("dp"), lax.axis_size("cls")
    dp_index, cls_index = lax.axis_index("dp"), lax.axis_index("cls")
    kind_rows = current_patches.shape[0]
    replay_count = 2 * kind_rows
    group_rows = 3 * kind_rows
    normal_count = kind_rows * dp_count
    patch_part = current_patches.shape[1]
    cur_own, rep_own = kind_rows // cls_count, replay_count // cls_count
    images = cur_own + rep_own
    class_part = head_weight.shape[1]
    vblock = vector_weight.shape[0] * dp_count * cls_count // BLOCKS
    tuned = dp_count == GRID_DP and cls_count == GRID_CLS and replay_count == 2 * dp_count
    masters = (patch_weight, attention_weight, up_weight, down_weight, head_weight, vector_weight)
    moments = (patch_moment, attention_moment, up_moment, down_moment, head_moment, vector_moment)
    averages = (patch_average, attention_average, up_average, down_average, head_average, vector_average)

    def views(v, j):
        return v[0].T if j in (1, 3) else v[0] if j == 2 else v

    current_view, buffer_view = current_patches.transpose(1, 0, 2), buffer_patches.transpose(1, 0, 2)
    if tuned:
        pack = pl.pallas_call(
            pack_weights_kernel,
            out_shape=sds((R_ONE + R_TWO + R_MASK, D), bf16),
            cost_estimate=cost(2),
            compiler_params=params_of(60),
        )

    def exchange(sent):
        own, near, far = sent
        far = lax.ppermute(far, "cls", flip(4, 2))
        return [own, lax.ppermute(near, "cls", flip(4, 1)), far, lax.ppermute(far[1], "cls", flip(4, 1))]

    def pick(find, stored, *operands):
        out_shape = [sds((PIX_ROWS, PD), bf16)] * 2 + [sds((2, PIX_ROWS, PD), bf16)]
        return pl.pallas_call(
            functools.partial(pick_kernel, cur_own, rep_own, find),
            out_shape=out_shape + ([sds((3, 8), i32)] if find else []),
            in_specs=[SMEM] * (4 if find else 1) + [ANY, ANY, VMEM],
            out_specs=[VMEM] * 3 + ([SMEM] if find else []),
            scratch_shapes=[
                pltpu.VMEM((patch_part, stored, PD), bf16),
                pltpu.VMEM((patch_part, kind_rows, PD), bf16),
                pltpu.VMEM((PD // 128, patch_part * stored, 128), f32),
                pltpu.VMEM((PD // 128, patch_part * kind_rows, 128), f32),
                pltpu.VMEM((stored, CPAD), f32),
                pltpu.VMEM((PIX_ROWS, PD), f32),
                pltpu.SMEM((replay_count,), i32),
                pltpu.SemaphoreType.DMA((patch_part // 7 + 1,)),
            ],
            cost_estimate=cost(7),
            compiler_params=params_of(60),
        )(*operands)

    if tuned:
        *sent, meta = pick(
            True,
            buffer_patches.shape[0],
            replay_owner.reshape(-1),
            replay_row,
            current_labels,
            buffer_labels,
            current_view,
            buffer_view,
            buffer_logits,
        )
        got = exchange(sent)
        got[1], vec = lax.optimization_barrier((got[1], vector_weight))
        vec = jnp.pad(vec, (0, 8 * D - vblock)).reshape(8, D)
        packed = pack(
            views(attention_weight, 1), patch_weight, vec, views(up_weight, 2), views(down_weight, 3), head_weight, seen_mask
        )
    else:
        moved, logits, labels, places = plain_replay(
            buffer_patches, buffer_logits, buffer_labels, replay_owner, replay_row, kind_rows
        )
        sent = pick(False, moved.shape[0], places, current_view, moved.transpose(1, 0, 2), logits)
        got = exchange(sent)
        row_mask = jnp.pad(seen_mask.astype(bf16), ((0, 0), (0, CPAD - class_part)))
        row_mask = lax.all_gather(row_mask, "cls").astype(f32)
        mask_rows = [
            lax.dynamic_slice_in_dim(row_mask, cls_index * cur_own, cur_own, 1),
            lax.dynamic_slice_in_dim(row_mask, kind_rows + cls_index * rep_own, rep_own, 1),
            jnp.zeros((cls_count, 8 - images, CPAD), f32),
        ]
        given = jnp.concatenate(mask_rows, axis=1)
        kinds = jnp.where(jnp.arange(replay_count) < kind_rows, 1, 2).astype(i32)
        labels = jnp.where(kinds == 1, 0, labels)

        def own(current, replayed, fill):
            return jnp.concatenate(
                [
                    lax.dynamic_slice_in_dim(current, cls_index * cur_own, cur_own, 0),
                    lax.dynamic_slice_in_dim(replayed, cls_index * rep_own, rep_own, 0),
                    jnp.full((8 - images,), fill, i32),
                ]
            )

        nothing = jnp.zeros_like(current_labels)
        meta = jnp.stack([own(current_labels, labels, 0), own(nothing, kinds, 3), jnp.zeros((8,), i32)])

    if tuned:
        column = [packed] + [to_z(packed, k) for k in (1, 2, 3)]
        near_one = jnp.stack([v[:R_ONE] for v in column])
        near_two = jnp.stack([v[R_ONE:] for v in column])
        near_one, got[2] = lax.optimization_barrier((near_one, got[2]))
        at_x, at_y = to_x(near_one), to_y(near_one)
        at_x, near_two = lax.optimization_barrier((at_x, near_two))
        at_x, at_y, at_xy = lax.optimization_barrier((at_x, at_y, to_y(at_x)))
        one = gather_blocks(near_one, at_x, at_y, at_xy)
        two_x, two_y = to_x(near_two), to_y(near_two)
    else:
        one, two = plain_gather(masters, vblock)
        two = [jnp.pad(v, ((0, 0), (0, R_MASK), (0, 0))) for v in two]

    n = 2
    steps = images // n
    whole = lambda shape: pl.BlockSpec(shape, lambda i: (0,) * len(shape))
    per = lambda width: pl.BlockSpec((n, ROWS_T, width), lambda i: (i, 0, 0))
    pieces = [whole((PIX_ROWS, PD))] * 2 + [pl.BlockSpec((1, PIX_ROWS, PD), lambda i: (0, 0, 0)), whole((PIX_ROWS, PD))]
    x0, qkv, attn, prm, hb, soft = pl.pallas_call(
        functools.partial(embed_kernel, tuned, vblock, n, images),
        grid=(steps,),
        in_specs=[whole((4, R_ONE, D))] * 8 + pieces,
        out_specs=[per(D), per(3 * D)] + [whole(shape) for shape in ((4 * D, D), (16, D), (8, CPAD), (4, 8, CPAD))],
        out_shape=[
            sds((images, ROWS_T, D), f32),
            sds((images, ROWS_T, 3 * D), bf16),
            sds((4 * D, D), bf16),
            sds((16, D), f32),
            sds((8, CPAD), f32),
            sds((4, 8, CPAD), f32),
        ],
        scratch_shapes=[
            pltpu.VMEM((PD, D), f32),
            pltpu.VMEM((PD, D), bf16),
            pltpu.VMEM((BLOCKS, 8, D), f32),
            pltpu.VMEM((V_ROWS, D), f32),
            pltpu.VMEM((ROWS_T, D), f32),
            pltpu.VMEM((4 * PIX_ROWS, D), f32),
            pltpu.VMEM((images, ROWS_T, D), f32),
        ],
        cost_estimate=cost(8),
        compiler_params=params_of(34),
    )(*one, *got)
    if tuned:
        two_x, two_y, hb = lax.optimization_barrier((two_x, two_y, hb))
        two_xy = to_y(two_x)
    out_part = pl.BlockSpec((D, D), lambda i: (3, 0))
    half = lambda width: pl.BlockSpec((images // 2, ROWS_T, width), lambda i: (i, 0, 0))
    att, x1 = pl.pallas_call(
        functools.partial(attend_kernel, images // 2),
        grid=(2,),
        in_specs=[out_part, whole((16, D)), half(D), half(3 * D)],
        out_specs=[half(D), half(D)],
        out_shape=[sds((images, ROWS_T, D), bf16), sds((images, ROWS_T, D), f32)],
        cost_estimate=cost(10),
        compiler_params=params_of(24),
    )(attn, prm, x0, qkv)

    if tuned:
        two_xy, x1 = lax.optimization_barrier((two_xy, x1))
        two = gather_blocks(near_two, two_x, two_y, two_xy)

    scales = (1.0 / normal_count, LABEL_WEIGHT / normal_count, LOGIT_WEIGHT / (normal_count * C))
    dx1, keep_two, send_two, vgrad, hgrad, loss = run_middle(
        tuned, images // 2, images, scales, *([] if tuned else [given]), *two, prm, hb, soft, meta, x1
    )

    def attend_back(first, *operands):
        begin, count = (0, 1) if first else (1, steps - 1)
        some = lambda width: pl.BlockSpec((n, ROWS_T, width), lambda i: (i + begin, 0, 0))
        return pl.pallas_call(
            functools.partial(attend_back_kernel, n, first),
            grid=(count,),
            in_specs=[out_part, whole((16, D)), some(3 * D), some(D), some(D)] + ([] if first else [whole((D, D)), ANY]),
            out_specs=[some(3 * D), whole((D, D)), whole((16, D))],
            out_shape=[sds((images, ROWS_T, 3 * D), bf16), sds((D, D), f32), sds((16, D), f32)],
            input_output_aliases={} if first else {6: 0},
            cost_estimate=cost(6 * count),
            compiler_params=params_of(22),
        )(*operands)

    dqkv, acc_out, vgrad = attend_back(True, attn, vgrad, qkv, att, dx1)
    if tuned:
        a_code, a_keep, b_code, b_keep = scatter_first(keep_two, to_core(send_two), SECTIONS_TWO)
        a_code, b_code, vgrad = lax.optimization_barrier((a_code, b_code, vgrad))
        moving = (to_x(a_code), to_y(b_code))
    dqkv, acc_out, vgrad = attend_back(False, attn, vgrad, qkv, att, dx1, acc_out, dqkv)
    acc = pl.pallas_call(
        functools.partial(qkv_back_kernel, n),
        grid=(steps,),
        in_specs=[whole((16, D)), per(D), per(3 * D), whole((D, D))],
        out_specs=whole((4 * D, D)),
        out_shape=sds((4 * D, D), f32),
        cost_estimate=cost(6),
        compiler_params=params_of(22),
    )(prm, x0, dqkv, acc_out)
    if tuned:
        acc, a_keep = lax.optimization_barrier((acc, a_keep))
        a_code, a_rest, b_code, b_rest = scatter_second(a_keep, b_keep, *moving, SECTIONS_TWO)
        a_code, b_code, vgrad = lax.optimization_barrier((a_code, b_code, vgrad))
        moving = (to_y(a_code), to_x(b_code))
    acc_patch, blocks = pl.pallas_call(
        functools.partial(unit_back_kernel, n, vblock, images),
        grid=(steps,),
        in_specs=[whole((3 * D, D)), whole((16, D)), whole((16, D)), whole((8, CPAD))]
        + pieces
        + [per(D), per(3 * D), per(D)],
        out_specs=[whole((PD, D)), whole((BLOCKS, 8, D))],
        out_shape=[sds((PD, D), f32), sds((BLOCKS, 8, D), f32)],
        scratch_shapes=[
            pltpu.VMEM((16, D), f32),
            pltpu.VMEM((images, ROWS_T, D), f32),
            pltpu.VMEM((4 * PIX_ROWS, D), f32),
            pltpu.VMEM((V_ROWS, D), f32),
        ],
        cost_estimate=cost(6),
        compiler_params=params_of(28),
    )(attn, prm, vgrad, hgrad, *got, x0, dqkv, dx1)
    if tuned:
        rest_two, code_two = scatter_third_pair(a_rest, b_rest, *moving, SECTIONS_TWO)
        code_two, blocks = lax.optimization_barrier((code_two, blocks))
    keep_one, send_one = pl.pallas_call(
        functools.partial(block_back_kernel, tuned),
        out_shape=[sds((16, R_ONE, D), f32), sds((16, R_ONE + R_CODE, D), jnp.int16)],
        cost_estimate=cost(2),
        compiler_params=params_of(20),
    )(acc, acc_patch, blocks)

    if tuned:
        a_code, a_keep, b_code, b_keep = scatter_first(keep_one, to_core(send_one), SECTIONS_ONE)
        code_two, a_code, b_code = lax.optimization_barrier((code_two, a_code, b_code))
        moving = (to_x(a_code), to_y(b_code))
        own_two, code_two = scatter_near(rest_two, to_z(code_two, 1), SECTIONS_TWO)
        code_two, a_keep = lax.optimization_barrier((code_two, a_keep))
        a_code, a_rest, b_code, b_rest = scatter_second(a_keep, b_keep, *moving, SECTIONS_ONE)
        code_two, a_code, b_code = lax.optimization_barrier((code_two, a_code, b_code))
        moving = (to_y(a_code), to_x(b_code))
        share_two, sums = scatter_fourth(own_two, [to_z(code_two, 2)], SECTIONS_TWO, loss)
        own_one, *codes_one = scatter_third(a_rest, b_rest, *moving, SECTIONS_ONE)
        last_one = [to_z(code, k + 1) for k, code in enumerate(codes_one)]
        share_one, sums = scatter_fourth(own_one, last_one, SECTIONS_ONE, sums)
    else:
        shares = plain_scatter((keep_one, send_one), (keep_two, send_two), vblock)
        squares = sum(jnp.sum(share * share) for share in shares)
        sums = loss + jnp.where(lax.broadcasted_iota(i32, (8, 128), 1) == 0, squares, 0.0)
    if tuned:
        states = [views(v, j) for j in range(6) for v in (masters[j], moments[j], averages[j])]
        vector_share = share_one[72:80].reshape(-1)[:vblock]
        totals, *news = pl.pallas_call(
            update_kernel,
            out_shape=[sds((2,), f32)] + [sds(v.shape, f32) for v in states],
            in_specs=[VMEM] * 25,
            out_specs=[SMEM] + [VMEM] * 18,
            compiler_params=params_of(24),
        )(*sums_along_z(sums), share_one, share_two, vector_share, *states)
        results = [totals[0], totals[1]]
        for j in range(18):
            results.append(news[j].T[None] if j // 3 in (1, 3) else news[j][None] if j // 3 == 2 else news[j])
    else:
        sums = lax.psum(sums, ("dp", "cls"))
        norm_value = jnp.sqrt(sums[0, 0])
        clip_factor = jnp.minimum(1.0, CLIP_NORM / (norm_value + 1e-06))
        results = [sums[0, 1], norm_value]
        for weight, moment, average, share in zip(masters, moments, averages, shares):
            results += list(advance(weight, moment, average, share, clip_factor))
    return tuple(results)


def solution(mesh):
    split_rows, split_columns = P(("dp", "cls"), None), P(None, None, ("dp", "cls"))
    states = (
        [split_rows] * 3
        + [split_columns] * 3
        + [P(None, "dp", "cls")] * 3
        + [P(None, "cls", "dp")] * 3
        + [P("dp", "cls")] * 3
        + [P(("dp", "cls"))] * 3
    )
    in_specs = (
        P("dp", "cls", None),
        P("dp"),
        P("dp", "cls", None),
        P("dp", "cls"),
        P("dp"),
        P(),
        P(),
        P("dp", "cls"),
        *states,
    )
    out_specs = (P(), P(), *states)
    return jax.shard_map(on_device, mesh=mesh, in_specs=in_specs, out_specs=out_specs, check_vma=False)
```

```python
import functools
import math

import jax
import jax.numpy as jnp
from jax import lax
from jax.experimental import pallas as pl
from jax.experimental.pallas import tpu as pltpu
from jax.sharding import PartitionSpec as P

D = 384
HEADS = 6
HD = 64
FF = 1536
C = 1000
PD = 768
TOK = 197
PATCHES = 196
PARAMS = 2531176

NORM_EPS = 1e-06
SCORE_SCALE = 0.125
LOGIT_WEIGHT = 0.3
LABEL_WEIGHT = 0.8
MOMENTUM_DECAY = 0.9
AVERAGE_KEEP = 0.75
CLIP_NORM = 0.005
RATE = 0.03 * math.sqrt(PARAMS) / CLIP_NORM

ROWS_T = 208
GRID_DP, GRID_CLS = 8, 4
BLOCKS = GRID_DP * GRID_CLS
CPART = C // GRID_CLS
CPAD = 256
F_CHUNK = 512
R_ONE = 80
R_TWO = 128
R_MASK = 16
PIX_ROWS = 304
V_ROWS = 232
HEAD_AT = (TOK + 4) * D
LAYER_AT = HEAD_AT + C

bf16 = jnp.bfloat16
f32 = jnp.float32
i32 = jnp.int32

ANY = pl.BlockSpec(memory_space=pl.ANY)
VMEM = pl.BlockSpec(memory_space=pltpu.VMEM)
SMEM = pl.BlockSpec(memory_space=pltpu.SMEM)


def sds(shape, dtype):
    return jax.ShapeDtypeStruct(shape, dtype)


def cost(micros):
    return pl.CostEstimate(flops=int(micros * 1e8), bytes_accessed=1 << 20, transcendentals=0)


def params_of(limit_mib, **more):
    return pltpu.CompilerParams(vmem_limit_bytes=limit_mib << 20, **more)


def nn(a, b):
    return lax.dot_general(a, b, (((1,), (0,)), ((), ())), preferred_element_type=f32)


def nt(a, b):
    return lax.dot_general(a, b, (((1,), (1,)), ((), ())), preferred_element_type=f32)


def tn(a, b):
    return lax.dot_general(a, b, (((0,), (0,)), ((), ())), preferred_element_type=f32)


def gelu_parts(values):
    bell = jnp.exp(-0.5 * values * values)
    t = 1.0 / (1.0 + (0.3275911 * 0.5**0.5) * jnp.abs(values))
    tail = 0.5 * 1.061405429 * t - 0.5 * 1.453152027
    tail = tail * t + 0.5 * 1.421413741
    tail = tail * t - 0.5 * 0.284496736
    tail = (tail * t + 0.5 * 0.254829592) * t * bell
    return jnp.where(values < 0.0, tail, 1.0 - tail), bell * (1.0 / math.sqrt(2.0 * math.pi))


def normalize(values):
    centred = values - jnp.mean(values, axis=-1, keepdims=True)
    inverse = lax.rsqrt(jnp.mean(centred * centred, axis=-1, keepdims=True) + NORM_EPS)
    return (centred * inverse, inverse)


def normalize_back(unit, inverse, grad_unit):
    return inverse * (
        grad_unit
        - jnp.mean(grad_unit, axis=-1, keepdims=True)
        - unit * jnp.mean(grad_unit * unit, axis=-1, keepdims=True)
    )


def advance(weight, moment, average, grad, clip_factor):
    clipped = clip_factor * grad
    moment_new = MOMENTUM_DECAY * moment + clipped
    weight_new = weight - RATE * (clipped + MOMENTUM_DECAY * moment_new)
    average_new = AVERAGE_KEEP * average + (1.0 - AVERAGE_KEEP) * weight_new
    return (weight_new, moment_new, average_new)


def pack_head(block):
    a, b, c = block[..., :16, :], block[..., 16:32, :], block[..., 32:, :]
    top = jnp.concatenate([a, b[..., :128]], axis=-1)
    low = jnp.concatenate([b[..., 128:], c], axis=-1)
    return jnp.concatenate([top, low], axis=-2)


def unpack_head(block):
    top, low = block[..., :16, :], block[..., 16:, :]
    b = jnp.concatenate([top[..., 256:], low[..., :128]], axis=-1)
    return jnp.concatenate([top[..., :256], b, low[..., 128:]], axis=-2)


def me_of(tuned):
    if tuned:
        return lax.axis_index("dp") * GRID_CLS + lax.axis_index("cls")
    return 0


def grad_place(s):
    core, x, y, z = s & 1, (s >> 1) & 1, (s >> 2) & 1, s >> 3
    if z < 2:
        return core, (0 if x else 4) + 2 * y + z
    return core, (8 if y else 12) + 2 * x + (z - 2)


R_CODE = 16
SECTIONS_ONE = (0, 48, 72, 80)
SECTIONS_TWO = (0, 32, 80, 128)


def coded(sections):
    return sections[-1] + (R_CODE if sections == SECTIONS_TWO else 0)


def thrice(row):
    return jnp.concatenate([row] * 3, axis=1)


def to_code(values):
    return jnp.clip(values, -32767.0, 32767.0).astype(i32).astype(jnp.int16)


def encode(block, sections, out):
    rows = sections[-1]
    inside = coded(sections) == rows
    powers = []
    for j, (a, b) in enumerate(zip(sections[:-1], sections[1:])):
        part = block[j] if isinstance(block, list) else block[a:b]
        most = jnp.max(jnp.abs(part), axis=0, keepdims=True)
        if inside:
            most = jnp.maximum(jnp.maximum(most[:, :128], most[:, 128:256]), most[:, 256:])
        power = jnp.clip(jnp.ceil(jnp.log2(jnp.maximum(most, 1e-30))), -99.0, 126.0)
        powers.append(power)
        code = jnp.round(part * jnp.exp2(15.0 - (thrice(power) if inside else power)))
        if inside and b == rows:
            last = lax.broadcasted_iota(i32, code.shape, 0) == code.shape[0] - 1
            code = jnp.where(last, jnp.concatenate(powers, axis=1), code)
        out[a:b, :] = to_code(code)
    if not inside:
        powers.append(jnp.zeros((R_CODE - len(powers), D), f32))
        out[rows : rows + R_CODE, :] = to_code(jnp.concatenate(powers, axis=0))


def put_block(parts, sections, keep, send, core, place):
    if core:
        encode(parts, sections, send.at[place])
    else:
        for part, a, b in zip(parts, sections[:-1], sections[1:]):
            keep[place, a:b, :] = part


def decode(code, sections):
    rows = sections[-1]
    parts = [code[a:b, :].astype(i32).astype(f32) for a, b in zip(sections[:-1], sections[1:])]
    if coded(sections) == rows:
        row = parts[-1][-1:]
        powers = [thrice(row[:, j * 128 : (j + 1) * 128]) for j in range(3)]
        last = lax.broadcasted_iota(i32, parts[-1].shape, 0) == parts[-1].shape[0] - 1
        parts[-1] = jnp.where(last, 0.0, parts[-1])
    else:
        rest = code[rows : rows + R_CODE, :].astype(i32).astype(f32)
        powers = [rest[j : j + 1] for j in range(3)]
    return jnp.concatenate([part * jnp.exp2(power - 15.0) for part, power in zip(parts, powers)], axis=0)


def pack_mask(block):
    a, b, c = block[:8], block[8:16], block[16:]
    top = jnp.concatenate([a, b[:, :128]], axis=1)
    return jnp.concatenate([top, jnp.concatenate([b[:, 128:], c], axis=1)], axis=0)


def unpack_mask(block):
    top, low = block[:8], block[8:]
    b = jnp.concatenate([top[:, 256:], low[:, :128]], axis=1)
    return jnp.concatenate([top[:, :256], b, low[:, 128:]], axis=0)


def pack_weights_kernel(attn, patch, vec, up, down, head, seen, out):
    one, two = out.at[0:R_ONE], out.at[R_ONE:]
    one[0:48, :] = attn[...].astype(bf16)
    one[48:80, :] = jnp.concatenate([patch[...], vec[...]], axis=0).astype(bf16)
    block = jnp.concatenate([head[...], jnp.zeros((48, CPAD - CPART), f32)], axis=1)
    two[0:32, :] = pack_head(block).astype(bf16)
    two[32:80, :] = up[...].astype(bf16)
    two[80:128, :] = down[...].astype(bf16)
    mask = jnp.concatenate([seen[...].astype(f32), jnp.zeros((seen.shape[0], CPAD - CPART), f32)], axis=1)
    two[128:144, :] = pack_mask(mask).astype(bf16)


def pick_kernel(cur_own, rep_own, find, *refs):
    if find:
        owner, row, cur_labels, buf_labels, cur, buf, logits, o0, o1, far, meta, *scratch = refs
    else:
        row, cur, buf, logits, o0, o1, far, *scratch = refs
    stage, stage_cur, wide, wide_cur, soft, res, slots, sems = scratch
    parts, stored, _ = stage.shape
    kind = stage_cur.shape[1]
    chunk = 7
    copies = [pltpu.make_async_copy(cur, stage_cur, sems.at[parts // chunk])]
    for j in range(parts // chunk):
        part = pl.ds(j * chunk, chunk)
        copies.append(pltpu.make_async_copy(buf.at[part], stage.at[part], sems.at[j]))
    for copy in copies:
        copy.start()
    me = lax.axis_index("cls")
    if find:
        mine = lax.axis_index("dp")

        def look(i, count):
            hit = owner[i] == mine

            @pl.when(hit)
            def _():
                slots[count] = i

            return count + jnp.where(hit, 1, 0)

        lax.fori_loop(0, owner.shape[0], look, 0)
        for m in range(8):
            if m < cur_own:
                meta[0, m] = cur_labels[me * cur_own + m]
                meta[1, m] = 0
                meta[2, m] = mine * 3 * kind + me * cur_own + m
            elif m < cur_own + rep_own:
                i = slots[me * rep_own + m - cur_own]
                at = lax.rem(i, 2 * kind)
                meta[0, m] = jnp.where(at < kind, 0, buf_labels[row[i]])
                meta[1, m] = jnp.where(at < kind, 1, 2)
                meta[2, m] = lax.div(i, 2 * kind) * 3 * kind + kind + at
            else:
                meta[0, m] = 0
                meta[1, m] = 3
                meta[2, m] = 0
    else:
        for k in range(4 * rep_own):
            slots[k] = k
    soft[...] = jnp.zeros_like(soft)
    soft[:, :CPART] = logits[...].astype(f32)
    for j, copy in enumerate(copies):
        copy.wait()
        for lanes in range(PD // 128):
            at = slice(lanes * 128, (lanes + 1) * 128)
            if j == 0:
                wide_cur[lanes] = stage_cur[:, :, at].astype(f32).reshape(parts * kind, 128)
            else:
                one = stage[(j - 1) * chunk : j * chunk, :, at].astype(f32).reshape(chunk * stored, 128)
                wide[lanes, (j - 1) * chunk * stored : j * chunk * stored, :] = one
    images = cur_own + rep_own
    res[images * parts :, :] = jnp.zeros((PIX_ROWS - images * parts, PD), f32)
    for k, out in enumerate((o0, o1, far.at[0], far.at[1])):
        to = me ^ k
        for m in range(images):
            if m >= cur_own:
                r = row[slots[to * rep_own + m - cur_own]]
                at = (m % 3) * CPAD
                res[images * parts + m // 3 : images * parts + m // 3 + 1, at : at + CPAD] = soft[pl.ds(r, 1), :]
            for lanes in range(PD // 128):
                if m < cur_own:
                    one = wide_cur[lanes, pl.ds(to * cur_own + m, parts, stride=kind), :]
                else:
                    one = wide[lanes, pl.ds(r, parts, stride=stored), :]
                res[m * parts : (m + 1) * parts, lanes * 128 : (lanes + 1) * 128] = one
        out[...] = res[...].astype(bf16)


def spread_vector(vblock, blocks, flat):
    flat[...] = jnp.zeros_like(flat)
    lane = lax.broadcasted_iota(i32, (8, D), 1)
    for d in range(BLOCKS):
        q, s = divmod(vblock * d, D)
        b = blocks[d]
        if s:
            b = pltpu.roll(b, s, 1)
        flat[q : q + 8, :] = flat[q : q + 8, :] + jnp.where(lane >= s, b, 0.0)
        if s:
            flat[q + 1 : q + 9, :] = flat[q + 1 : q + 9, :] + jnp.where(lane < s, b, 0.0)


def cut_vector(vblock, flat, blocks):
    lane = lax.broadcasted_iota(i32, (8, D), 1)
    place = lax.broadcasted_iota(i32, (8, D), 0) * D + lane
    for d in range(BLOCKS):
        q, s = divmod(vblock * d, D)
        b = flat[q : q + 8, :]
        if s:
            a = pltpu.roll(b, D - s, 1)
            b = pltpu.roll(flat[q + 1 : q + 9, :], D - s, 1)
            b = jnp.where(lane < D - s, a, b)
        blocks[d] = jnp.where(place < vblock, b, 0.0)


def layer_vectors(flat):
    row, s = divmod(LAYER_AT, D)
    lane = lax.broadcasted_iota(i32, (12, D), 1)
    a = pltpu.roll(flat[row : row + 16, :], D - s, 1)
    return jnp.where(lane < D - s, a[0:12], a[1:13])


def head_vector(flat):
    rows = []
    wide = lax.broadcasted_iota(i32, (1, D), 1)
    for part in range(GRID_CLS):
        row, s = divmod(HEAD_AT + part * CPART, D)
        a = flat[row : row + 1, :]
        if s:
            a = pltpu.roll(jnp.broadcast_to(a, (8, D)), D - s, 1)[0:1]
            b = pltpu.roll(jnp.broadcast_to(flat[row + 1 : row + 2, :], (8, D)), D - s, 1)[0:1]
            a = jnp.where(wide < D - s, a, b)
        rows.append(jnp.where(wide < CPART, a, 0.0)[:, :CPAD])
    return jnp.concatenate(rows, axis=0)


def store_flat(flat, at, values, count):
    row, s = divmod(at, D)
    wide = lax.broadcasted_iota(i32, (1, D), 1)
    values = jnp.where(wide < count, values, 0.0)
    if s:
        values = pltpu.roll(jnp.broadcast_to(values, (8, D)), s, 1)[0:1]
        flat[row + 1 : row + 2, :] = flat[row + 1 : row + 2, :] + jnp.where(wide < s, values, 0.0)
    flat[row : row + 1, :] = flat[row : row + 1, :] + jnp.where(wide >= s, values, 0.0)


def piece_of(weights, corners, s):
    a, z = s & 7, s >> 3
    return weights[a].at[z] if a < 6 else corners[(a - 6) * 2 + (z >> 1)].at[z & 1]


def head_masks():
    keys = lax.broadcasted_iota(i32, (1, ROWS_T, ROWS_T), 1) < TOK
    low = lax.broadcasted_iota(i32, (ROWS_T, 128), 1) < HD
    low_t = lax.broadcasted_iota(i32, (128, ROWS_T), 0) < HD
    return keys, low, low_t


def apart(two, low, axis):
    none = jnp.zeros_like(two)
    return jnp.concatenate([jnp.where(low, two, none), jnp.where(low, none, two)], axis=axis)


def pair_probs(q2, k2, keys, low):
    scores = nt(apart(k2, low, 0), q2).reshape(2, ROWS_T, ROWS_T) * SCORE_SCALE
    scores = jnp.where(keys, scores, -1e30)
    powers = jnp.exp(scores - jnp.max(scores, axis=1, keepdims=True))
    return powers * (1.0 / jnp.sum(powers, axis=1, keepdims=True))


def embed_kernel(tuned, vblock, n, images, *refs):
    (w0, w1, w2, w3, w4, w5, w6, w7, w8, w9, p0, p1, p2, p3, x0_out, qkv_out, attn, prm, hb, soft,
     patch_wide, patch, blocks, flat, table, rows, x0_all) = refs
    weights = (w0, w1, w2, w3, w4, w5)
    corners = (w6, w7, w8, w9)
    p2 = p2.at[0]
    me = me_of(tuned)
    part = lax.axis_index("cls")
    per = PATCHES // 4

    @pl.when(pl.program_id(0) == 0)
    def _():
        for s in range(BLOCKS):
            d = s ^ me
            w = piece_of(weights, corners, s)
            attn[pl.ds(pl.multiple_of(d * 48, 16), 48), :] = w[0:48, :]
            rest = w[48:80, :].astype(f32)
            patch_wide[pl.ds(pl.multiple_of(d * 24, 8), 24), :] = rest[0:24]
            blocks[d] = rest[24:32]
        patch[...] = patch_wide[...].astype(bf16)
        spread_vector(vblock, blocks, flat)
        prm[0:12, :] = layer_vectors(flat)
        prm[12:13, :] = flat[TOK + 1 : TOK + 2, :]
        prm[13:14, :] = flat[TOK + 2 : TOK + 3, :]
        prm[14:16, :] = jnp.zeros((2, D), f32)
        hb[0:4, :] = head_vector(flat)
        hb[4:8, :] = jnp.zeros((4, CPAD), f32)
        bias = flat[TOK : TOK + 1, :]
        table[...] = jnp.zeros_like(table)
        for k in range(4):
            for q in range(4):

                @pl.when((part ^ k) == q)
                def _(k=k, q=q):
                    table[k * per : k * per + per, :] = flat[1 + q * per : 1 + q * per + per, :] + bias

        table[PATCHES : PATCHES + 1, :] = flat[0:1, :] + flat[TOK + 3 : TOK + 4, :]
        soft[...] = jnp.zeros_like(soft)
        for k, piece in enumerate((p0, p1, p2, p3)):
            rows[k * PIX_ROWS : (k + 1) * PIX_ROWS, :] = nn(piece[...], patch[...])
            stored = piece[PIX_ROWS - 16 :, :].astype(f32)
            at = images * per - (PIX_ROWS - 16)
            for m in range(images):
                soft[part ^ k, m : m + 1, :] = stored[at + m // 3 : at + m // 3 + 1, (m % 3) * CPAD : (m % 3 + 1) * CPAD]
        for m in range(images):
            x0_all[m] = table[...]
            for k in range(4):
                at = slice(k * per, k * per + per)
                begin = k * PIX_ROWS + m * per
                x0_all[m, at, :] = x0_all[m, at, :] + rows[begin : begin + per, :]

    tokens = n * ROWS_T
    x0 = x0_all[pl.ds(pl.program_id(0) * n, n)]
    x0_out[...] = x0
    unit, _ = normalize(x0)
    normed = (unit * prm[0:1, :] + prm[1:2, :]).astype(bf16).reshape(tokens, D)
    for j, bias in ((0, prm[2:3, :]), (1, None), (2, prm[3:4, :])):
        one = nt(normed, attn[j * D : (j + 1) * D, :])
        if bias is not None:
            one = one + bias
        qkv_out[:, :, j * D : (j + 1) * D] = one.astype(bf16).reshape(n, ROWS_T, D)


def attend_kernel(n, w_out, prm, x0, qkv, att_out, x1_out):
    tokens = n * ROWS_T
    keys, low, low_t = head_masks()
    for i in range(n):
        for p in range(HEADS // 2):
            at = p * 128
            q2 = qkv[i, :, at : at + 128]
            v2t = qkv[i, :, 2 * D + at : 2 * D + at + 128].T
            probs = pair_probs(q2, qkv[i, :, D + at : D + at + 128], keys, low).astype(bf16)
            both = nn(apart(v2t, low_t, 1), probs.reshape(2 * ROWS_T, ROWS_T))
            att_out[i, :, at : at + 128] = both.T.astype(bf16)
    branch = nt(att_out[...].reshape(tokens, D), w_out[...]) + prm[4:5, :]
    x1_out[...] = x0[...] + branch.reshape(n, ROWS_T, D)


def middle_kernel(tuned, n, images, scales, *refs):
    if not tuned:
        given, *refs = refs
    (w0, w1, w2, w3, w4, w5, w6, w7, w8, w9, prm, hb, soft, meta, x1_in,
     dx1_out, keep, send, vgrad, hgrad, loss,
     w_up, w_down, w_head, act, slope, mask, masks_all, pooled, dpooled, glow, acc_up, acc_down,
     normed_all, dy_all, dup_all, up_bias, up_sum) = refs
    weights = (w0, w1, w2, w3, w4, w5)
    corners = (w6, w7, w8, w9)
    me = me_of(tuned)
    step = pl.program_id(0)
    last = pl.num_programs(0) - 1

    @pl.when(step == 0)
    def _():
        for s in range(BLOCKS):
            d = s ^ me
            dp, cl = d >> 2, d & 3
            w = piece_of(weights, corners, s)
            rows = pl.ds(pl.multiple_of(dp * 48, 16), 48)
            w_head[cl, rows, :] = unpack_head(w[0:32, :])
            columns = pl.ds(pl.multiple_of(cl * D, 128), D)
            w_up[rows, columns] = w[32:80, :]
            w_down[rows, columns] = w[80:128, :]
            if tuned:
                seen = unpack_mask(w[128:144, :].astype(f32))
                masks_all[cl, pl.ds(pl.multiple_of(dp * 24, 8), 24), :] = seen
        if tuned:
            mask[...] = jnp.zeros_like(mask)
            for m in range(images):
                for q in range(4):
                    mask[q, m : m + 1, :] = masks_all[q, pl.ds(meta[2, m], 1), :]
        else:
            mask[...] = given[...]
        for c in range(4):
            up_bias[:, c * D : (c + 1) * D] = prm[8 + c : 9 + c, :]
        up_sum[...] = jnp.zeros_like(up_sum)
        vgrad[...] = jnp.zeros_like(vgrad)
        pooled[...] = jnp.zeros_like(pooled)

    tokens = n * ROWS_T
    x1 = x1_in[...].reshape(tokens, D)
    unit_two, inverse_two = normalize(x1)
    normed = (unit_two * prm[5:6, :] + prm[6:7, :]).astype(bf16)
    total = jnp.zeros((tokens, D), f32)
    mine = pl.ds(pl.multiple_of(step * tokens, 16), tokens)
    normed_all[mine, :] = normed
    chunks = [slice(c, c + F_CHUNK) for c in range(0, FF, F_CHUNK)]
    for c in chunks:
        pre = nn(normed, w_up[:, c]) + up_bias[:, c]
        half, bell = gelu_parts(pre)
        hot = (pre * half).astype(bf16)
        act[mine, c] = hot
        slope[:, c] = half + pre * bell
        total = total + nt(hot, w_down[:, c])
    x2 = x1 + (total + prm[7:8, :])
    unit, inverse = normalize(x2)
    real = lax.broadcasted_iota(i32, (ROWS_T, D), 0) < TOK
    sums = []
    for i in range(n):
        u = unit[i * ROWS_T : (i + 1) * ROWS_T]
        sums.append(jnp.sum(jnp.where(real, u, 0.0), axis=0, keepdims=True))
        pooled[pl.ds(step * n + i, 1), :] = sums[i] * (1.0 / TOK) * prm[12:13, :] + prm[13:14, :]

    low = pooled[...].astype(bf16)
    rows8 = (16, CPAD)
    row_id = lax.broadcasted_iota(i32, rows8, 0)
    lane = lax.broadcasted_iota(i32, rows8, 1)
    label = jnp.full(rows8, -1, i32)
    weight = jnp.zeros(rows8, f32)
    squared = jnp.zeros(rows8, f32)
    for i in range(images):
        kind = meta[1, i]
        label = jnp.where(row_id == i, meta[0, i], label)
        weight = jnp.where(row_id == i, jnp.where(kind == 0, scales[0], jnp.where(kind == 2, scales[1], 0.0)), weight)
        squared = jnp.where(row_id == i, jnp.where(kind == 1, 1.0, 0.0), squared)
    inside = lane < CPART
    logits, hots, lives, masks, tops = [], [], [], [], []
    pad = jnp.zeros((8, CPAD), f32)
    for q in range(4):
        one = nn(low, w_head[q]) + hb[q : q + 1, :]
        hot = (lane + q * CPART == label) & inside
        seen = (jnp.concatenate([mask[q], pad], axis=0) > 0.5) & inside
        logits.append(one)
        hots.append(hot)
        masks.append(seen)
        lives.append(seen | hot)
        tops.append(jnp.max(jnp.where(inside, one, -3e38), axis=1, keepdims=True))
    top = jnp.maximum(jnp.maximum(tops[0], tops[1]), jnp.maximum(tops[2], tops[3]))
    alive = sum(
        jnp.sum(jnp.where(lives[q], jnp.exp(logits[q] - top), 0.0), axis=1, keepdims=True) for q in range(4)
    )
    norm = top + jnp.log(alive)
    target = sum(jnp.sum(jnp.where(hots[q], logits[q], 0.0), axis=1, keepdims=True) for q in range(4))
    cross = norm - target
    value = jnp.sum(jnp.where(weight[:, 0:1] > 0, weight[:, 0:1] * cross, 0.0))
    back = jnp.zeros((16, D), f32)
    for q in range(4):
        gap = jnp.where(masks[q], logits[q] - jnp.concatenate([soft[q], pad], axis=0), 0.0)
        value = value + scales[2] * jnp.sum(squared * gap * gap)
        share = jnp.where(lives[q], jnp.exp(logits[q] - norm), 0.0)
        grad = weight * (share - jnp.where(hots[q], 1.0, 0.0)) + squared * (2.0 * scales[2]) * gap
        g = grad.astype(bf16)
        glow[q] = g
        back = back + nt(g, w_head[q])
    dpooled[...] = back

    pieces = []
    for i in range(n):
        grad = dpooled[pl.ds(step * n + i, 1), :]
        vgrad[12:13, :] = vgrad[12:13, :] + grad * (1.0 / TOK) * sums[i]
        vgrad[13:14, :] = vgrad[13:14, :] + grad
        dz = grad * (1.0 / TOK) * prm[12:13, :]
        u = unit[i * ROWS_T : (i + 1) * ROWS_T]
        d = inverse[i * ROWS_T : (i + 1) * ROWS_T] * (
            dz - jnp.mean(dz, axis=-1, keepdims=True) - u * jnp.mean(dz * u, axis=-1, keepdims=True)
        )
        pieces.append(jnp.where(real, d, 0.0))
    dx2 = jnp.concatenate(pieces, axis=0)
    dy = dx2.astype(bf16)
    vgrad[7:8, :] = vgrad[7:8, :] + jnp.sum(dy.astype(f32), axis=0, keepdims=True)
    dy_all[mine, :] = dy
    dnormed = jnp.zeros((tokens, D), f32)
    for c in chunks:
        dup = (nn(dy, w_down[:, c]) * slope[:, c]).astype(bf16)
        up_sum[:, c] = up_sum[:, c] + jnp.sum(dup.astype(f32), axis=0, keepdims=True)
        dup_all[mine, c] = dup
        dnormed = dnormed + nt(dup, w_up[:, c])
    vgrad[5:6, :] = vgrad[5:6, :] + jnp.sum(dnormed * unit_two, axis=0, keepdims=True)
    vgrad[6:7, :] = vgrad[6:7, :] + jnp.sum(dnormed, axis=0, keepdims=True)
    dx1 = dx2 + normalize_back(unit_two, inverse_two, dnormed * prm[5:6, :])
    dx1_out[...] = dx1.reshape(n, ROWS_T, D)

    @pl.when(step == last)
    def _():
        loss[...] = jnp.where(lax.broadcasted_iota(i32, loss.shape, 1) == 0, 0.0, value)
        hgrad[...] = jnp.zeros_like(hgrad)
        for q in range(4):
            hgrad[q : q + 1, :] = jnp.sum(glow[q].astype(f32), axis=0, keepdims=True)
        for c in range(4):
            vgrad[8 + c : 9 + c, :] = up_sum[:, c * D : (c + 1) * D]
        for q in range(4):
            slope[0:D, q * CPAD : (q + 1) * CPAD] = tn(low, glow[q])
        for c in chunks:
            acc_down[:, c] = tn(dy_all[...], act[:, c])
            acc_up[:, c] = tn(normed_all[...], dup_all[:, c])
        for s in range(BLOCKS):
            d = s ^ me
            dp, cl = d >> 2, d & 3
            core, place = grad_place(s)
            rows = pl.ds(pl.multiple_of(dp * 48, 8), 48)
            columns = pl.ds(pl.multiple_of(cl * D, 128), D)
            head = slope[rows, pl.ds(pl.multiple_of(cl * CPAD, 128), CPAD)]
            block = [pack_head(head), acc_up[rows, columns], acc_down[rows, columns]]
            put_block(block, SECTIONS_TWO, keep, send, core, place)


def run_middle(tuned, n, images, scales, *operands):
    steps = images // n
    whole = lambda shape: pl.BlockSpec(shape, lambda i: (0,) * len(shape))
    per = lambda width: pl.BlockSpec((n, ROWS_T, width), lambda i: (i, 0, 0))
    return pl.pallas_call(
        functools.partial(middle_kernel, tuned, n, images, scales),
        grid=(steps,),
        in_specs=[whole((4, 8, CPAD))] * (0 if tuned else 1)
        + [whole((4, R_TWO + R_MASK, D))] * 6
        + [whole((2, R_TWO + R_MASK, D))] * 4
        + [whole((16, D)), whole((8, CPAD)), whole((4, 8, CPAD))]
        + [SMEM, per(D)],
        out_specs=[
            per(D),
            whole((16, R_TWO, D)),
            whole((16, coded(SECTIONS_TWO), D)),
            whole((16, D)),
            whole((8, CPAD)),
            whole((8, 128)),
        ],
        out_shape=[
            sds((images, ROWS_T, D), f32),
            sds((16, R_TWO, D), f32),
            sds((16, coded(SECTIONS_TWO), D), jnp.int16),
            sds((16, D), f32),
            sds((8, CPAD), f32),
            sds((8, 128), f32),
        ],
        scratch_shapes=[
            pltpu.VMEM((D, FF), bf16),
            pltpu.VMEM((D, FF), bf16),
            pltpu.VMEM((4, D, CPAD), bf16),
            pltpu.VMEM((images * ROWS_T, FF), bf16),
            pltpu.VMEM((n * ROWS_T, FF), f32),
            pltpu.VMEM((4, 8, CPAD), f32),
            pltpu.VMEM((4, GRID_DP * 24, CPAD), f32),
            pltpu.VMEM((16, D), f32),
            pltpu.VMEM((16, D), f32),
            pltpu.VMEM((4, 16, CPAD), bf16),
            pltpu.VMEM((D, FF), f32),
            pltpu.VMEM((D, FF), f32),
            pltpu.VMEM((images * ROWS_T, D), bf16),
            pltpu.VMEM((images * ROWS_T, D), bf16),
            pltpu.VMEM((images * ROWS_T, FF), bf16),
            pltpu.VMEM((1, FF), f32),
            pltpu.VMEM((1, FF), f32),
        ],
        cost_estimate=cost(30),
        compiler_params=params_of(36),
    )(*operands)


def attend_back_kernel(n, first, *refs):
    if first:
        (w_out, vgrad_in, qkv, att, dx1_in, dqkv, acc, vgrad) = refs
    else:
        (w_out, vgrad_in, qkv, att, dx1_in, acc_in, _, dqkv, acc, vgrad) = refs

    @pl.when(pl.program_id(0) == 0)
    def _():
        acc[...] = jnp.zeros_like(acc) if first else acc_in[...]
        vgrad[...] = vgrad_in[...]

    tokens = n * ROWS_T
    dout = dx1_in[...].reshape(tokens, D).astype(bf16)
    vgrad[4:5, :] = vgrad[4:5, :] + jnp.sum(dout.astype(f32), axis=0, keepdims=True)
    acc[...] = acc[...] + tn(dout, att[...].reshape(tokens, D))
    datt = nn(dout, w_out[...]).astype(bf16)
    keys, low, low_t = head_masks()
    both = (2 * ROWS_T, ROWS_T)
    for i in range(n):
        rows = slice(i * ROWS_T, (i + 1) * ROWS_T)
        for p in range(HEADS // 2):
            at = p * 128
            q2 = qkv[i, :, at : at + 128]
            k2 = qkv[i, :, D + at : D + at + 128]
            v2 = qkv[i, :, 2 * D + at : 2 * D + at + 128]
            do = datt[rows, at : at + 128]
            probs = pair_probs(q2, k2, keys, low)
            dprobs = nt(apart(v2, low, 0), do).reshape(probs.shape)
            mean = jnp.sum(probs * dprobs, axis=1, keepdims=True)
            dscores = (probs * (dprobs - mean)).astype(bf16).reshape(both)
            dq = nn(apart(k2.T, low_t, 1), dscores)
            dk = nn(dscores, q2)
            dv = nn(probs.astype(bf16).reshape(both), do)
            dqkv[i, :, at : at + 128] = (dq * SCORE_SCALE).T.astype(bf16)
            dk = jnp.where(low, dk[:ROWS_T], dk[ROWS_T:]) * SCORE_SCALE
            dqkv[i, :, D + at : D + at + 128] = dk.astype(bf16)
            dv = jnp.where(low, dv[:ROWS_T], dv[ROWS_T:])
            dqkv[i, :, 2 * D + at : 2 * D + at + 128] = dv.astype(bf16)


def unit_back_kernel(n, vblock, images, *refs):
    (w_in, prm, vgrad_in, hgrad, p0, p1, p2, p3, x0, dqkv_in, dx1_in,
     acc_patch, blocks, vgrad, dx0_all, rows, flat) = refs
    p2 = p2.at[0]
    part = lax.axis_index("cls")
    per = PATCHES // 4

    @pl.when(pl.program_id(0) == 0)
    def _():
        vgrad[...] = vgrad_in[...]

    tokens = n * ROWS_T
    dx1 = dx1_in[...].reshape(tokens, D)
    dqkv = dqkv_in[...].reshape(tokens, 3 * D)
    vgrad[2:3, :] = vgrad[2:3, :] + jnp.sum(dqkv[:, 0:D].astype(f32), axis=0, keepdims=True)
    vgrad[3:4, :] = vgrad[3:4, :] + jnp.sum(dqkv[:, 2 * D : 3 * D].astype(f32), axis=0, keepdims=True)
    unit, inverse = normalize(x0[...].reshape(tokens, D))
    dnormed = nn(dqkv, w_in[...])
    vgrad[0:1, :] = vgrad[0:1, :] + jnp.sum(dnormed * unit, axis=0, keepdims=True)
    vgrad[1:2, :] = vgrad[1:2, :] + jnp.sum(dnormed, axis=0, keepdims=True)
    dx0 = dx1 + normalize_back(unit, inverse, dnormed * prm[0:1, :])
    dx0_all[pl.ds(pl.program_id(0) * n, n)] = dx0.reshape(n, ROWS_T, D)

    @pl.when(pl.program_id(0) == pl.num_programs(0) - 1)
    def _():
        rows[...] = jnp.zeros_like(rows)
        for m in range(images):
            for k in range(4):
                begin = k * PIX_ROWS + m * per
                rows[begin : begin + per, :] = dx0_all[m, k * per : k * per + per, :]
        low = rows[...].astype(bf16)
        total = tn(p0[...], low[:PIX_ROWS])
        for k, piece in ((1, p1), (2, p2), (3, p3)):
            total = total + tn(piece[...], low[k * PIX_ROWS : (k + 1) * PIX_ROWS])
        acc_patch[...] = total
        position = dx0_all[0]
        for m in range(1, images):
            position = position + dx0_all[m]
        flat[...] = jnp.zeros_like(flat)
        for k in range(4):
            for q in range(4):

                @pl.when((part ^ k) == q)
                def _(k=k, q=q):
                    flat[1 + q * per : 1 + q * per + per, :] = position[k * per : k * per + per, :]

        first = position[PATCHES : PATCHES + 1, :]
        flat[0:1, :] = first
        flat[TOK : TOK + 1, :] = jnp.sum(position[0:PATCHES, :], axis=0, keepdims=True)
        flat[TOK + 1 : TOK + 2, :] = vgrad[12:13, :]
        flat[TOK + 2 : TOK + 3, :] = vgrad[13:14, :]
        flat[TOK + 3 : TOK + 4, :] = first
        for q in range(GRID_CLS):
            wide = jnp.concatenate([hgrad[q : q + 1, :], jnp.zeros((1, D - CPAD), f32)], axis=1)
            store_flat(flat, HEAD_AT + q * CPART, wide, CPART)
        for j in range(12):
            store_flat(flat, LAYER_AT + j * D, vgrad[j : j + 1, :], D)
        cut_vector(vblock, flat, blocks)


def qkv_back_kernel(n, prm, x0, dqkv_in, acc_out, acc):
    @pl.when(pl.program_id(0) == 0)
    def _():
        acc[0 : 3 * D, :] = jnp.zeros((3 * D, D), f32)
        acc[3 * D : 4 * D, :] = acc_out[...]

    tokens = n * ROWS_T
    dqkv = dqkv_in[...].reshape(tokens, 3 * D)
    unit, _ = normalize(x0[...].reshape(tokens, D))
    normed = (unit * prm[0:1, :] + prm[1:2, :]).astype(bf16)
    for j in range(3):
        at = slice(j * D, (j + 1) * D)
        acc[at, :] = acc[at, :] + tn(dqkv[:, at], normed)


def block_back_kernel(tuned, acc, acc_patch, blocks, keep, send):
    me = me_of(tuned)
    for s in range(BLOCKS):
        d = s ^ me
        core, place = grad_place(s)
        rows48, rows24 = pl.ds(pl.multiple_of(d * 48, 8), 48), pl.ds(pl.multiple_of(d * 24, 8), 24)
        put_block([acc[rows48, :], acc_patch[rows24, :], blocks[d]], SECTIONS_ONE, keep, send, core, place)


def update_kernel(v0, v1, v2, v3, one, two, vec, *refs):
    ins, (loss_out, norm_out, *outs) = refs[:18], refs[18:]
    sums = (v0[...] + v1[...]) + (v2[...] + v3[...])
    norm = jnp.sqrt(sums[0, 0])
    loss_out[0] = sums[0, 1]
    norm_out[0] = norm
    clip = jnp.minimum(1.0, CLIP_NORM / (norm + 1e-06))
    grads = [
        one[48:72, :],
        one[0:48, :],
        two[32:80, :],
        two[80:128, :],
        unpack_head(two[0:32, :])[:, :CPART],
        vec[...],
    ]
    for j, grad in enumerate(grads):
        news = advance(ins[3 * j][...], ins[3 * j + 1][...], ins[3 * j + 2][...], grad, clip)
        for k in range(3):
            outs[3 * j + k][...] = news[k]


def flip(n, k):
    return [(i, i ^ k) for i in range(n)]


def to_core(v):
    return lax.ppermute(v, "cls", flip(4, 1))


def to_x(v):
    return lax.ppermute(v, "cls", flip(4, 2))


def to_y(v):
    return lax.ppermute(v, "dp", flip(8, 1))


def to_z(v, k):
    return lax.ppermute(v, "dp", flip(8, 2 * k))


def gather_blocks(near, at_x, at_y, corner):
    whole = [w for v in (near, at_x, at_y) for w in (v, to_core(v))]
    return whole + corner + [to_core(v) for v in corner]


def corner_of(at_x, at_y):
    return [to_y(at_x[:2]), to_x(at_y[2:])]


def first_kernel(sections, keep, got, send_a, keep_a, send_b, keep_b):
    encode(keep[0, 0] + decode(got.at[0, 0], sections), sections, send_a.at[0])
    keep_a[0] = keep[1, 0] + decode(got.at[1, 0], sections)
    encode(keep[2, 0] + decode(got.at[2, 0], sections), sections, send_b.at[0])
    keep_b[0] = keep[3, 0] + decode(got.at[3, 0], sections)


def second_kernel(sections, keep_a, keep_b, got_a, got_b, send_a, rest_a, send_b, rest_b):
    for keep, got, send, rest in ((keep_a, got_a, send_a, rest_a), (keep_b, got_b, send_b, rest_b)):
        rest[0] = keep[0, 0] + decode(got.at[0, 0], sections)
        encode(keep[1, 0] + decode(got.at[1, 0], sections), sections, send.at[0])


def third_kernel(sections, keep_a, keep_b, got_a, got_b, own, send_1, send_2, send_3):
    own[...] = keep_a[0] + decode(got_a.at[0], sections)
    encode(keep_a[1] + decode(got_a.at[1], sections), sections, send_1)
    encode(keep_b[0] + decode(got_b.at[0], sections), sections, send_2)
    encode(keep_b[1] + decode(got_b.at[1], sections), sections, send_3)


def third_pair_kernel(sections, keep_a, keep_b, got_a, got_b, rest, send):
    for j, (keep, got) in enumerate(((keep_a, got_a), (keep_b, got_b))):
        rest[j] = keep[0] + decode(got.at[0], sections)
        encode(keep[1] + decode(got.at[1], sections), sections, send.at[j])


def near_kernel(sections, rest, got, own, send):
    own[...] = rest[0] + decode(got.at[0], sections)
    encode(rest[1] + decode(got.at[1], sections), sections, send)


def fourth_kernel(sections, own, *refs):
    *got, before, share, sums = refs
    total = own[...]
    for code in got:
        total = total + decode(code, sections)
    share[...] = total
    lane = lax.broadcasted_iota(i32, (8, 128), 1)
    sums[...] = before[...] + jnp.where(lane == 0, jnp.sum(total * total), 0.0)


def scatter_first(keep, got, sections):
    rows = sections[-1]
    quarters = [pl.BlockSpec((4, 1, r, D), lambda j: (0, j, 0, 0)) for r in (rows, coded(sections))]
    wide, code = pl.BlockSpec((1, rows, D), lambda j: (j, 0, 0)), pl.BlockSpec((1, coded(sections), D), lambda j: (j, 0, 0))
    return pl.pallas_call(
        functools.partial(first_kernel, sections),
        grid=(4,),
        in_specs=quarters,
        out_specs=[code, wide, code, wide],
        out_shape=[sds((4, coded(sections), D), jnp.int16), sds((4, rows, D), f32)] * 2,
        cost_estimate=cost(4),
        compiler_params=params_of(16),
    )(*[v.reshape((4, 4) + v.shape[1:]) for v in (keep, got)])


def scatter_second(keep_a, keep_b, got_a, got_b, sections):
    rows = sections[-1]
    pairs, codes = [pl.BlockSpec((2, 1, r, D), lambda j: (0, j, 0, 0)) for r in (rows, coded(sections))]
    wide, code = [pl.BlockSpec((1, r, D), lambda j: (j, 0, 0)) for r in (rows, coded(sections))]
    return pl.pallas_call(
        functools.partial(second_kernel, sections),
        grid=(2,),
        in_specs=[pairs] * 2 + [codes] * 2,
        out_specs=[code, wide, code, wide],
        out_shape=[sds((2, coded(sections), D), jnp.int16), sds((2, rows, D), f32)] * 2,
        cost_estimate=cost(2),
        compiler_params=params_of(16),
    )(*[v.reshape((2, 2) + v.shape[1:]) for v in (keep_a, keep_b, got_a, got_b)])


def scatter_third(keep_a, keep_b, got_a, got_b, sections):
    rows = sections[-1]
    return pl.pallas_call(
        functools.partial(third_kernel, sections),
        out_shape=[sds((rows, D), f32)] + [sds((coded(sections), D), jnp.int16)] * 3,
        cost_estimate=cost(2),
        compiler_params=params_of(16),
    )(keep_a, keep_b, got_a, got_b)


def scatter_third_pair(keep_a, keep_b, got_a, got_b, sections):
    rows = sections[-1]
    return pl.pallas_call(
        functools.partial(third_pair_kernel, sections),
        out_shape=[sds((2, rows, D), f32), sds((2, coded(sections), D), jnp.int16)],
        compiler_params=params_of(16),
    )(keep_a, keep_b, got_a, got_b)


def scatter_near(rest, got, sections):
    rows = sections[-1]
    return pl.pallas_call(
        functools.partial(near_kernel, sections),
        out_shape=[sds((rows, D), f32), sds((coded(sections), D), jnp.int16)],
        compiler_params=params_of(16),
    )(rest, got)


def scatter_fourth(own, got, sections, before):
    return pl.pallas_call(
        functools.partial(fourth_kernel, sections),
        out_shape=[sds(own.shape, f32), sds((8, 128), f32)],
        cost_estimate=cost(2),
        compiler_params=params_of(16),
    )(own, *got, before)


def sums_along_z(v):
    v = v + to_core(v)
    v = (v + to_x(v)) + (to_y(v) + lax.ppermute(v, ("dp", "cls"), flip(BLOCKS, GRID_CLS + 2)))
    return [v] + [to_z(v, k) for k in (1, 2, 3)]


def plain_gather(masters, vblock):
    patch, attention, up, down, head, vector = [w.astype(bf16) for w in masters]
    both = ("dp", "cls")
    patch = lax.all_gather(patch, both, axis=0, tiled=True).reshape(BLOCKS, 24, D)
    attention = lax.all_gather(attention, both, axis=2, tiled=True)[0].T.reshape(BLOCKS, 48, D)
    vector = lax.all_gather(vector, both, axis=0, tiled=True).reshape(BLOCKS, vblock)
    vector = jnp.pad(vector, ((0, 0), (0, 8 * D - vblock))).reshape(BLOCKS, 8, D)
    up = lax.all_gather(lax.all_gather(up, "dp", axis=1, tiled=True), "cls", axis=2, tiled=True)[0]
    down = lax.all_gather(lax.all_gather(down, "dp", axis=2, tiled=True), "cls", axis=1, tiled=True)[0].T
    head = lax.all_gather(lax.all_gather(head, "dp", axis=0, tiled=True), "cls", axis=1, tiled=True)
    up, down = [
        w.reshape(GRID_DP, 48, GRID_CLS, D).transpose(0, 2, 1, 3).reshape(BLOCKS, 48, D) for w in (up, down)
    ]
    head = head.reshape(GRID_DP, 48, GRID_CLS, CPART).transpose(0, 2, 1, 3).reshape(BLOCKS, 48, CPART)
    head = pack_head(jnp.pad(head, ((0, 0), (0, 0), (0, CPAD - CPART))))
    one = jnp.concatenate([attention, patch, vector], axis=1).reshape(4, 8, R_ONE, D)
    two = jnp.concatenate([head, up, down], axis=1).reshape(4, 8, R_TWO, D)
    return [one[:, a] for a in range(8)], [two[:, a] for a in range(8)]


def plain_scatter(one, two, vblock):
    def in_order(keep, send, sections):
        send = [decode(send[j], sections) for j in range(16)]
        return jnp.stack([(keep, send)[grad_place(s)[0]][grad_place(s)[1]] for s in range(BLOCKS)])

    one, two = in_order(*one, SECTIONS_ONE), in_order(*two, SECTIONS_TWO)
    both = ("dp", "cls")
    attention = one[:, 0:48].reshape(4 * D, D).T[None]
    patch = one[:, 48:72].reshape(PD, D)
    vector = one[:, 72:80].reshape(BLOCKS, 8 * D)[:, :vblock].reshape(-1)
    up, down = [
        w.reshape(GRID_DP, GRID_CLS, 48, D).transpose(0, 2, 1, 3).reshape(D, FF)
        for w in (two[:, 32:80], two[:, 80:128])
    ]
    head = unpack_head(two[:, 0:32])[:, :, :CPART]
    head = head.reshape(GRID_DP, GRID_CLS, 48, CPART).transpose(0, 2, 1, 3).reshape(D, C)

    def split(v, at_dp, at_cls):
        v = lax.psum_scatter(v, "dp", scatter_dimension=at_dp, tiled=True)
        return lax.psum_scatter(v, "cls", scatter_dimension=at_cls, tiled=True)

    return (
        lax.psum_scatter(patch, both, scatter_dimension=0, tiled=True),
        lax.psum_scatter(attention, both, scatter_dimension=2, tiled=True),
        split(up, 0, 1)[None],
        split(down.T, 1, 0)[None],
        split(head, 0, 1),
        lax.psum_scatter(vector, both, scatter_dimension=0, tiled=True),
    )


def take_rows_kernel(rows, source, out, sem):
    def one(i, carry):
        copy = pltpu.make_async_copy(source.at[rows[i]], out.at[i], sem)
        copy.start()
        copy.wait()
        return carry

    lax.fori_loop(0, out.shape[0], one, 0)


def take_rows(source, rows):
    return pl.pallas_call(
        take_rows_kernel,
        out_shape=sds((rows.shape[0],) + source.shape[1:], source.dtype),
        in_specs=[SMEM, ANY],
        out_specs=ANY,
        scratch_shapes=[pltpu.SemaphoreType.DMA(())],
    )(rows, source)


def pick_small(source, rows):
    hot = (rows[:, None] == jnp.arange(source.shape[0])[None, :]).astype(f32)
    return jnp.dot(hot, source.astype(f32), precision=lax.Precision.HIGHEST)


def plain_replay(buffer_patches, buffer_logits, buffer_labels, replay_owner, replay_row, kind_rows):
    dp_count, dp_index = lax.axis_size("dp"), lax.axis_index("dp")
    replay_count = 2 * kind_rows
    capacity = max(2, -(-replay_count // dp_count))
    table = lax.all_gather(buffer_labels, "dp", axis=0, tiled=True)
    owners = replay_owner[:, 0].reshape(dp_count, replay_count)
    local_rows = replay_row.reshape(dp_count, replay_count)
    earlier = jnp.arange(replay_count)[None, :] < jnp.arange(replay_count)[:, None]
    same_owner = owners[:, :, None] == owners[:, None, :]
    ranks = jnp.sum(jnp.where(same_owner & earlier[None], 1, 0), axis=2).astype(i32)
    slot_ids = jnp.arange(capacity, dtype=i32)
    wanted = (owners == dp_index)[:, :, None] & (ranks[:, :, None] == slot_ids[None, None, :])
    slot_rows = jnp.sum(jnp.where(wanted, local_rows[:, :, None], 0), axis=1).reshape(-1)
    pixels = take_rows(buffer_patches, slot_rows)
    logits = pick_small(buffer_logits, slot_rows).astype(bf16)
    pixels = lax.all_to_all(pixels, "dp", split_axis=0, concat_axis=0, tiled=True)
    logits = lax.all_to_all(logits, "dp", split_axis=0, concat_axis=0, tiled=True)
    my_owners, my_ranks, my_rows = [
        lax.dynamic_index_in_dim(v, dp_index, 0, keepdims=False) for v in (owners, ranks, local_rows)
    ]
    places = my_owners * buffer_labels.shape[0] + my_rows
    labels = jnp.sum(jnp.where(places[:, None] == jnp.arange(table.shape[0])[None, :], table[None, :], 0), axis=1)
    return pixels, logits, labels.astype(i32), (my_owners * capacity + my_ranks).astype(i32)


def on_device(
    current_patches,
    current_labels,
    buffer_patches,
    buffer_logits,
    buffer_labels,
    replay_owner,
    replay_row,
    seen_mask,
    patch_weight,
    patch_moment,
    patch_average,
    attention_weight,
    attention_moment,
    attention_average,
    up_weight,
    up_moment,
    up_average,
    down_weight,
    down_moment,
    down_average,
    head_weight,
    head_moment,
    head_average,
    vector_weight,
    vector_moment,
    vector_average,
):
    dp_count, cls_count = lax.axis_size("dp"), lax.axis_size("cls")
    dp_index, cls_index = lax.axis_index("dp"), lax.axis_index("cls")
    kind_rows = current_patches.shape[0]
    replay_count = 2 * kind_rows
    group_rows = 3 * kind_rows
    normal_count = kind_rows * dp_count
    patch_part = current_patches.shape[1]
    cur_own, rep_own = kind_rows // cls_count, replay_count // cls_count
    images = cur_own + rep_own
    class_part = head_weight.shape[1]
    vblock = vector_weight.shape[0] * dp_count * cls_count // BLOCKS
    tuned = dp_count == GRID_DP and cls_count == GRID_CLS and replay_count == 2 * dp_count
    masters = (patch_weight, attention_weight, up_weight, down_weight, head_weight, vector_weight)
    moments = (patch_moment, attention_moment, up_moment, down_moment, head_moment, vector_moment)
    averages = (patch_average, attention_average, up_average, down_average, head_average, vector_average)

    def views(v, j):
        return v[0].T if j in (1, 3) else v[0] if j == 2 else v

    current_view, buffer_view = current_patches.transpose(1, 0, 2), buffer_patches.transpose(1, 0, 2)
    if tuned:
        pack = pl.pallas_call(
            pack_weights_kernel,
            out_shape=sds((R_ONE + R_TWO + R_MASK, D), bf16),
            cost_estimate=cost(2),
            compiler_params=params_of(60),
        )

    def exchange(sent):
        own, near, far = sent
        far = lax.ppermute(far, "cls", flip(4, 2))
        return [own, lax.ppermute(near, "cls", flip(4, 1)), far, lax.ppermute(far[1], "cls", flip(4, 1))]

    def pick(find, stored, *operands):
        out_shape = [sds((PIX_ROWS, PD), bf16)] * 2 + [sds((2, PIX_ROWS, PD), bf16)]
        return pl.pallas_call(
            functools.partial(pick_kernel, cur_own, rep_own, find),
            out_shape=out_shape + ([sds((3, 8), i32)] if find else []),
            in_specs=[SMEM] * (4 if find else 1) + [ANY, ANY, VMEM],
            out_specs=[VMEM] * 3 + ([SMEM] if find else []),
            scratch_shapes=[
                pltpu.VMEM((patch_part, stored, PD), bf16),
                pltpu.VMEM((patch_part, kind_rows, PD), bf16),
                pltpu.VMEM((PD // 128, patch_part * stored, 128), f32),
                pltpu.VMEM((PD // 128, patch_part * kind_rows, 128), f32),
                pltpu.VMEM((stored, CPAD), f32),
                pltpu.VMEM((PIX_ROWS, PD), f32),
                pltpu.SMEM((replay_count,), i32),
                pltpu.SemaphoreType.DMA((patch_part // 7 + 1,)),
            ],
            cost_estimate=cost(7),
            compiler_params=params_of(60),
        )(*operands)

    if tuned:
        *sent, meta = pick(
            True,
            buffer_patches.shape[0],
            replay_owner.reshape(-1),
            replay_row,
            current_labels,
            buffer_labels,
            current_view,
            buffer_view,
            buffer_logits,
        )
        got = exchange(sent)
        got[1], vec = lax.optimization_barrier((got[1], vector_weight))
        vec = jnp.pad(vec, (0, 8 * D - vblock)).reshape(8, D)
        packed = pack(
            views(attention_weight, 1), patch_weight, vec, views(up_weight, 2), views(down_weight, 3), head_weight, seen_mask
        )
    else:
        moved, logits, labels, places = plain_replay(
            buffer_patches, buffer_logits, buffer_labels, replay_owner, replay_row, kind_rows
        )
        sent = pick(False, moved.shape[0], places, current_view, moved.transpose(1, 0, 2), logits)
        got = exchange(sent)
        row_mask = jnp.pad(seen_mask.astype(bf16), ((0, 0), (0, CPAD - class_part)))
        row_mask = lax.all_gather(row_mask, "cls").astype(f32)
        mask_rows = [
            lax.dynamic_slice_in_dim(row_mask, cls_index * cur_own, cur_own, 1),
            lax.dynamic_slice_in_dim(row_mask, kind_rows + cls_index * rep_own, rep_own, 1),
            jnp.zeros((cls_count, 8 - images, CPAD), f32),
        ]
        given = jnp.concatenate(mask_rows, axis=1)
        kinds = jnp.where(jnp.arange(replay_count) < kind_rows, 1, 2).astype(i32)
        labels = jnp.where(kinds == 1, 0, labels)

        def own(current, replayed, fill):
            return jnp.concatenate(
                [
                    lax.dynamic_slice_in_dim(current, cls_index * cur_own, cur_own, 0),
                    lax.dynamic_slice_in_dim(replayed, cls_index * rep_own, rep_own, 0),
                    jnp.full((8 - images,), fill, i32),
                ]
            )

        nothing = jnp.zeros_like(current_labels)
        meta = jnp.stack([own(current_labels, labels, 0), own(nothing, kinds, 3), jnp.zeros((8,), i32)])

    if tuned:
        column = [packed] + [to_z(packed, k) for k in (1, 2, 3)]
        near_one = jnp.stack([v[:R_ONE] for v in column])
        near_two = jnp.stack([v[R_ONE:] for v in column])
        near_one, got[2] = lax.optimization_barrier((near_one, got[2]))
        at_x, at_y = to_x(near_one), to_y(near_one)
        at_x, near_two = lax.optimization_barrier((at_x, near_two))
        at_x, at_y, corner = lax.optimization_barrier((at_x, at_y, corner_of(at_x, at_y)))
        one = gather_blocks(near_one, at_x, at_y, corner)
        two_x, two_y = to_x(near_two), to_y(near_two)
    else:
        one, two = plain_gather(masters, vblock)
        two = [jnp.pad(v, ((0, 0), (0, R_MASK), (0, 0))) for v in two]
        one, two = [w[:6] + [v[half : half + 2] for v in w[6:] for half in (0, 2)] for w in (one, two)]

    n = 2
    steps = images // n
    whole = lambda shape: pl.BlockSpec(shape, lambda i: (0,) * len(shape))
    per = lambda width: pl.BlockSpec((n, ROWS_T, width), lambda i: (i, 0, 0))
    pieces = [whole((PIX_ROWS, PD))] * 2 + [pl.BlockSpec((1, PIX_ROWS, PD), lambda i: (0, 0, 0)), whole((PIX_ROWS, PD))]
    x0, qkv, attn, prm, hb, soft = pl.pallas_call(
        functools.partial(embed_kernel, tuned, vblock, n, images),
        grid=(steps,),
        in_specs=[whole((4, R_ONE, D))] * 6 + [whole((2, R_ONE, D))] * 4 + pieces,
        out_specs=[per(D), per(3 * D)] + [whole(shape) for shape in ((4 * D, D), (16, D), (8, CPAD), (4, 8, CPAD))],
        out_shape=[
            sds((images, ROWS_T, D), f32),
            sds((images, ROWS_T, 3 * D), bf16),
            sds((4 * D, D), bf16),
            sds((16, D), f32),
            sds((8, CPAD), f32),
            sds((4, 8, CPAD), f32),
        ],
        scratch_shapes=[
            pltpu.VMEM((PD, D), f32),
            pltpu.VMEM((PD, D), bf16),
            pltpu.VMEM((BLOCKS, 8, D), f32),
            pltpu.VMEM((V_ROWS, D), f32),
            pltpu.VMEM((ROWS_T, D), f32),
            pltpu.VMEM((4 * PIX_ROWS, D), f32),
            pltpu.VMEM((images, ROWS_T, D), f32),
        ],
        cost_estimate=cost(8),
        compiler_params=params_of(34),
    )(*one, *got)
    if tuned:
        two_x, two_y, hb = lax.optimization_barrier((two_x, two_y, hb))
        corner = corner_of(two_x, two_y)
    out_part = pl.BlockSpec((D, D), lambda i: (3, 0))
    half = lambda width: pl.BlockSpec((images // 2, ROWS_T, width), lambda i: (i, 0, 0))
    att, x1 = pl.pallas_call(
        functools.partial(attend_kernel, images // 2),
        grid=(2,),
        in_specs=[out_part, whole((16, D)), half(D), half(3 * D)],
        out_specs=[half(D), half(D)],
        out_shape=[sds((images, ROWS_T, D), bf16), sds((images, ROWS_T, D), f32)],
        cost_estimate=cost(10),
        compiler_params=params_of(24),
    )(attn, prm, x0, qkv)

    if tuned:
        corner, x1 = lax.optimization_barrier((corner, x1))
        two = gather_blocks(near_two, two_x, two_y, corner)

    scales = (1.0 / normal_count, LABEL_WEIGHT / normal_count, LOGIT_WEIGHT / (normal_count * C))
    dx1, keep_two, send_two, vgrad, hgrad, loss = run_middle(
        tuned, images // 2, images, scales, *([] if tuned else [given]), *two, prm, hb, soft, meta, x1
    )

    def attend_back(first, *operands):
        begin, count = (0, 1) if first else (1, steps - 1)
        some = lambda width: pl.BlockSpec((n, ROWS_T, width), lambda i: (i + begin, 0, 0))
        return pl.pallas_call(
            functools.partial(attend_back_kernel, n, first),
            grid=(count,),
            in_specs=[out_part, whole((16, D)), some(3 * D), some(D), some(D)] + ([] if first else [whole((D, D)), ANY]),
            out_specs=[some(3 * D), whole((D, D)), whole((16, D))],
            out_shape=[sds((images, ROWS_T, 3 * D), bf16), sds((D, D), f32), sds((16, D), f32)],
            input_output_aliases={} if first else {6: 0},
            cost_estimate=cost(6 * count),
            compiler_params=params_of(22),
        )(*operands)

    dqkv, acc_out, vgrad = attend_back(True, attn, vgrad, qkv, att, dx1)
    if tuned:
        a_code, a_keep, b_code, b_keep = scatter_first(keep_two, to_core(send_two), SECTIONS_TWO)
        a_code, b_code, vgrad = lax.optimization_barrier((a_code, b_code, vgrad))
        moving = (to_x(a_code), to_y(b_code))
    dqkv, acc_out, vgrad = attend_back(False, attn, vgrad, qkv, att, dx1, acc_out, dqkv)
    acc = pl.pallas_call(
        functools.partial(qkv_back_kernel, n),
        grid=(steps,),
        in_specs=[whole((16, D)), per(D), per(3 * D), whole((D, D))],
        out_specs=whole((4 * D, D)),
        out_shape=sds((4 * D, D), f32),
        cost_estimate=cost(6),
        compiler_params=params_of(22),
    )(prm, x0, dqkv, acc_out)
    if tuned:
        acc, a_keep = lax.optimization_barrier((acc, a_keep))
        a_code, a_rest, b_code, b_rest = scatter_second(a_keep, b_keep, *moving, SECTIONS_TWO)
        a_code, b_code, vgrad = lax.optimization_barrier((a_code, b_code, vgrad))
        moving = (to_y(a_code), to_x(b_code))
    acc_patch, blocks = pl.pallas_call(
        functools.partial(unit_back_kernel, n, vblock, images),
        grid=(steps,),
        in_specs=[whole((3 * D, D)), whole((16, D)), whole((16, D)), whole((8, CPAD))]
        + pieces
        + [per(D), per(3 * D), per(D)],
        out_specs=[whole((PD, D)), whole((BLOCKS, 8, D))],
        out_shape=[sds((PD, D), f32), sds((BLOCKS, 8, D), f32)],
        scratch_shapes=[
            pltpu.VMEM((16, D), f32),
            pltpu.VMEM((images, ROWS_T, D), f32),
            pltpu.VMEM((4 * PIX_ROWS, D), f32),
            pltpu.VMEM((V_ROWS, D), f32),
        ],
        cost_estimate=cost(6),
        compiler_params=params_of(28),
    )(attn, prm, vgrad, hgrad, *got, x0, dqkv, dx1)
    if tuned:
        rest_two, code_two = scatter_third_pair(a_rest, b_rest, *moving, SECTIONS_TWO)
        code_two, blocks = lax.optimization_barrier((code_two, blocks))
    keep_one, send_one = pl.pallas_call(
        functools.partial(block_back_kernel, tuned),
        out_shape=[sds((16, R_ONE, D), f32), sds((16, coded(SECTIONS_ONE), D), jnp.int16)],
        cost_estimate=cost(2),
        compiler_params=params_of(20),
    )(acc, acc_patch, blocks)

    if tuned:
        a_code, a_keep, b_code, b_keep = scatter_first(keep_one, to_core(send_one), SECTIONS_ONE)
        code_two, a_code, b_code = lax.optimization_barrier((code_two, a_code, b_code))
        moving = (to_x(a_code), to_y(b_code))
        own_two, code_two = scatter_near(rest_two, to_z(code_two, 1), SECTIONS_TWO)
        code_two, a_keep = lax.optimization_barrier((code_two, a_keep))
        a_code, a_rest, b_code, b_rest = scatter_second(a_keep, b_keep, *moving, SECTIONS_ONE)
        code_two, a_code, b_code = lax.optimization_barrier((code_two, a_code, b_code))
        moving = (to_y(a_code), to_x(b_code))
        share_two, sums = scatter_fourth(own_two, [to_z(code_two, 2)], SECTIONS_TWO, loss)
        own_one, *codes_one = scatter_third(a_rest, b_rest, *moving, SECTIONS_ONE)
        last_one = [to_z(code, k + 1) for k, code in enumerate(codes_one)]
        share_one, sums = scatter_fourth(own_one, last_one, SECTIONS_ONE, sums)
    else:
        shares = plain_scatter((keep_one, send_one), (keep_two, send_two), vblock)
        squares = sum(jnp.sum(share * share) for share in shares)
        sums = loss + jnp.where(lax.broadcasted_iota(i32, (8, 128), 1) == 0, squares, 0.0)
    if tuned:
        states = [views(v, j) for j in range(6) for v in (masters[j], moments[j], averages[j])]
        vector_share = share_one[72:80].reshape(-1)[:vblock]
        loss, norm_value, *news = pl.pallas_call(
            update_kernel,
            out_shape=[sds((1,), f32)] * 2 + [sds(v.shape, f32) for v in states],
            in_specs=[VMEM] * 25,
            out_specs=[SMEM] * 2 + [VMEM] * 18,
            compiler_params=params_of(24),
        )(*sums_along_z(sums), share_one, share_two, vector_share, *states)
        results = [loss.reshape(()), norm_value.reshape(())]
        for j in range(18):
            results.append(news[j].T[None] if j // 3 in (1, 3) else news[j][None] if j // 3 == 2 else news[j])
    else:
        sums = lax.psum(sums, ("dp", "cls"))
        norm_value = jnp.sqrt(sums[0, 0])
        clip_factor = jnp.minimum(1.0, CLIP_NORM / (norm_value + 1e-06))
        results = [sums[0, 1], norm_value]
        for weight, moment, average, share in zip(masters, moments, averages, shares):
            results += list(advance(weight, moment, average, share, clip_factor))
    return tuple(results)


def solution(mesh):
    split_rows, split_columns = P(("dp", "cls"), None), P(None, None, ("dp", "cls"))
    states = (
        [split_rows] * 3
        + [split_columns] * 3
        + [P(None, "dp", "cls")] * 3
        + [P(None, "cls", "dp")] * 3
        + [P("dp", "cls")] * 3
        + [P(("dp", "cls"))] * 3
    )
    in_specs = (
        P("dp", "cls", None),
        P("dp"),
        P("dp", "cls", None),
        P("dp", "cls"),
        P("dp"),
        P(),
        P(),
        P("dp", "cls"),
        *states,
    )
    out_specs = (P(), P(), *states)
    return jax.shard_map(on_device, mesh=mesh, in_specs=in_specs, out_specs=out_specs, check_vma=False)
```

```python
import functools
import math

import jax
import jax.numpy as jnp
from jax import lax
from jax.experimental import pallas as pl
from jax.experimental.pallas import tpu as pltpu
from jax.sharding import PartitionSpec as P

D = 384
HEADS = 6
HD = 64
FF = 1536
C = 1000
PD = 768
TOK = 197
PATCHES = 196
PARAMS = 2531176

NORM_EPS = 1e-06
SCORE_SCALE = 0.125
LOGIT_WEIGHT = 0.3
LABEL_WEIGHT = 0.8
MOMENTUM_DECAY = 0.9
AVERAGE_KEEP = 0.75
CLIP_NORM = 0.005
RATE = 0.03 * math.sqrt(PARAMS) / CLIP_NORM

ROWS_T = 208
GRID_DP, GRID_CLS = 8, 4
BLOCKS = GRID_DP * GRID_CLS
CPART = C // GRID_CLS
CPAD = 256
F_CHUNK = 512
R_ONE = 80
R_TWO = 128
R_MASK = 16
PIX_ROWS = 304
V_ROWS = 232
HEAD_AT = (TOK + 4) * D
LAYER_AT = HEAD_AT + C

bf16 = jnp.bfloat16
f32 = jnp.float32
i32 = jnp.int32

ANY = pl.BlockSpec(memory_space=pl.ANY)
VMEM = pl.BlockSpec(memory_space=pltpu.VMEM)
SMEM = pl.BlockSpec(memory_space=pltpu.SMEM)


def sds(shape, dtype):
    return jax.ShapeDtypeStruct(shape, dtype)


def cost(micros):
    return pl.CostEstimate(flops=int(micros * 1e8), bytes_accessed=1 << 20, transcendentals=0)


def params_of(limit_mib, **more):
    return pltpu.CompilerParams(vmem_limit_bytes=limit_mib << 20, **more)


def nn(a, b):
    return lax.dot_general(a, b, (((1,), (0,)), ((), ())), preferred_element_type=f32)


def nt(a, b):
    return lax.dot_general(a, b, (((1,), (1,)), ((), ())), preferred_element_type=f32)


def tn(a, b):
    return lax.dot_general(a, b, (((0,), (0,)), ((), ())), preferred_element_type=f32)


def gelu_parts(values):
    bell = jnp.exp(-0.5 * values * values)
    t = 1.0 / (1.0 + (0.3275911 * 0.5**0.5) * jnp.abs(values))
    tail = 0.5 * 1.061405429 * t - 0.5 * 1.453152027
    tail = tail * t + 0.5 * 1.421413741
    tail = tail * t - 0.5 * 0.284496736
    tail = (tail * t + 0.5 * 0.254829592) * t * bell
    return jnp.where(values < 0.0, tail, 1.0 - tail), bell * (1.0 / math.sqrt(2.0 * math.pi))


def normalize(values):
    centred = values - jnp.mean(values, axis=-1, keepdims=True)
    inverse = lax.rsqrt(jnp.mean(centred * centred, axis=-1, keepdims=True) + NORM_EPS)
    return (centred * inverse, inverse)


def normalize_back(unit, inverse, grad_unit):
    return inverse * (
        grad_unit
        - jnp.mean(grad_unit, axis=-1, keepdims=True)
        - unit * jnp.mean(grad_unit * unit, axis=-1, keepdims=True)
    )


def advance(weight, moment, average, grad, clip_factor):
    clipped = clip_factor * grad
    moment_new = MOMENTUM_DECAY * moment + clipped
    weight_new = weight - RATE * (clipped + MOMENTUM_DECAY * moment_new)
    average_new = AVERAGE_KEEP * average + (1.0 - AVERAGE_KEEP) * weight_new
    return (weight_new, moment_new, average_new)


def pack_head(block):
    a, b, c = block[..., :16, :], block[..., 16:32, :], block[..., 32:, :]
    top = jnp.concatenate([a, b[..., :128]], axis=-1)
    low = jnp.concatenate([b[..., 128:], c], axis=-1)
    return jnp.concatenate([top, low], axis=-2)


def unpack_head(block):
    top, low = block[..., :16, :], block[..., 16:, :]
    b = jnp.concatenate([top[..., 256:], low[..., :128]], axis=-1)
    return jnp.concatenate([top[..., :256], b, low[..., 128:]], axis=-2)


def me_of(tuned):
    if tuned:
        return lax.axis_index("dp") * GRID_CLS + lax.axis_index("cls")
    return 0


def grad_place(s):
    core, x, y, z = s & 1, (s >> 1) & 1, (s >> 2) & 1, s >> 3
    if z < 2:
        return core, (0 if x else 4) + 2 * y + z
    return core, (8 if y else 12) + 2 * x + (z - 2)


R_CODE = 16
SECTIONS_ONE = (0, 48, 72, 80)
SECTIONS_TWO = (0, 32, 80, 128)
SECTIONS_ATTENTION, SECTIONS_REST = (0, 48), (0, 24, 32)


def coded(sections):
    return sections[-1] + (R_CODE if sections in (SECTIONS_TWO, SECTIONS_ATTENTION) else 0)


def thrice(row):
    return jnp.concatenate([row] * 3, axis=1)


def to_code(values):
    return jnp.clip(values, -32767.0, 32767.0).astype(i32).astype(jnp.int16)


def encode(block, sections, out):
    rows = sections[-1]
    inside = coded(sections) == rows
    powers = []
    for j, (a, b) in enumerate(zip(sections[:-1], sections[1:])):
        part = block[j] if isinstance(block, list) else block[a:b]
        most = jnp.max(jnp.abs(part), axis=0, keepdims=True)
        if inside:
            most = jnp.maximum(jnp.maximum(most[:, :128], most[:, 128:256]), most[:, 256:])
        power = jnp.clip(jnp.ceil(jnp.log2(jnp.maximum(most, 1e-30))), -99.0, 126.0)
        powers.append(power)
        code = jnp.round(part * jnp.exp2(15.0 - (thrice(power) if inside else power)))
        if inside and b == rows:
            last = lax.broadcasted_iota(i32, code.shape, 0) == code.shape[0] - 1
            spare = [jnp.zeros_like(power)] * (3 - len(powers))
            code = jnp.where(last, jnp.concatenate(powers + spare, axis=1), code)
        out[a:b, :] = to_code(code)
    if not inside:
        powers.append(jnp.zeros((R_CODE - len(powers), D), f32))
        out[rows : rows + R_CODE, :] = to_code(jnp.concatenate(powers, axis=0))


def put_block(parts, sections, keep, send, core, place):
    if core:
        encode(parts, sections, send.at[place])
    else:
        for part, a, b in zip(parts, sections[:-1], sections[1:]):
            keep[place, a:b, :] = part


def decode(code, sections):
    rows = sections[-1]
    parts = [code[a:b, :].astype(i32).astype(f32) for a, b in zip(sections[:-1], sections[1:])]
    if coded(sections) == rows:
        row = parts[-1][-1:]
        powers = [thrice(row[:, j * 128 : (j + 1) * 128]) for j in range(len(parts))]
        last = lax.broadcasted_iota(i32, parts[-1].shape, 0) == parts[-1].shape[0] - 1
        parts[-1] = jnp.where(last, 0.0, parts[-1])
    else:
        rest = code[rows : rows + R_CODE, :].astype(i32).astype(f32)
        powers = [rest[j : j + 1] for j in range(len(parts))]
    return jnp.concatenate([part * jnp.exp2(power - 15.0) for part, power in zip(parts, powers)], axis=0)


def pack_mask(block):
    a, b, c = block[:8], block[8:16], block[16:]
    top = jnp.concatenate([a, b[:, :128]], axis=1)
    return jnp.concatenate([top, jnp.concatenate([b[:, 128:], c], axis=1)], axis=0)


def unpack_mask(block):
    top, low = block[:8], block[8:]
    b = jnp.concatenate([top[:, 256:], low[:, :128]], axis=1)
    return jnp.concatenate([top[:, :256], b, low[:, 128:]], axis=0)


def pack_weights_kernel(attn, patch, vec, up, down, head, seen, out):
    one, two = out.at[0:R_ONE], out.at[R_ONE:]
    one[0:48, :] = attn[...].astype(bf16)
    one[48:80, :] = jnp.concatenate([patch[...], vec[...]], axis=0).astype(bf16)
    block = jnp.concatenate([head[...], jnp.zeros((48, CPAD - CPART), f32)], axis=1)
    two[0:32, :] = pack_head(block).astype(bf16)
    two[32:80, :] = up[...].astype(bf16)
    two[80:128, :] = down[...].astype(bf16)
    mask = jnp.concatenate([seen[...].astype(f32), jnp.zeros((seen.shape[0], CPAD - CPART), f32)], axis=1)
    two[128:144, :] = pack_mask(mask).astype(bf16)


def pick_kernel(cur_own, rep_own, find, *refs):
    if find:
        owner, row, cur_labels, buf_labels, cur, buf, logits, o0, o1, far, meta, *scratch = refs
    else:
        row, cur, buf, logits, o0, o1, far, *scratch = refs
    stage, stage_cur, wide, wide_cur, soft, res, slots, sems = scratch
    parts, stored, _ = stage.shape
    kind = stage_cur.shape[1]
    chunk = 7
    copies = [pltpu.make_async_copy(cur, stage_cur, sems.at[parts // chunk])]
    for j in range(parts // chunk):
        part = pl.ds(j * chunk, chunk)
        copies.append(pltpu.make_async_copy(buf.at[part], stage.at[part], sems.at[j]))
    for copy in copies:
        copy.start()
    me = lax.axis_index("cls")
    if find:
        mine = lax.axis_index("dp")

        def look(i, count):
            hit = owner[i] == mine

            @pl.when(hit)
            def _():
                slots[count] = i

            return count + jnp.where(hit, 1, 0)

        lax.fori_loop(0, owner.shape[0], look, 0)
        for m in range(8):
            if m < cur_own:
                meta[0, m] = cur_labels[me * cur_own + m]
                meta[1, m] = 0
                meta[2, m] = mine * 3 * kind + me * cur_own + m
            elif m < cur_own + rep_own:
                i = slots[me * rep_own + m - cur_own]
                at = lax.rem(i, 2 * kind)
                meta[0, m] = jnp.where(at < kind, 0, buf_labels[row[i]])
                meta[1, m] = jnp.where(at < kind, 1, 2)
                meta[2, m] = lax.div(i, 2 * kind) * 3 * kind + kind + at
            else:
                meta[0, m] = 0
                meta[1, m] = 3
                meta[2, m] = 0
    else:
        for k in range(4 * rep_own):
            slots[k] = k
    soft[...] = jnp.zeros_like(soft)
    soft[:, :CPART] = logits[...].astype(f32)
    for j, copy in enumerate(copies):
        copy.wait()
        for lanes in range(PD // 128):
            at = slice(lanes * 128, (lanes + 1) * 128)
            if j == 0:
                wide_cur[lanes] = stage_cur[:, :, at].astype(f32).reshape(parts * kind, 128)
            else:
                one = stage[(j - 1) * chunk : j * chunk, :, at].astype(f32).reshape(chunk * stored, 128)
                wide[lanes, (j - 1) * chunk * stored : j * chunk * stored, :] = one
    images = cur_own + rep_own
    res[images * parts :, :] = jnp.zeros((PIX_ROWS - images * parts, PD), f32)
    for k, out in enumerate((o0, o1, far.at[0], far.at[1])):
        to = me ^ k
        for m in range(images):
            if m >= cur_own:
                r = row[slots[to * rep_own + m - cur_own]]
                at = (m % 3) * CPAD
                res[images * parts + m // 3 : images * parts + m // 3 + 1, at : at + CPAD] = soft[pl.ds(r, 1), :]
            for lanes in range(PD // 128):
                if m < cur_own:
                    one = wide_cur[lanes, pl.ds(to * cur_own + m, parts, stride=kind), :]
                else:
                    one = wide[lanes, pl.ds(r, parts, stride=stored), :]
                res[m * parts : (m + 1) * parts, lanes * 128 : (lanes + 1) * 128] = one
        out[...] = res[...].astype(bf16)


def spread_vector(vblock, blocks, flat):
    flat[...] = jnp.zeros_like(flat)
    lane = lax.broadcasted_iota(i32, (8, D), 1)
    for d in range(BLOCKS):
        q, s = divmod(vblock * d, D)
        b = blocks[d]
        if s:
            b = pltpu.roll(b, s, 1)
        flat[q : q + 8, :] = flat[q : q + 8, :] + jnp.where(lane >= s, b, 0.0)
        if s:
            flat[q + 1 : q + 9, :] = flat[q + 1 : q + 9, :] + jnp.where(lane < s, b, 0.0)


def cut_vector(vblock, flat, blocks):
    lane = lax.broadcasted_iota(i32, (8, D), 1)
    place = lax.broadcasted_iota(i32, (8, D), 0) * D + lane
    for d in range(BLOCKS):
        q, s = divmod(vblock * d, D)
        b = flat[q : q + 8, :]
        if s:
            a = pltpu.roll(b, D - s, 1)
            b = pltpu.roll(flat[q + 1 : q + 9, :], D - s, 1)
            b = jnp.where(lane < D - s, a, b)
        blocks[d] = jnp.where(place < vblock, b, 0.0)


def layer_vectors(flat):
    row, s = divmod(LAYER_AT, D)
    lane = lax.broadcasted_iota(i32, (12, D), 1)
    a = pltpu.roll(flat[row : row + 16, :], D - s, 1)
    return jnp.where(lane < D - s, a[0:12], a[1:13])


def head_vector(flat):
    rows = []
    wide = lax.broadcasted_iota(i32, (1, D), 1)
    for part in range(GRID_CLS):
        row, s = divmod(HEAD_AT + part * CPART, D)
        a = flat[row : row + 1, :]
        if s:
            a = pltpu.roll(jnp.broadcast_to(a, (8, D)), D - s, 1)[0:1]
            b = pltpu.roll(jnp.broadcast_to(flat[row + 1 : row + 2, :], (8, D)), D - s, 1)[0:1]
            a = jnp.where(wide < D - s, a, b)
        rows.append(jnp.where(wide < CPART, a, 0.0)[:, :CPAD])
    return jnp.concatenate(rows, axis=0)


def store_flat(flat, at, values, count):
    row, s = divmod(at, D)
    wide = lax.broadcasted_iota(i32, (1, D), 1)
    values = jnp.where(wide < count, values, 0.0)
    if s:
        values = pltpu.roll(jnp.broadcast_to(values, (8, D)), s, 1)[0:1]
        flat[row + 1 : row + 2, :] = flat[row + 1 : row + 2, :] + jnp.where(wide < s, values, 0.0)
    flat[row : row + 1, :] = flat[row : row + 1, :] + jnp.where(wide >= s, values, 0.0)


def piece_of(weights, corners, s):
    a, z = s & 7, s >> 3
    return weights[a].at[z] if a < 6 else corners[(a - 6) * 2 + (z >> 1)].at[z & 1]


def head_masks():
    keys = lax.broadcasted_iota(i32, (1, ROWS_T, ROWS_T), 1) < TOK
    low = lax.broadcasted_iota(i32, (ROWS_T, 128), 1) < HD
    low_t = lax.broadcasted_iota(i32, (128, ROWS_T), 0) < HD
    return keys, low, low_t


def apart(two, low, axis):
    none = jnp.zeros_like(two)
    return jnp.concatenate([jnp.where(low, two, none), jnp.where(low, none, two)], axis=axis)


def pair_probs(q2, k2, keys, low):
    scores = nt(apart(k2, low, 0), q2).reshape(2, ROWS_T, ROWS_T) * SCORE_SCALE
    scores = jnp.where(keys, scores, -1e30)
    powers = jnp.exp(scores - jnp.max(scores, axis=1, keepdims=True))
    return powers * (1.0 / jnp.sum(powers, axis=1, keepdims=True))


def embed_kernel(tuned, vblock, n, images, *refs):
    (w0, w1, w2, w3, w4, w5, w6, w7, w8, w9, p0, p1, p2, p3, x0_out, qkv_out, attn, prm, hb, soft,
     patch_wide, patch, blocks, flat, table, rows, x0_all) = refs
    weights = (w0, w1, w2, w3, w4, w5)
    corners = (w6, w7, w8, w9)
    p2 = p2.at[0]
    me = me_of(tuned)
    part = lax.axis_index("cls")
    per = PATCHES // 4

    @pl.when(pl.program_id(0) == 0)
    def _():
        for s in range(BLOCKS):
            d = s ^ me
            w = piece_of(weights, corners, s)
            attn[pl.ds(pl.multiple_of(d * 48, 16), 48), :] = w[0:48, :]
            rest = w[48:80, :].astype(f32)
            patch_wide[pl.ds(pl.multiple_of(d * 24, 8), 24), :] = rest[0:24]
            blocks[d] = rest[24:32]
        patch[...] = patch_wide[...].astype(bf16)
        spread_vector(vblock, blocks, flat)
        prm[0:12, :] = layer_vectors(flat)
        prm[12:13, :] = flat[TOK + 1 : TOK + 2, :]
        prm[13:14, :] = flat[TOK + 2 : TOK + 3, :]
        prm[14:16, :] = jnp.zeros((2, D), f32)
        hb[0:4, :] = head_vector(flat)
        hb[4:8, :] = jnp.zeros((4, CPAD), f32)
        bias = flat[TOK : TOK + 1, :]
        table[...] = jnp.zeros_like(table)
        for k in range(4):
            for q in range(4):

                @pl.when((part ^ k) == q)
                def _(k=k, q=q):
                    table[k * per : k * per + per, :] = flat[1 + q * per : 1 + q * per + per, :] + bias

        table[PATCHES : PATCHES + 1, :] = flat[0:1, :] + flat[TOK + 3 : TOK + 4, :]
        soft[...] = jnp.zeros_like(soft)
        for k, piece in enumerate((p0, p1, p2, p3)):
            rows[k * PIX_ROWS : (k + 1) * PIX_ROWS, :] = nn(piece[...], patch[...])
            stored = piece[PIX_ROWS - 16 :, :].astype(f32)
            at = images * per - (PIX_ROWS - 16)
            for m in range(images):
                soft[part ^ k, m : m + 1, :] = stored[at + m // 3 : at + m // 3 + 1, (m % 3) * CPAD : (m % 3 + 1) * CPAD]
        for m in range(images):
            x0_all[m] = table[...]
            for k in range(4):
                at = slice(k * per, k * per + per)
                begin = k * PIX_ROWS + m * per
                x0_all[m, at, :] = x0_all[m, at, :] + rows[begin : begin + per, :]

    tokens = n * ROWS_T
    x0 = x0_all[pl.ds(pl.program_id(0) * n, n)]
    x0_out[...] = x0
    unit, _ = normalize(x0)
    normed = (unit * prm[0:1, :] + prm[1:2, :]).astype(bf16).reshape(tokens, D)
    for j, bias in ((0, prm[2:3, :]), (1, None), (2, prm[3:4, :])):
        one = nt(normed, attn[j * D : (j + 1) * D, :])
        if bias is not None:
            one = one + bias
        qkv_out[:, :, j * D : (j + 1) * D] = one.astype(bf16).reshape(n, ROWS_T, D)


def attend_kernel(n, w_out, prm, x0, qkv, att_out, x1_out):
    tokens = n * ROWS_T
    keys, low, low_t = head_masks()
    for i in range(n):
        for p in range(HEADS // 2):
            at = p * 128
            q2 = qkv[i, :, at : at + 128]
            v2t = qkv[i, :, 2 * D + at : 2 * D + at + 128].T
            probs = pair_probs(q2, qkv[i, :, D + at : D + at + 128], keys, low).astype(bf16)
            both = nn(apart(v2t, low_t, 1), probs.reshape(2 * ROWS_T, ROWS_T))
            att_out[i, :, at : at + 128] = both.T.astype(bf16)
    branch = nt(att_out[...].reshape(tokens, D), w_out[...]) + prm[4:5, :]
    x1_out[...] = x0[...] + branch.reshape(n, ROWS_T, D)


def middle_kernel(tuned, n, images, scales, *refs):
    if not tuned:
        given, *refs = refs
    (w0, w1, w2, w3, w4, w5, w6, w7, w8, w9, prm, hb, soft, meta, x1_in,
     dx1_out, keep, send, vgrad, hgrad, loss,
     w_up, w_down, w_head, act, slope, mask, masks_all, pooled, dpooled, glow, acc_up, acc_down,
     normed_all, dy_all, dup_all, up_bias, up_sum) = refs
    weights = (w0, w1, w2, w3, w4, w5)
    corners = (w6, w7, w8, w9)
    me = me_of(tuned)
    step = pl.program_id(0)
    last = pl.num_programs(0) - 1

    @pl.when(step == 0)
    def _():
        for s in range(BLOCKS):
            d = s ^ me
            dp, cl = d >> 2, d & 3
            w = piece_of(weights, corners, s)
            rows = pl.ds(pl.multiple_of(dp * 48, 16), 48)
            w_head[cl, rows, :] = unpack_head(w[0:32, :])
            columns = pl.ds(pl.multiple_of(cl * D, 128), D)
            w_up[rows, columns] = w[32:80, :]
            w_down[rows, columns] = w[80:128, :]
            if tuned:
                seen = unpack_mask(w[128:144, :].astype(f32))
                masks_all[cl, pl.ds(pl.multiple_of(dp * 24, 8), 24), :] = seen
        if tuned:
            mask[...] = jnp.zeros_like(mask)
            for m in range(images):
                for q in range(4):
                    mask[q, m : m + 1, :] = masks_all[q, pl.ds(meta[2, m], 1), :]
        else:
            mask[...] = given[...]
        for c in range(4):
            up_bias[:, c * D : (c + 1) * D] = prm[8 + c : 9 + c, :]
        up_sum[...] = jnp.zeros_like(up_sum)
        vgrad[...] = jnp.zeros_like(vgrad)
        pooled[...] = jnp.zeros_like(pooled)

    tokens = n * ROWS_T
    x1 = x1_in[...].reshape(tokens, D)
    unit_two, inverse_two = normalize(x1)
    normed = (unit_two * prm[5:6, :] + prm[6:7, :]).astype(bf16)
    total = jnp.zeros((tokens, D), f32)
    mine = pl.ds(pl.multiple_of(step * tokens, 16), tokens)
    normed_all[mine, :] = normed
    chunks = [slice(c, c + F_CHUNK) for c in range(0, FF, F_CHUNK)]
    for c in chunks:
        pre = nn(normed, w_up[:, c]) + up_bias[:, c]
        half, bell = gelu_parts(pre)
        hot = (pre * half).astype(bf16)
        act[mine, c] = hot
        slope[:, c] = half + pre * bell
        total = total + nt(hot, w_down[:, c])
    x2 = x1 + (total + prm[7:8, :])
    unit, inverse = normalize(x2)
    real = lax.broadcasted_iota(i32, (ROWS_T, D), 0) < TOK
    sums = []
    for i in range(n):
        u = unit[i * ROWS_T : (i + 1) * ROWS_T]
        sums.append(jnp.sum(jnp.where(real, u, 0.0), axis=0, keepdims=True))
        pooled[pl.ds(step * n + i, 1), :] = sums[i] * (1.0 / TOK) * prm[12:13, :] + prm[13:14, :]

    low = pooled[...].astype(bf16)
    rows8 = (16, CPAD)
    row_id = lax.broadcasted_iota(i32, rows8, 0)
    lane = lax.broadcasted_iota(i32, rows8, 1)
    label = jnp.full(rows8, -1, i32)
    weight = jnp.zeros(rows8, f32)
    squared = jnp.zeros(rows8, f32)
    for i in range(images):
        kind = meta[1, i]
        label = jnp.where(row_id == i, meta[0, i], label)
        weight = jnp.where(row_id == i, jnp.where(kind == 0, scales[0], jnp.where(kind == 2, scales[1], 0.0)), weight)
        squared = jnp.where(row_id == i, jnp.where(kind == 1, 1.0, 0.0), squared)
    inside = lane < CPART
    logits, hots, lives, masks, tops = [], [], [], [], []
    pad = jnp.zeros((8, CPAD), f32)
    for q in range(4):
        one = nn(low, w_head[q]) + hb[q : q + 1, :]
        hot = (lane + q * CPART == label) & inside
        seen = (jnp.concatenate([mask[q], pad], axis=0) > 0.5) & inside
        logits.append(one)
        hots.append(hot)
        masks.append(seen)
        lives.append(seen | hot)
        tops.append(jnp.max(jnp.where(inside, one, -3e38), axis=1, keepdims=True))
    top = jnp.maximum(jnp.maximum(tops[0], tops[1]), jnp.maximum(tops[2], tops[3]))
    alive = sum(
        jnp.sum(jnp.where(lives[q], jnp.exp(logits[q] - top), 0.0), axis=1, keepdims=True) for q in range(4)
    )
    norm = top + jnp.log(alive)
    target = sum(jnp.sum(jnp.where(hots[q], logits[q], 0.0), axis=1, keepdims=True) for q in range(4))
    cross = norm - target
    value = jnp.sum(jnp.where(weight[:, 0:1] > 0, weight[:, 0:1] * cross, 0.0))
    back = jnp.zeros((16, D), f32)
    for q in range(4):
        gap = jnp.where(masks[q], logits[q] - jnp.concatenate([soft[q], pad], axis=0), 0.0)
        value = value + scales[2] * jnp.sum(squared * gap * gap)
        share = jnp.where(lives[q], jnp.exp(logits[q] - norm), 0.0)
        grad = weight * (share - jnp.where(hots[q], 1.0, 0.0)) + squared * (2.0 * scales[2]) * gap
        g = grad.astype(bf16)
        glow[q] = g
        back = back + nt(g, w_head[q])
    dpooled[...] = back

    pieces = []
    for i in range(n):
        grad = dpooled[pl.ds(step * n + i, 1), :]
        vgrad[12:13, :] = vgrad[12:13, :] + grad * (1.0 / TOK) * sums[i]
        vgrad[13:14, :] = vgrad[13:14, :] + grad
        dz = grad * (1.0 / TOK) * prm[12:13, :]
        u = unit[i * ROWS_T : (i + 1) * ROWS_T]
        d = inverse[i * ROWS_T : (i + 1) * ROWS_T] * (
            dz - jnp.mean(dz, axis=-1, keepdims=True) - u * jnp.mean(dz * u, axis=-1, keepdims=True)
        )
        pieces.append(jnp.where(real, d, 0.0))
    dx2 = jnp.concatenate(pieces, axis=0)
    dy = dx2.astype(bf16)
    vgrad[7:8, :] = vgrad[7:8, :] + jnp.sum(dy.astype(f32), axis=0, keepdims=True)
    dy_all[mine, :] = dy
    dnormed = jnp.zeros((tokens, D), f32)
    for c in chunks:
        dup = (nn(dy, w_down[:, c]) * slope[:, c]).astype(bf16)
        up_sum[:, c] = up_sum[:, c] + jnp.sum(dup.astype(f32), axis=0, keepdims=True)
        dup_all[mine, c] = dup
        dnormed = dnormed + nt(dup, w_up[:, c])
    vgrad[5:6, :] = vgrad[5:6, :] + jnp.sum(dnormed * unit_two, axis=0, keepdims=True)
    vgrad[6:7, :] = vgrad[6:7, :] + jnp.sum(dnormed, axis=0, keepdims=True)
    dx1 = dx2 + normalize_back(unit_two, inverse_two, dnormed * prm[5:6, :])
    dx1_out[...] = dx1.reshape(n, ROWS_T, D)

    @pl.when(step == last)
    def _():
        loss[...] = jnp.where(lax.broadcasted_iota(i32, loss.shape, 1) == 0, 0.0, value)
        hgrad[...] = jnp.zeros_like(hgrad)
        for q in range(4):
            hgrad[q : q + 1, :] = jnp.sum(glow[q].astype(f32), axis=0, keepdims=True)
        for c in range(4):
            vgrad[8 + c : 9 + c, :] = up_sum[:, c * D : (c + 1) * D]
        for q in range(4):
            slope[0:D, q * CPAD : (q + 1) * CPAD] = tn(low, glow[q])
        for c in chunks:
            acc_down[:, c] = tn(dy_all[...], act[:, c])
            acc_up[:, c] = tn(normed_all[...], dup_all[:, c])
        for s in range(BLOCKS):
            d = s ^ me
            dp, cl = d >> 2, d & 3
            core, place = grad_place(s)
            rows = pl.ds(pl.multiple_of(dp * 48, 8), 48)
            columns = pl.ds(pl.multiple_of(cl * D, 128), D)
            head = slope[rows, pl.ds(pl.multiple_of(cl * CPAD, 128), CPAD)]
            block = [pack_head(head), acc_up[rows, columns], acc_down[rows, columns]]
            put_block(block, SECTIONS_TWO, keep, send, core, place)


def run_middle(tuned, n, images, scales, *operands):
    steps = images // n
    whole = lambda shape: pl.BlockSpec(shape, lambda i: (0,) * len(shape))
    per = lambda width: pl.BlockSpec((n, ROWS_T, width), lambda i: (i, 0, 0))
    return pl.pallas_call(
        functools.partial(middle_kernel, tuned, n, images, scales),
        grid=(steps,),
        in_specs=[whole((4, 8, CPAD))] * (0 if tuned else 1)
        + [whole((4, R_TWO + R_MASK, D))] * 6
        + [whole((2, R_TWO + R_MASK, D))] * 4
        + [whole((16, D)), whole((8, CPAD)), whole((4, 8, CPAD))]
        + [SMEM, per(D)],
        out_specs=[
            per(D),
            whole((16, R_TWO, D)),
            whole((16, coded(SECTIONS_TWO), D)),
            whole((16, D)),
            whole((8, CPAD)),
            whole((8, 128)),
        ],
        out_shape=[
            sds((images, ROWS_T, D), f32),
            sds((16, R_TWO, D), f32),
            sds((16, coded(SECTIONS_TWO), D), jnp.int16),
            sds((16, D), f32),
            sds((8, CPAD), f32),
            sds((8, 128), f32),
        ],
        scratch_shapes=[
            pltpu.VMEM((D, FF), bf16),
            pltpu.VMEM((D, FF), bf16),
            pltpu.VMEM((4, D, CPAD), bf16),
            pltpu.VMEM((images * ROWS_T, FF), bf16),
            pltpu.VMEM((n * ROWS_T, FF), f32),
            pltpu.VMEM((4, 8, CPAD), f32),
            pltpu.VMEM((4, GRID_DP * 24, CPAD), f32),
            pltpu.VMEM((16, D), f32),
            pltpu.VMEM((16, D), f32),
            pltpu.VMEM((4, 16, CPAD), bf16),
            pltpu.VMEM((D, FF), f32),
            pltpu.VMEM((D, FF), f32),
            pltpu.VMEM((images * ROWS_T, D), bf16),
            pltpu.VMEM((images * ROWS_T, D), bf16),
            pltpu.VMEM((images * ROWS_T, FF), bf16),
            pltpu.VMEM((1, FF), f32),
            pltpu.VMEM((1, FF), f32),
        ],
        cost_estimate=cost(30),
        compiler_params=params_of(36),
    )(*operands)


def attend_back_kernel(n, first, *refs):
    if first:
        (w_out, vgrad_in, qkv, att, dx1_in, dqkv, acc, vgrad) = refs
    else:
        (w_out, vgrad_in, qkv, att, dx1_in, acc_in, _, dqkv, acc, vgrad) = refs

    @pl.when(pl.program_id(0) == 0)
    def _():
        acc[...] = jnp.zeros_like(acc) if first else acc_in[...]
        vgrad[...] = vgrad_in[...]

    tokens = n * ROWS_T
    dout = dx1_in[...].reshape(tokens, D).astype(bf16)
    vgrad[4:5, :] = vgrad[4:5, :] + jnp.sum(dout.astype(f32), axis=0, keepdims=True)
    acc[...] = acc[...] + tn(dout, att[...].reshape(tokens, D))
    datt = nn(dout, w_out[...]).astype(bf16)
    keys, low, low_t = head_masks()
    both = (2 * ROWS_T, ROWS_T)
    for i in range(n):
        rows = slice(i * ROWS_T, (i + 1) * ROWS_T)
        for p in range(HEADS // 2):
            at = p * 128
            q2 = qkv[i, :, at : at + 128]
            k2 = qkv[i, :, D + at : D + at + 128]
            v2 = qkv[i, :, 2 * D + at : 2 * D + at + 128]
            do = datt[rows, at : at + 128]
            probs = pair_probs(q2, k2, keys, low)
            dprobs = nt(apart(v2, low, 0), do).reshape(probs.shape)
            mean = jnp.sum(probs * dprobs, axis=1, keepdims=True)
            dscores = (probs * (dprobs - mean)).astype(bf16).reshape(both)
            dq = nn(apart(k2.T, low_t, 1), dscores)
            dk = nn(dscores, q2)
            dv = nn(probs.astype(bf16).reshape(both), do)
            dqkv[i, :, at : at + 128] = (dq * SCORE_SCALE).T.astype(bf16)
            dk = jnp.where(low, dk[:ROWS_T], dk[ROWS_T:]) * SCORE_SCALE
            dqkv[i, :, D + at : D + at + 128] = dk.astype(bf16)
            dv = jnp.where(low, dv[:ROWS_T], dv[ROWS_T:])
            dqkv[i, :, 2 * D + at : 2 * D + at + 128] = dv.astype(bf16)


def unit_back_kernel(n, vblock, images, *refs):
    (w_in, prm, vgrad_in, hgrad, p0, p1, p2, p3, x0, dqkv_in, dx1_in,
     acc_patch, blocks, vgrad, dx0_all, rows, flat) = refs
    p2 = p2.at[0]
    part = lax.axis_index("cls")
    per = PATCHES // 4

    @pl.when(pl.program_id(0) == 0)
    def _():
        vgrad[...] = vgrad_in[...]

    tokens = n * ROWS_T
    dx1 = dx1_in[...].reshape(tokens, D)
    dqkv = dqkv_in[...].reshape(tokens, 3 * D)
    vgrad[2:3, :] = vgrad[2:3, :] + jnp.sum(dqkv[:, 0:D].astype(f32), axis=0, keepdims=True)
    vgrad[3:4, :] = vgrad[3:4, :] + jnp.sum(dqkv[:, 2 * D : 3 * D].astype(f32), axis=0, keepdims=True)
    unit, inverse = normalize(x0[...].reshape(tokens, D))
    dnormed = nn(dqkv, w_in[...])
    vgrad[0:1, :] = vgrad[0:1, :] + jnp.sum(dnormed * unit, axis=0, keepdims=True)
    vgrad[1:2, :] = vgrad[1:2, :] + jnp.sum(dnormed, axis=0, keepdims=True)
    dx0 = dx1 + normalize_back(unit, inverse, dnormed * prm[0:1, :])
    dx0_all[pl.ds(pl.program_id(0) * n, n)] = dx0.reshape(n, ROWS_T, D)

    @pl.when(pl.program_id(0) == pl.num_programs(0) - 1)
    def _():
        rows[...] = jnp.zeros_like(rows)
        for m in range(images):
            for k in range(4):
                begin = k * PIX_ROWS + m * per
                rows[begin : begin + per, :] = dx0_all[m, k * per : k * per + per, :]
        low = rows[...].astype(bf16)
        total = tn(p0[...], low[:PIX_ROWS])
        for k, piece in ((1, p1), (2, p2), (3, p3)):
            total = total + tn(piece[...], low[k * PIX_ROWS : (k + 1) * PIX_ROWS])
        acc_patch[...] = total
        position = dx0_all[0]
        for m in range(1, images):
            position = position + dx0_all[m]
        flat[...] = jnp.zeros_like(flat)
        for k in range(4):
            for q in range(4):

                @pl.when((part ^ k) == q)
                def _(k=k, q=q):
                    flat[1 + q * per : 1 + q * per + per, :] = position[k * per : k * per + per, :]

        first = position[PATCHES : PATCHES + 1, :]
        flat[0:1, :] = first
        flat[TOK : TOK + 1, :] = jnp.sum(position[0:PATCHES, :], axis=0, keepdims=True)
        flat[TOK + 1 : TOK + 2, :] = vgrad[12:13, :]
        flat[TOK + 2 : TOK + 3, :] = vgrad[13:14, :]
        flat[TOK + 3 : TOK + 4, :] = first
        for q in range(GRID_CLS):
            wide = jnp.concatenate([hgrad[q : q + 1, :], jnp.zeros((1, D - CPAD), f32)], axis=1)
            store_flat(flat, HEAD_AT + q * CPART, wide, CPART)
        for j in range(12):
            store_flat(flat, LAYER_AT + j * D, vgrad[j : j + 1, :], D)
        cut_vector(vblock, flat, blocks)


def qkv_back_kernel(n, tuned, prm, x0, dqkv_in, acc_out, keep, send, acc):
    @pl.when(pl.program_id(0) == 0)
    def _():
        acc[0 : 3 * D, :] = jnp.zeros((3 * D, D), f32)
        acc[3 * D : 4 * D, :] = acc_out[...]

    tokens = n * ROWS_T
    dqkv = dqkv_in[...].reshape(tokens, 3 * D)
    unit, _ = normalize(x0[...].reshape(tokens, D))
    normed = (unit * prm[0:1, :] + prm[1:2, :]).astype(bf16)
    for j in range(3):
        at = slice(j * D, (j + 1) * D)
        acc[at, :] = acc[at, :] + tn(dqkv[:, at], normed)

    @pl.when(pl.program_id(0) == pl.num_programs(0) - 1)
    def _():
        me = me_of(tuned)
        for s in range(BLOCKS):
            core, place = grad_place(s)
            block = acc[pl.ds(pl.multiple_of((s ^ me) * 48, 8), 48), :]
            put_block([block], SECTIONS_ATTENTION, keep, send, core, place)


def block_back_kernel(tuned, acc_patch, blocks, keep, send):
    me = me_of(tuned)
    for s in range(BLOCKS):
        d = s ^ me
        core, place = grad_place(s)
        rows = pl.ds(pl.multiple_of(d * 24, 8), 24)
        put_block([acc_patch[rows, :], blocks[d]], SECTIONS_REST, keep, send, core, place)


def update_kernel(v0, v1, v2, v3, one, two, vec, *refs):
    ins, (loss_out, norm_out, *outs) = refs[:18], refs[18:]
    sums = (v0[...] + v1[...]) + (v2[...] + v3[...])
    norm = jnp.sqrt(sums[0, 0])
    loss_out[0] = sums[0, 1]
    norm_out[0] = norm
    clip = jnp.minimum(1.0, CLIP_NORM / (norm + 1e-06))
    grads = [
        one[48:72, :],
        one[0:48, :],
        two[32:80, :],
        two[80:128, :],
        unpack_head(two[0:32, :])[:, :CPART],
        vec[...],
    ]
    for j, grad in enumerate(grads):
        news = advance(ins[3 * j][...], ins[3 * j + 1][...], ins[3 * j + 2][...], grad, clip)
        for k in range(3):
            outs[3 * j + k][...] = news[k]


def flip(n, k):
    return [(i, i ^ k) for i in range(n)]


def to_core(v):
    return lax.ppermute(v, "cls", flip(4, 1))


def to_x(v):
    return lax.ppermute(v, "cls", flip(4, 2))


def to_y(v):
    return lax.ppermute(v, "dp", flip(8, 1))


def to_z(v, k):
    return lax.ppermute(v, "dp", flip(8, 2 * k))


def gather_blocks(near, at_x, at_y, corner):
    whole = [w for v in (near, at_x, at_y) for w in (v, to_core(v))]
    return whole + corner + [to_core(v) for v in corner]


def corner_of(at_x, at_y):
    return [to_y(at_x[:2]), to_x(at_y[2:])]


def first_kernel(pieces, sections, *refs):
    *pairs, send_a, keep_a, send_b, keep_b = refs

    def total(j):
        sums = [
            keep[j, 0] + decode(got.at[j, 0], piece) for keep, got, piece in zip(pairs[::2], pairs[1::2], pieces)
        ]
        return jnp.concatenate(sums, axis=0)

    encode(total(0), sections, send_a.at[0])
    keep_a[0] = total(1)
    encode(total(2), sections, send_b.at[0])
    keep_b[0] = total(3)


def second_kernel(sections, keep_a, keep_b, got_a, got_b, send_a, rest_a, send_b, rest_b):
    for keep, got, send, rest in ((keep_a, got_a, send_a, rest_a), (keep_b, got_b, send_b, rest_b)):
        rest[0] = keep[0, 0] + decode(got.at[0, 0], sections)
        encode(keep[1, 0] + decode(got.at[1, 0], sections), sections, send.at[0])


def third_kernel(sections, keep_a, keep_b, got_a, got_b, own, send_1, send_2, send_3):
    own[...] = keep_a[0] + decode(got_a.at[0], sections)
    encode(keep_a[1] + decode(got_a.at[1], sections), sections, send_1)
    encode(keep_b[0] + decode(got_b.at[0], sections), sections, send_2)
    encode(keep_b[1] + decode(got_b.at[1], sections), sections, send_3)


def third_pair_kernel(sections, keep_a, keep_b, got_a, got_b, rest, send):
    for j, (keep, got) in enumerate(((keep_a, got_a), (keep_b, got_b))):
        rest[j] = keep[0] + decode(got.at[0], sections)
        encode(keep[1] + decode(got.at[1], sections), sections, send.at[j])


def near_kernel(sections, rest, got, own, send):
    own[...] = rest[0] + decode(got.at[0], sections)
    encode(rest[1] + decode(got.at[1], sections), sections, send)


def fourth_kernel(sections, own, *refs):
    *got, before, share, sums = refs
    total = own[...]
    for code in got:
        total = total + decode(code, sections)
    share[...] = total
    lane = lax.broadcasted_iota(i32, (8, 128), 1)
    sums[...] = before[...] + jnp.where(lane == 0, jnp.sum(total * total), 0.0)


def scatter_first(pairs, pieces, sections):
    rows = sections[-1]
    operands = [v for pair in pairs for v in pair]
    wide, code = [pl.BlockSpec((1, r, D), lambda j: (j, 0, 0)) for r in (rows, coded(sections))]
    return pl.pallas_call(
        functools.partial(first_kernel, pieces, sections),
        grid=(4,),
        in_specs=[pl.BlockSpec((4, 1, v.shape[1], D), lambda j: (0, j, 0, 0)) for v in operands],
        out_specs=[code, wide, code, wide],
        out_shape=[sds((4, coded(sections), D), jnp.int16), sds((4, rows, D), f32)] * 2,
        compiler_params=params_of(16),
    )(*[v.reshape((4, 4) + v.shape[1:]) for v in operands])


def scatter_second(keep_a, keep_b, got_a, got_b, sections):
    rows = sections[-1]
    pairs, codes = [pl.BlockSpec((2, 1, r, D), lambda j: (0, j, 0, 0)) for r in (rows, coded(sections))]
    wide, code = [pl.BlockSpec((1, r, D), lambda j: (j, 0, 0)) for r in (rows, coded(sections))]
    return pl.pallas_call(
        functools.partial(second_kernel, sections),
        grid=(2,),
        in_specs=[pairs] * 2 + [codes] * 2,
        out_specs=[code, wide, code, wide],
        out_shape=[sds((2, coded(sections), D), jnp.int16), sds((2, rows, D), f32)] * 2,
        cost_estimate=cost(2),
        compiler_params=params_of(16),
    )(*[v.reshape((2, 2) + v.shape[1:]) for v in (keep_a, keep_b, got_a, got_b)])


def scatter_third(keep_a, keep_b, got_a, got_b, sections):
    rows = sections[-1]
    return pl.pallas_call(
        functools.partial(third_kernel, sections),
        out_shape=[sds((rows, D), f32)] + [sds((coded(sections), D), jnp.int16)] * 3,
        cost_estimate=cost(2),
        compiler_params=params_of(16),
    )(keep_a, keep_b, got_a, got_b)


def scatter_third_pair(keep_a, keep_b, got_a, got_b, sections):
    rows = sections[-1]
    return pl.pallas_call(
        functools.partial(third_pair_kernel, sections),
        out_shape=[sds((2, rows, D), f32), sds((2, coded(sections), D), jnp.int16)],
        compiler_params=params_of(16),
    )(keep_a, keep_b, got_a, got_b)


def scatter_near(rest, got, sections):
    rows = sections[-1]
    return pl.pallas_call(
        functools.partial(near_kernel, sections),
        out_shape=[sds((rows, D), f32), sds((coded(sections), D), jnp.int16)],
        compiler_params=params_of(16),
    )(rest, got)


def scatter_fourth(own, got, sections, before):
    return pl.pallas_call(
        functools.partial(fourth_kernel, sections),
        out_shape=[sds(own.shape, f32), sds((8, 128), f32)],
        cost_estimate=cost(2),
        compiler_params=params_of(16),
    )(own, *got, before)


def sums_along_z(v):
    v = v + to_core(v)
    v = (v + to_x(v)) + (to_y(v) + lax.ppermute(v, ("dp", "cls"), flip(BLOCKS, GRID_CLS + 2)))
    return [v] + [to_z(v, k) for k in (1, 2, 3)]


def plain_gather(masters, vblock):
    patch, attention, up, down, head, vector = [w.astype(bf16) for w in masters]
    both = ("dp", "cls")
    patch = lax.all_gather(patch, both, axis=0, tiled=True).reshape(BLOCKS, 24, D)
    attention = lax.all_gather(attention, both, axis=2, tiled=True)[0].T.reshape(BLOCKS, 48, D)
    vector = lax.all_gather(vector, both, axis=0, tiled=True).reshape(BLOCKS, vblock)
    vector = jnp.pad(vector, ((0, 0), (0, 8 * D - vblock))).reshape(BLOCKS, 8, D)
    up = lax.all_gather(lax.all_gather(up, "dp", axis=1, tiled=True), "cls", axis=2, tiled=True)[0]
    down = lax.all_gather(lax.all_gather(down, "dp", axis=2, tiled=True), "cls", axis=1, tiled=True)[0].T
    head = lax.all_gather(lax.all_gather(head, "dp", axis=0, tiled=True), "cls", axis=1, tiled=True)
    up, down = [
        w.reshape(GRID_DP, 48, GRID_CLS, D).transpose(0, 2, 1, 3).reshape(BLOCKS, 48, D) for w in (up, down)
    ]
    head = head.reshape(GRID_DP, 48, GRID_CLS, CPART).transpose(0, 2, 1, 3).reshape(BLOCKS, 48, CPART)
    head = pack_head(jnp.pad(head, ((0, 0), (0, 0), (0, CPAD - CPART))))
    one = jnp.concatenate([attention, patch, vector], axis=1).reshape(4, 8, R_ONE, D)
    two = jnp.concatenate([head, up, down], axis=1).reshape(4, 8, R_TWO, D)
    return [one[:, a] for a in range(8)], [two[:, a] for a in range(8)]


def plain_scatter(att, rest, two, vblock):
    def in_order(keep, send, sections):
        send = [decode(send[j], sections) for j in range(16)]
        return jnp.stack([(keep, send)[grad_place(s)[0]][grad_place(s)[1]] for s in range(BLOCKS)])

    one = jnp.concatenate([in_order(*att, SECTIONS_ATTENTION), in_order(*rest, SECTIONS_REST)], axis=1)
    two = in_order(*two, SECTIONS_TWO)
    both = ("dp", "cls")
    attention = one[:, 0:48].reshape(4 * D, D).T[None]
    patch = one[:, 48:72].reshape(PD, D)
    vector = one[:, 72:80].reshape(BLOCKS, 8 * D)[:, :vblock].reshape(-1)
    up, down = [
        w.reshape(GRID_DP, GRID_CLS, 48, D).transpose(0, 2, 1, 3).reshape(D, FF)
        for w in (two[:, 32:80], two[:, 80:128])
    ]
    head = unpack_head(two[:, 0:32])[:, :, :CPART]
    head = head.reshape(GRID_DP, GRID_CLS, 48, CPART).transpose(0, 2, 1, 3).reshape(D, C)

    def split(v, at_dp, at_cls):
        v = lax.psum_scatter(v, "dp", scatter_dimension=at_dp, tiled=True)
        return lax.psum_scatter(v, "cls", scatter_dimension=at_cls, tiled=True)

    return (
        lax.psum_scatter(patch, both, scatter_dimension=0, tiled=True),
        lax.psum_scatter(attention, both, scatter_dimension=2, tiled=True),
        split(up, 0, 1)[None],
        split(down.T, 1, 0)[None],
        split(head, 0, 1),
        lax.psum_scatter(vector, both, scatter_dimension=0, tiled=True),
    )


def take_rows_kernel(rows, source, out, sem):
    def one(i, carry):
        copy = pltpu.make_async_copy(source.at[rows[i]], out.at[i], sem)
        copy.start()
        copy.wait()
        return carry

    lax.fori_loop(0, out.shape[0], one, 0)


def take_rows(source, rows):
    return pl.pallas_call(
        take_rows_kernel,
        out_shape=sds((rows.shape[0],) + source.shape[1:], source.dtype),
        in_specs=[SMEM, ANY],
        out_specs=ANY,
        scratch_shapes=[pltpu.SemaphoreType.DMA(())],
    )(rows, source)


def pick_small(source, rows):
    hot = (rows[:, None] == jnp.arange(source.shape[0])[None, :]).astype(f32)
    return jnp.dot(hot, source.astype(f32), precision=lax.Precision.HIGHEST)


def plain_replay(buffer_patches, buffer_logits, buffer_labels, replay_owner, replay_row, kind_rows):
    dp_count, dp_index = lax.axis_size("dp"), lax.axis_index("dp")
    replay_count = 2 * kind_rows
    capacity = max(2, -(-replay_count // dp_count))
    table = lax.all_gather(buffer_labels, "dp", axis=0, tiled=True)
    owners = replay_owner[:, 0].reshape(dp_count, replay_count)
    local_rows = replay_row.reshape(dp_count, replay_count)
    earlier = jnp.arange(replay_count)[None, :] < jnp.arange(replay_count)[:, None]
    same_owner = owners[:, :, None] == owners[:, None, :]
    ranks = jnp.sum(jnp.where(same_owner & earlier[None], 1, 0), axis=2).astype(i32)
    slot_ids = jnp.arange(capacity, dtype=i32)
    wanted = (owners == dp_index)[:, :, None] & (ranks[:, :, None] == slot_ids[None, None, :])
    slot_rows = jnp.sum(jnp.where(wanted, local_rows[:, :, None], 0), axis=1).reshape(-1)
    pixels = take_rows(buffer_patches, slot_rows)
    logits = pick_small(buffer_logits, slot_rows).astype(bf16)
    pixels = lax.all_to_all(pixels, "dp", split_axis=0, concat_axis=0, tiled=True)
    logits = lax.all_to_all(logits, "dp", split_axis=0, concat_axis=0, tiled=True)
    my_owners, my_ranks, my_rows = [
        lax.dynamic_index_in_dim(v, dp_index, 0, keepdims=False) for v in (owners, ranks, local_rows)
    ]
    places = my_owners * buffer_labels.shape[0] + my_rows
    labels = jnp.sum(jnp.where(places[:, None] == jnp.arange(table.shape[0])[None, :], table[None, :], 0), axis=1)
    return pixels, logits, labels.astype(i32), (my_owners * capacity + my_ranks).astype(i32)


def on_device(
    current_patches,
    current_labels,
    buffer_patches,
    buffer_logits,
    buffer_labels,
    replay_owner,
    replay_row,
    seen_mask,
    patch_weight,
    patch_moment,
    patch_average,
    attention_weight,
    attention_moment,
    attention_average,
    up_weight,
    up_moment,
    up_average,
    down_weight,
    down_moment,
    down_average,
    head_weight,
    head_moment,
    head_average,
    vector_weight,
    vector_moment,
    vector_average,
):
    dp_count, cls_count = lax.axis_size("dp"), lax.axis_size("cls")
    dp_index, cls_index = lax.axis_index("dp"), lax.axis_index("cls")
    kind_rows = current_patches.shape[0]
    replay_count = 2 * kind_rows
    group_rows = 3 * kind_rows
    normal_count = kind_rows * dp_count
    patch_part = current_patches.shape[1]
    cur_own, rep_own = kind_rows // cls_count, replay_count // cls_count
    images = cur_own + rep_own
    class_part = head_weight.shape[1]
    vblock = vector_weight.shape[0] * dp_count * cls_count // BLOCKS
    tuned = dp_count == GRID_DP and cls_count == GRID_CLS and replay_count == 2 * dp_count
    masters = (patch_weight, attention_weight, up_weight, down_weight, head_weight, vector_weight)
    moments = (patch_moment, attention_moment, up_moment, down_moment, head_moment, vector_moment)
    averages = (patch_average, attention_average, up_average, down_average, head_average, vector_average)

    def views(v, j):
        return v[0].T if j in (1, 3) else v[0] if j == 2 else v

    current_view, buffer_view = current_patches.transpose(1, 0, 2), buffer_patches.transpose(1, 0, 2)
    if tuned:
        pack = pl.pallas_call(
            pack_weights_kernel,
            out_shape=sds((R_ONE + R_TWO + R_MASK, D), bf16),
            cost_estimate=cost(2),
            compiler_params=params_of(60),
        )

    def exchange(sent):
        own, near, far = sent
        far = lax.ppermute(far, "cls", flip(4, 2))
        return [own, lax.ppermute(near, "cls", flip(4, 1)), far, lax.ppermute(far[1], "cls", flip(4, 1))]

    def pick(find, stored, *operands):
        out_shape = [sds((PIX_ROWS, PD), bf16)] * 2 + [sds((2, PIX_ROWS, PD), bf16)]
        return pl.pallas_call(
            functools.partial(pick_kernel, cur_own, rep_own, find),
            out_shape=out_shape + ([sds((3, 8), i32)] if find else []),
            in_specs=[SMEM] * (4 if find else 1) + [ANY, ANY, VMEM],
            out_specs=[VMEM] * 3 + ([SMEM] if find else []),
            scratch_shapes=[
                pltpu.VMEM((patch_part, stored, PD), bf16),
                pltpu.VMEM((patch_part, kind_rows, PD), bf16),
                pltpu.VMEM((PD // 128, patch_part * stored, 128), f32),
                pltpu.VMEM((PD // 128, patch_part * kind_rows, 128), f32),
                pltpu.VMEM((stored, CPAD), f32),
                pltpu.VMEM((PIX_ROWS, PD), f32),
                pltpu.SMEM((replay_count,), i32),
                pltpu.SemaphoreType.DMA((patch_part // 7 + 1,)),
            ],
            cost_estimate=cost(7),
            compiler_params=params_of(60),
        )(*operands)

    if tuned:
        *sent, meta = pick(
            True,
            buffer_patches.shape[0],
            replay_owner.reshape(-1),
            replay_row,
            current_labels,
            buffer_labels,
            current_view,
            buffer_view,
            buffer_logits,
        )
        got = exchange(sent)
        got[1], vec = lax.optimization_barrier((got[1], vector_weight))
        vec = jnp.pad(vec, (0, 8 * D - vblock)).reshape(8, D)
        packed = pack(
            views(attention_weight, 1), patch_weight, vec, views(up_weight, 2), views(down_weight, 3), head_weight, seen_mask
        )
    else:
        moved, logits, labels, places = plain_replay(
            buffer_patches, buffer_logits, buffer_labels, replay_owner, replay_row, kind_rows
        )
        sent = pick(False, moved.shape[0], places, current_view, moved.transpose(1, 0, 2), logits)
        got = exchange(sent)
        row_mask = jnp.pad(seen_mask.astype(bf16), ((0, 0), (0, CPAD - class_part)))
        row_mask = lax.all_gather(row_mask, "cls").astype(f32)
        mask_rows = [
            lax.dynamic_slice_in_dim(row_mask, cls_index * cur_own, cur_own, 1),
            lax.dynamic_slice_in_dim(row_mask, kind_rows + cls_index * rep_own, rep_own, 1),
            jnp.zeros((cls_count, 8 - images, CPAD), f32),
        ]
        given = jnp.concatenate(mask_rows, axis=1)
        kinds = jnp.where(jnp.arange(replay_count) < kind_rows, 1, 2).astype(i32)
        labels = jnp.where(kinds == 1, 0, labels)

        def own(current, replayed, fill):
            return jnp.concatenate(
                [
                    lax.dynamic_slice_in_dim(current, cls_index * cur_own, cur_own, 0),
                    lax.dynamic_slice_in_dim(replayed, cls_index * rep_own, rep_own, 0),
                    jnp.full((8 - images,), fill, i32),
                ]
            )

        nothing = jnp.zeros_like(current_labels)
        meta = jnp.stack([own(current_labels, labels, 0), own(nothing, kinds, 3), jnp.zeros((8,), i32)])

    if tuned:
        column = [packed] + [to_z(packed, k) for k in (1, 2, 3)]
        near_one = jnp.stack([v[:R_ONE] for v in column])
        near_two = jnp.stack([v[R_ONE:] for v in column])
        near_one, got[2] = lax.optimization_barrier((near_one, got[2]))
        at_x, at_y = to_x(near_one), to_y(near_one)
        at_x, near_two = lax.optimization_barrier((at_x, near_two))
        at_x, at_y, corner = lax.optimization_barrier((at_x, at_y, corner_of(at_x, at_y)))
        one = gather_blocks(near_one, at_x, at_y, corner)
        two_x, two_y = to_x(near_two), to_y(near_two)
    else:
        one, two = plain_gather(masters, vblock)
        two = [jnp.pad(v, ((0, 0), (0, R_MASK), (0, 0))) for v in two]
        one, two = [w[:6] + [v[half : half + 2] for v in w[6:] for half in (0, 2)] for w in (one, two)]

    n = 2
    steps = images // n
    whole = lambda shape: pl.BlockSpec(shape, lambda i: (0,) * len(shape))
    per = lambda width: pl.BlockSpec((n, ROWS_T, width), lambda i: (i, 0, 0))
    half = lambda width: pl.BlockSpec((images // 2, ROWS_T, width), lambda i: (i, 0, 0))
    pieces = [whole((PIX_ROWS, PD))] * 2 + [pl.BlockSpec((1, PIX_ROWS, PD), lambda i: (0, 0, 0)), whole((PIX_ROWS, PD))]
    x0, qkv, attn, prm, hb, soft = pl.pallas_call(
        functools.partial(embed_kernel, tuned, vblock, images // 2, images),
        grid=(2,),
        in_specs=[whole((4, R_ONE, D))] * 6 + [whole((2, R_ONE, D))] * 4 + pieces,
        out_specs=[half(D), half(3 * D)] + [whole(shape) for shape in ((4 * D, D), (16, D), (8, CPAD), (4, 8, CPAD))],
        out_shape=[
            sds((images, ROWS_T, D), f32),
            sds((images, ROWS_T, 3 * D), bf16),
            sds((4 * D, D), bf16),
            sds((16, D), f32),
            sds((8, CPAD), f32),
            sds((4, 8, CPAD), f32),
        ],
        scratch_shapes=[
            pltpu.VMEM((PD, D), f32),
            pltpu.VMEM((PD, D), bf16),
            pltpu.VMEM((BLOCKS, 8, D), f32),
            pltpu.VMEM((V_ROWS, D), f32),
            pltpu.VMEM((ROWS_T, D), f32),
            pltpu.VMEM((4 * PIX_ROWS, D), f32),
            pltpu.VMEM((images, ROWS_T, D), f32),
        ],
        cost_estimate=cost(8),
        compiler_params=params_of(34),
    )(*one, *got)
    if tuned:
        two_x, two_y, hb = lax.optimization_barrier((two_x, two_y, hb))
        corner = corner_of(two_x, two_y)
    out_part = pl.BlockSpec((D, D), lambda i: (3, 0))
    att, x1 = pl.pallas_call(
        functools.partial(attend_kernel, images // 2),
        grid=(2,),
        in_specs=[out_part, whole((16, D)), half(D), half(3 * D)],
        out_specs=[half(D), half(D)],
        out_shape=[sds((images, ROWS_T, D), bf16), sds((images, ROWS_T, D), f32)],
        cost_estimate=cost(10),
        compiler_params=params_of(24),
    )(attn, prm, x0, qkv)

    if tuned:
        corner, x1 = lax.optimization_barrier((corner, x1))
        two = gather_blocks(near_two, two_x, two_y, corner)

    scales = (1.0 / normal_count, LABEL_WEIGHT / normal_count, LOGIT_WEIGHT / (normal_count * C))
    dx1, keep_two, send_two, vgrad, hgrad, loss = run_middle(
        tuned, images // 2, images, scales, *([] if tuned else [given]), *two, prm, hb, soft, meta, x1
    )

    def attend_back(first, *operands):
        begin, count = (0, 1) if first else (1, steps - 1)
        some = lambda width: pl.BlockSpec((n, ROWS_T, width), lambda i: (i + begin, 0, 0))
        return pl.pallas_call(
            functools.partial(attend_back_kernel, n, first),
            grid=(count,),
            in_specs=[out_part, whole((16, D)), some(3 * D), some(D), some(D)] + ([] if first else [whole((D, D)), ANY]),
            out_specs=[some(3 * D), whole((D, D)), whole((16, D))],
            out_shape=[sds((images, ROWS_T, 3 * D), bf16), sds((D, D), f32), sds((16, D), f32)],
            input_output_aliases={} if first else {6: 0},
            cost_estimate=cost(6 * count),
            compiler_params=params_of(22),
        )(*operands)

    dqkv, acc_out, vgrad = attend_back(True, attn, vgrad, qkv, att, dx1)
    if tuned:
        a_code, a_keep, b_code, b_keep = scatter_first([(keep_two, to_core(send_two))], (SECTIONS_TWO,), SECTIONS_TWO)
        a_code, b_code, vgrad = lax.optimization_barrier((a_code, b_code, vgrad))
        moving = (to_x(a_code), to_y(b_code))
    dqkv, acc_out, vgrad = attend_back(False, attn, vgrad, qkv, att, dx1, acc_out, dqkv)
    keep_att, send_att = pl.pallas_call(
        functools.partial(qkv_back_kernel, images // 2, tuned),
        grid=(2,),
        in_specs=[whole((16, D)), half(D), half(3 * D), whole((D, D))],
        out_specs=[whole((16, 48, D)), whole((16, coded(SECTIONS_ATTENTION), D))],
        out_shape=[sds((16, 48, D), f32), sds((16, coded(SECTIONS_ATTENTION), D), jnp.int16)],
        scratch_shapes=[pltpu.VMEM((4 * D, D), f32)],
        cost_estimate=cost(6),
        compiler_params=params_of(22),
    )(prm, x0, dqkv, acc_out)
    if tuned:
        send_att, a_keep = lax.optimization_barrier((send_att, a_keep))
        a_code, a_rest, b_code, b_rest = scatter_second(a_keep, b_keep, *moving, SECTIONS_TWO)
        a_code, b_code, vgrad = lax.optimization_barrier((a_code, b_code, vgrad))
        moving = (to_y(a_code), to_x(b_code))
    acc_patch, blocks = pl.pallas_call(
        functools.partial(unit_back_kernel, images // 2, vblock, images),
        grid=(2,),
        in_specs=[whole((3 * D, D)), whole((16, D)), whole((16, D)), whole((8, CPAD))]
        + pieces
        + [half(D), half(3 * D), half(D)],
        out_specs=[whole((PD, D)), whole((BLOCKS, 8, D))],
        out_shape=[sds((PD, D), f32), sds((BLOCKS, 8, D), f32)],
        scratch_shapes=[
            pltpu.VMEM((16, D), f32),
            pltpu.VMEM((images, ROWS_T, D), f32),
            pltpu.VMEM((4 * PIX_ROWS, D), f32),
            pltpu.VMEM((V_ROWS, D), f32),
        ],
        cost_estimate=cost(6),
        compiler_params=params_of(28),
    )(attn, prm, vgrad, hgrad, *got, x0, dqkv, dx1)
    if tuned:
        rest_two, code_two = scatter_third_pair(a_rest, b_rest, *moving, SECTIONS_TWO)
        code_two, blocks = lax.optimization_barrier((code_two, blocks))
    keep_rest, send_rest = pl.pallas_call(
        functools.partial(block_back_kernel, tuned),
        out_shape=[sds((16, 32, D), f32), sds((16, coded(SECTIONS_REST), D), jnp.int16)],
        cost_estimate=cost(2),
        compiler_params=params_of(20),
    )(acc_patch, blocks)

    if tuned:
        a_code, a_keep, b_code, b_keep = scatter_first(
            [(keep_att, to_core(send_att)), (keep_rest, to_core(send_rest))],
            (SECTIONS_ATTENTION, SECTIONS_REST),
            SECTIONS_ONE,
        )
        code_two, a_code, b_code = lax.optimization_barrier((code_two, a_code, b_code))
        moving = (to_x(a_code), to_y(b_code))
        own_two, code_two = scatter_near(rest_two, to_z(code_two, 1), SECTIONS_TWO)
        code_two, a_keep = lax.optimization_barrier((code_two, a_keep))
        a_code, a_rest, b_code, b_rest = scatter_second(a_keep, b_keep, *moving, SECTIONS_ONE)
        code_two, a_code, b_code = lax.optimization_barrier((code_two, a_code, b_code))
        moving = (to_y(a_code), to_x(b_code))
        share_two, sums = scatter_fourth(own_two, [to_z(code_two, 2)], SECTIONS_TWO, loss)
        own_one, *codes_one = scatter_third(a_rest, b_rest, *moving, SECTIONS_ONE)
        last_one = [to_z(code, k + 1) for k, code in enumerate(codes_one)]
        share_one, sums = scatter_fourth(own_one, last_one, SECTIONS_ONE, sums)
    else:
        shares = plain_scatter((keep_att, send_att), (keep_rest, send_rest), (keep_two, send_two), vblock)
        squares = sum(jnp.sum(share * share) for share in shares)
        sums = loss + jnp.where(lax.broadcasted_iota(i32, (8, 128), 1) == 0, squares, 0.0)
    if tuned:
        states = [views(v, j) for j in range(6) for v in (masters[j], moments[j], averages[j])]
        vector_share = share_one[72:80].reshape(-1)[:vblock]
        loss, norm_value, *news = pl.pallas_call(
            update_kernel,
            out_shape=[sds((1,), f32)] * 2 + [sds(v.shape, f32) for v in states],
            in_specs=[VMEM] * 25,
            out_specs=[SMEM] * 2 + [VMEM] * 18,
            compiler_params=params_of(24),
        )(*sums_along_z(sums), share_one, share_two, vector_share, *states)
        results = [loss.reshape(()), norm_value.reshape(())]
        for j in range(18):
            results.append(news[j].T[None] if j // 3 in (1, 3) else news[j][None] if j // 3 == 2 else news[j])
    else:
        sums = lax.psum(sums, ("dp", "cls"))
        norm_value = jnp.sqrt(sums[0, 0])
        clip_factor = jnp.minimum(1.0, CLIP_NORM / (norm_value + 1e-06))
        results = [sums[0, 1], norm_value]
        for weight, moment, average, share in zip(masters, moments, averages, shares):
            results += list(advance(weight, moment, average, share, clip_factor))
    return tuple(results)


def solution(mesh):
    split_rows, split_columns = P(("dp", "cls"), None), P(None, None, ("dp", "cls"))
    states = (
        [split_rows] * 3
        + [split_columns] * 3
        + [P(None, "dp", "cls")] * 3
        + [P(None, "cls", "dp")] * 3
        + [P("dp", "cls")] * 3
        + [P(("dp", "cls"))] * 3
    )
    in_specs = (
        P("dp", "cls", None),
        P("dp"),
        P("dp", "cls", None),
        P("dp", "cls"),
        P("dp"),
        P(),
        P(),
        P("dp", "cls"),
        *states,
    )
    out_specs = (P(), P(), *states)
    return jax.shard_map(on_device, mesh=mesh, in_specs=in_specs, out_specs=out_specs, check_vma=False)
```
